512 devices in a mesh: leaf: 32 (over z, core), rows: 16 (over y, x).
Axes of the slice: x: 4, y: 4, z: 16, core: 2. Of those that a mesh axis runs over, the one named last changes fastest.
Arguments:
- loc_rhs: float32 [32, 16, 3, 256, 128], P('leaf', 'rows'), may hold values from -6 to 6
- loc_inv: float32 [32, 16, 3, 256, 256], P('leaf', 'rows'), as said below
- loc_low: float32 [32, 16, 3, 2, 256, 256], P('leaf', 'rows'), may hold values from -0.078125 to 0.078125
- loc_parent: int32 [32, 16, 3], P('leaf', 'rows'), may hold values from 0 to 1
- lvl_rhs: float32 [32, 4, 256, 2, 128], P('leaf', None, 'rows'), may hold values from -6 to 6
- lvl_inv: float32 [32, 4, 2, 256, 256], P('leaf', None, None, 'rows'), as said below
- lvl_low: float32 [32, 3, 2, 2, 256, 256], P('leaf', None, None, None, 'rows'), may hold values from -0.25 to 0.25
- lvl_parent: int32 [32, 3, 2], P('leaf'), may hold values from 0 to 3
Outputs:
- loc_sol: float32 [32, 16, 3, 256, 128], P('leaf', 'rows')
- lvl_sol: float32 [32, 4, 256, 2, 128], P('leaf', None, 'rows')
The draws below stay inside these ranges and needn't reach their ends.
Inputs may be any that keep to these rules, and one draw needn't show every extreme that they name: `loc_parent`: the level-0 slot, on the same leaf device, of each local supernode's parent. `lvl_parent`: for slot k at level l on leaf device p: a value v below 2 names slot v at level l + 1 on device p, a larger one slot v - 2 on device p XOR 2**l. `loc_inv`: lower triangular. `lvl_inv`: lower triangular.
All inputs are finite; a program needn't handle non-finite values.
Results may differ from the reference program's by a relative error of at most 0.00016.
Values sent between devices are 32-bit elements; how exact they have to be, the bound alone decides.
A program may use at most 64 MiB of HBM per device.

```python
import math
import jax
import jax.numpy as jnp
from jax import lax

B = 256
R = 128
LOC = 3
SN_LV = 2
LV = 4
N_LEAF = 32
N_ROWS = 16


def shape_lower(off_draw, diag_draw):
    row_index = lax.broadcasted_iota(jnp.int32, (B, B), 0)
    col_index = lax.broadcasted_iota(jnp.int32, (B, B), 1)
    lower_mask = (row_index > col_index).astype(jnp.float32)
    diagonal_mask = (row_index == col_index).astype(jnp.float32)
    return off_draw * lower_mask * (1.0 / math.sqrt(B)) + diag_draw * diagonal_mask


def draw_loc_inv(key, part):
    key = jax.random.fold_in(key, 11)
    full_shape = (N_LEAF, N_ROWS, LOC, B, B)
    key_off, key_diag = jax.random.split(key)
    off_draw = jax.random.normal(key_off, full_shape, jnp.float32)
    diag_draw = jax.random.uniform(key_diag, full_shape, jnp.float32, 0.8, 1.25)
    return shape_lower(off_draw, diag_draw)


def draw_lvl_inv(key, part):
    key = jax.random.fold_in(key, 23)
    full_shape = (N_LEAF, LV, SN_LV, B, B)
    key_off, key_diag = jax.random.split(key)
    off_draw = jax.random.normal(key_off, full_shape, jnp.float32)
    diag_draw = jax.random.uniform(key_diag, full_shape, jnp.float32, 0.8, 1.25)
    return shape_lower(off_draw, diag_draw)


def set_ends(entries, rng, least, top_value):
    spot = [jax.random.randint(jax.random.fold_in(rng, axis), (), 0, length) for axis, length in enumerate(entries.shape)]
    widest = entries.shape.index(max(entries.shape))
    neighbour = spot[:widest] + [(spot[widest] + 1) % entries.shape[widest]] + spot[widest + 1:]
    return entries.at[tuple(spot)].set(least).at[tuple(neighbour)].set(top_value)


def block_levels(own_key, extent, shards, smallest, top_value):
    loudness = 1.0
    for dim, parts in shards:
        steps = jax.random.uniform(jax.random.fold_in(jax.random.fold_in(own_key, 6), dim), (parts,), jnp.float32, smallest / len(shards), top_value / len(shards))
        loudness = loudness * jnp.repeat(jnp.exp(steps), extent[dim] // parts).reshape((-1,) + (1,) * (len(extent) - 1 - dim))
    return loudness


def centred(rng, extent, width, bound, cuts=(), dtype=jnp.bfloat16):
    values = width * jax.random.normal(rng, extent, jnp.float32)
    if cuts:
        values = values * block_levels(rng, extent, cuts, -0.22, 0.18)
    return jnp.clip(values, -bound, bound).astype(dtype)


def setup_inputs(seed: int = 0) -> dict:
    splits = jax.random.split(jax.random.key(seed), 9)
    return {
        "loc_rhs": centred(splits[0], (N_LEAF, N_ROWS, LOC, B, R), 1.0, 6.0, ((0, 32), (1, 16)), jnp.float32),
        "loc_inv": draw_loc_inv(jax.random.fold_in(splits[8], 71), 0),
        "loc_low": centred(splits[2], (N_LEAF, N_ROWS, LOC, 2, B, B), (B * N_ROWS * LOC // SN_LV) ** -0.5, 0.078125, ((0, 32), (1, 16)), jnp.float32),
        "loc_parent": set_ends(jax.random.randint(splits[3], (N_LEAF, N_ROWS, LOC), 0, SN_LV), jax.random.fold_in(splits[3], 1), 0, SN_LV - 1).astype(jnp.int32),
        "lvl_rhs": centred(splits[4], (N_LEAF, LV, B, SN_LV, R), 1.0, 6.0, ((0, 32), (2, 16)), jnp.float32),
        "lvl_inv": draw_lvl_inv(jax.random.fold_in(splits[8], 71), 0),
        "lvl_low": centred(splits[6], (N_LEAF, LV - 1, SN_LV, 2, B, B), (2 * B) ** -0.5, 0.25, ((0, 32), (4, 16)), jnp.float32),
        "lvl_parent": set_ends(jax.random.randint(splits[7], (N_LEAF, LV - 1, SN_LV), 0, 2 * SN_LV), jax.random.fold_in(splits[7], 1), 0, (2 * SN_LV) - 1).astype(jnp.int32),
    }


precise = lax.Precision.HIGHEST


def reference(loc_rhs, loc_inv, loc_low, loc_parent, lvl_rhs, lvl_inv, lvl_low, lvl_parent):
    leaves = jnp.arange(N_LEAF)
    solved_local = jnp.einsum('pqibc,pqicn->pqibn', loc_inv, loc_rhs, precision=precise)
    local_pick = (loc_parent[..., None] == jnp.arange(SN_LV)).astype(jnp.float32)
    contrib = jnp.einsum('pqijbc,pqicn->pqijbn', loc_low, solved_local, precision=precise)
    arrived = jnp.einsum('pqik,pqijbn->pbkjn', local_pick, contrib, precision=precise)
    above_sum = arrived[:, :, :, 0]
    pending = arrived[:, :, :, 1]
    solved_levels = []
    parent_picks = []
    for height in range(LV):
        moved = lvl_rhs[:, height] - above_sum
        solved_now = jnp.einsum('pkbc,pckn->pbkn', lvl_inv[:, height], moved, precision=precise)
        solved_levels.append(solved_now)
        if height + 1 < LV:
            kind_count = 2 if height + 2 < LV else 1
            parent_pick = (lvl_parent[:, height, :, None] == jnp.arange(2 * SN_LV)).astype(jnp.float32)
            parent_picks.append(parent_pick)
            contrib = jnp.einsum('pkjbc,pckn->pbkjn', lvl_low[:, height, :, :kind_count], solved_now, precision=precise)
            outgoing = jnp.concatenate([(contrib[:, :, :, 0] + pending)[:, :, :, None], contrib[:, :, :, 1:]], axis=3)
            packed = jnp.einsum('pkd,pbkjn->pbdjn', parent_pick, outgoing, precision=precise)
            partner = leaves ^ (1 << height)
            arrived = packed[:, :, :SN_LV] + packed[partner][:, :, SN_LV:]
            above_sum = arrived[:, :, :, 0]
            if kind_count == 2:
                pending = arrived[:, :, :, 1]
    top_level = LV - 1
    current = jnp.einsum('pkbc,pbkn->pckn', lvl_inv[:, top_level], solved_levels[top_level], precision=precise)
    results = [None] * LV
    results[top_level] = current
    current_parent = current
    for height in range(LV - 2, -1, -1):
        kind_count = 2 if height + 2 < LV else 1
        if kind_count == 1:
            shared = current[:, :, :, None]
        else:
            shared = jnp.stack([current, current_parent], axis=3)
        partner = leaves ^ (1 << height)
        pooled = jnp.concatenate([shared, shared[partner]], axis=2)
        above_x = jnp.einsum('pkd,pbdjn->pbkjn', parent_picks[height], pooled, precision=precise)
        summed = jnp.einsum('pkjbc,pbkjn->pckn', lvl_low[:, height, :, :kind_count], above_x, precision=precise)
        current_new = jnp.einsum('pkbc,pbkn->pckn', lvl_inv[:, height], solved_levels[height] - summed, precision=precise)
        results[height] = current_new
        current = current_new
        current_parent = above_x[:, :, :, 0]
    parent_x = jnp.einsum('pqik,pbkn->pqibn', local_pick, current, precision=precise)
    grand_x = jnp.einsum('pqik,pbkn->pqibn', local_pick, current_parent, precision=precise)
    summed_local = jnp.einsum('pqijbc,pqijbn->pqicn', loc_low, jnp.stack([parent_x, grand_x], axis=3), precision=precise)
    loc_sol = jnp.einsum('pqibc,pqibn->pqicn', loc_inv, solved_local - summed_local, precision=precise)
    return loc_sol, jnp.stack(results, axis=1)
```

```python
import functools

import jax
import jax.numpy as jnp
from jax import lax
from jax.experimental import pallas as pl
from jax.experimental.pallas import tpu as pltpu
from jax.sharding import PartitionSpec as P

MESH = pl.DeviceIdType.MESH
f32 = jnp.float32
bf16 = jnp.bfloat16

UNKNOWNS = 256
COLUMNS = 128
STRIP = 16
SHARE = 16
SHARES = 8
PEERS = 16
LOCALS = 3
LEVELS = 4
HALF = UNKNOWNS // 2
OCTET = 8
BLOCKS = (("inv", 0), ("low", 0, 0), ("low", 0, 1), ("inv", 1), ("low", 1, 0), ("low", 1, 1), ("inv", 2), ("low", 2, 0), ("inv", 3))
TRIOS = 3


def split(value):
    high = value.astype(bf16)
    return high, (value - high.astype(f32)).astype(bf16)


def dot(left, right, dim):
    return lax.dot_general(
        left, right, (((1,), (dim,)), ((), ())), preferred_element_type=f32
    )


def multiply(left, right, dim):
    return dot(left[0], right[0], dim) + dot(left[1], right[0], dim) + dot(left[0], right[1], dim)


def product(vectors, mat_high, mat_low, dim):
    return multiply(split(vectors), (mat_high, mat_low), dim)


def thin_product(vectors, mat_high, mat_low, dim):
    high = vectors.astype(bf16).astype(f32)
    both = jnp.concatenate([high, vectors - high], axis=0).astype(bf16)
    total = dot(both, mat_high, dim) + dot(both, mat_low, dim)
    return total[:SHARE] + total[SHARE:]


def regroup(tiles):
    group = lax.div(lax.broadcasted_iota(jnp.int32, (2, OCTET, 128), 2), STRIP)
    flat = tiles.reshape(PEERS * OCTET, 128)
    turned = [flat.reshape(2, 8, OCTET, 128)]
    for turn in range(1, 8):
        turned.append(pltpu.roll(flat, STRIP * turn, 1).reshape(2, 8, OCTET, 128))
    results = []
    for g in range(8):
        total = turned[-g % 8][:, 0]
        for m in range(1, 8):
            total = jnp.where(group == m, turned[(m - g) % 8][:, m], total)
        results.append(total)
    return results


def kinds_at(level):
    return 2 if level + 2 < LEVELS else 1


def inv_at(level):
    return BLOCKS.index(("inv", level))


def low_at(level, kind):
    return BLOCKS.index(("low", level, kind))


def trio(index):
    return slice(3 * index, 3 * index + 3)


def kernel(
    loc_names, loc_rhs, loc_inv, loc_low, lvl_rhs, lvl_inv, lvl_low, lvl_names,
    loc_out, sol_out,
    loc_parent, lvl_parent, rhs_s, inv_s, low_s, lvl_rhs_s, inv_high, inv_rest, low_high, low_rest, y_s,
    strips_s, snd, x_part, x_sum, y_part, y_sum, x_last, y_last, ride_snd, ride_rcv, names_snd, names_rcv,
    mats, mat_high, mat_rest, up_snd, up_rcv, down_snd, down_rcv,
    own_snd, ring_rcv, x_rcv, next_rcv, beside_rcv, sol_snd, sol_rcv, turned_s,
    load_sem, strips_sem, part_snd_sem, part_sem, last_snd_sem, last_sem,
    ride_snd_sem, ride_sem, names_snd_sem, names_sem, strip_snd_sem, strip_sem, ring_snd_sem, ring_sem, far_sem,
    pair_snd_sem, pair_sem, up_snd_sem, up_sem, down_snd_sem, down_sem, early_snd_sem, early_sem, late_snd_sem, late_sem,
    sol_snd_sem, sol_sem, beside_snd_sem, beside_sem,
):
    leaf = lax.axis_index("leaf")
    rows = lax.axis_index("rows")
    z, core = lax.div(leaf, 2), lax.rem(leaf, 2)
    y, x = lax.div(rows, 4), lax.rem(rows, 4)
    x_high, parity = lax.div(x, 2), lax.rem(x, 2)
    carried = 2 * z + x_high
    place = jnp.where(x_high == 0, parity, 1 - parity)
    share = 2 * y + core
    own = x_high == core

    def x_of(odd, slot):
        return 2 * odd + jnp.where(odd == 0, slot, 1 - slot)

    def around(value):
        return [value] + [jnp.where(value + n >= 4, value + n - 4, value + n) for n in range(1, 4)]

    slots, cores = [place, 1 - place], [core, 1 - core]
    ys, xs = around(y), around(x)
    carriers = [
        ((2 * z + there_core, 4 * there_y + x_of(core, slot)), 2 * there_y + there_core, slot)
        for there_y in ys
        for slot in slots
        for there_core in cores
    ]
    holders = [(carried, 4 * there_y + there_x) for there_y in ys for there_x in xs]
    x_carriers = [
        ((2 * z + there_core, 4 * y + x_of(core, slot)), slot, there_core)
        for slot in slots
        for there_core in cores
    ]
    x_holders = [(carried, 4 * y + there_x) for there_x in xs]
    sibling = (2 * z + 1 - core, rows)
    z_half = lax.rem(lax.div(z, 2), 2)
    beside = (leaf, rows + 1 - 2 * parity)
    partners = [[beside] + [(leaf, 4 * y + x_of(1 - x_high, slot)) for slot in range(2)]]
    for there_z in (z + 1 - 2 * lax.rem(z, 2), z + 2 - 4 * z_half):
        partners.append(
            [beside] + [(2 * there_z + core, 4 * y + x_of(x_high, slot)) for slot in range(2)]
        )
    y_up, y_far, y_down = ys[1], ys[2], ys[3]
    up, far, down = [(leaf, 4 * there_y + x) for there_y in (y_up, y_far, y_down)]

    loads = [
        pltpu.make_async_copy(loc_rhs, rhs_s, load_sem.at[0]),
        pltpu.make_async_copy(loc_inv, inv_s, load_sem.at[1]),
        pltpu.make_async_copy(loc_low, low_s, load_sem.at[2]),
        pltpu.make_async_copy(lvl_rhs, lvl_rhs_s, load_sem.at[3]),
        pltpu.make_async_copy(loc_names, loc_parent, load_sem.at[4]),
        pltpu.make_async_copy(lvl_names, lvl_parent, load_sem.at[5]),
    ]
    strip_loads = [
        pltpu.make_async_copy(
            lvl_inv.at[level], strips_s.at[:, inv_at(level)], strips_sem.at[inv_at(level)]
        )
        for level in range(LEVELS)
    ] + [
        pltpu.make_async_copy(
            lvl_low.at[level, :, 0 : kinds_at(level)],
            strips_s.at[:, low_at(level, 0) : low_at(level, 0) + kinds_at(level)],
            strips_sem.at[low_at(level, 0)],
        )
        for level in range(LEVELS - 1)
    ]
    for load in loads + strip_loads:
        load.start()

    barrier = pltpu.get_barrier_semaphore()

    def greet(device):
        pl.semaphore_signal(barrier, inc=1, device_id=device, device_id_type=MESH)

    others = [carrier[0] for carrier in carriers[1:]] + holders[1:] + [sibling, beside, up, far, down]
    others += [device for three in partners for device in three[1:]]
    for device in others:
        greet(device)

    @pl.when(jnp.logical_not(own))
    def _():
        greet(carriers[0][0])
        greet(holders[0])

    for load in loads[:2]:
        load.wait()
    for i in range(LOCALS):
        high, rest = split(inv_s[i])
        inv_high[i] = high
        inv_rest[i] = rest
        y_s[i] = product(rhs_s[i].T, high, rest, 1)
    pl.semaphore_wait(barrier, len(others) + jnp.where(own, 0, 2))

    def send(src, dst, send_sem, recv_sem, device):
        return pltpu.make_async_remote_copy(
            src_ref=src, dst_ref=dst, send_sem=send_sem, recv_sem=recv_sem,
            device_id=device, device_id_type=MESH,
        )

    def send_or_keep(copies):
        @pl.when(own)
        def _():
            for src, dst, send_sem, recv_sem, device in copies:
                pltpu.make_async_copy(src, dst, recv_sem).start()

        @pl.when(jnp.logical_not(own))
        def _():
            for copy in copies:
                send(*copy).start()

    def drain(ref, sem):
        pltpu.make_async_copy(ref, ref, sem).wait()

    strip = pl.ds(pl.multiple_of(STRIP * parity, STRIP), STRIP)
    first, second = slice(0, STRIP), slice(STRIP, 2 * STRIP)

    def along_x(index):
        copies = [
            (
                strips_s.at[slot, trio(index)], mats.at[trio(index), y, x_high, strip, :],
                strip_snd_sem, strip_sem.at[index], (2 * z + x_high, 4 * y + x_of(core, slot)),
            )
            for slot in slots
        ]
        send(*copies[1]).start()
        send_or_keep(copies[:1])

    def along_y(index):
        part = mats.at[trio(index), y, core]
        drain(part, strip_sem.at[index])
        for device in (up, down):
            send(part, part, ring_snd_sem, ring_sem.at[index], device).start()
        if index == 0:
            send(part, part, ring_snd_sem, far_sem.at[index], far).start()

    def to_far(index):
        drain(mats.at[trio(index), 0:2, core], ring_sem.at[index])
        for at_y, half_strip, device in ((y_down, first, up), (y_up, second, down)):
            part = mats.at[trio(index), at_y, core, half_strip, :]
            send(part, part, ring_snd_sem, far_sem.at[index], device).start()

    def to_sibling(index):
        if index == 0:
            drain(mats.at[trio(index), 0:2, core], ring_sem.at[index])
        drain(mats.at[trio(index), y_far, core], far_sem.at[index])
        part = mats.at[trio(index), :, core]
        send(part, part, pair_snd_sem, pair_sem.at[index], sibling).start()

    def take(index):
        drain(mats.at[trio(index), :, 1 - core], pair_sem.at[index])
        parts = {}
        for m in range(3 * index, 3 * index + 3):
            parts[BLOCKS[m]] = split(mats[m].reshape(UNKNOWNS, UNKNOWNS))
            if BLOCKS[m][0] == "inv":
                mat_high[m], mat_rest[m] = parts[BLOCKS[m]]
        for m in range(3 * index, 3 * index + 3):
            name, level = BLOCKS[m][:2]
            if name == "low":
                mat_high[m], mat_rest[m] = split(multiply(parts[BLOCKS[m]], parts["inv", level], 0))
            elif level + 1 == LEVELS:
                turned = split(mats[m].reshape(UNKNOWNS, UNKNOWNS).T)
                mat_high[m], mat_rest[m] = split(multiply(turned, parts[BLOCKS[m]], 0))

    def thin(vectors, m, dim):
        return thin_product(vectors, mat_high[m], mat_rest[m], dim)

    for load in strip_loads:
        load.wait()
    for index in range(TRIOS):
        along_x(index)
    for load in loads[2:]:
        load.wait()
    pick = [
        [jnp.where(loc_parent[i] == slot, 1.0, 0.0).astype(f32) for slot in range(2)]
        for i in range(LOCALS)
    ]

    y_others = [(up, y_up), (far, y_far), (down, y_down)]

    def local_updates(kind):
        for i in range(LOCALS):
            high, rest = split(low_s[i, kind])
            low_high[i, kind] = high
            low_rest[i, kind] = rest
            update = product(y_s[i], high, rest, 1).reshape(4, 2, SHARE, UNKNOWNS)
            for slot in range(2):
                if i == 0:
                    snd[kind, slot] = pick[i][slot] * update
                else:
                    snd[kind, slot] += pick[i][slot] * update

    def x_first():
        copies = [
            (snd.at[0, slot, :, there_core], x_part.at[x], part_snd_sem.at[0], part_sem.at[0], device)
            for device, slot, there_core in x_carriers
        ]
        for copy in copies[1:]:
            send(*copy).start()
        send_or_keep(copies[:1])

    def x_then_y():
        drain(x_part, part_sem.at[0])
        x_sum[...] = (x_part[0] + x_part[1]) + (x_part[2] + x_part[3])
        for device, there_y in y_others:
            send(
                x_sum.at[there_y], x_last.at[y], last_snd_sem.at[0], last_sem.at[0], device
            ).start()

    def y_first():
        for device, there_y in y_others:
            send(
                snd.at[1, :, there_y], y_part.at[y], part_snd_sem.at[1], part_sem.at[1], device
            ).start()

    def y_then_x():
        drain(y_part.at[0:3], part_sem.at[1])
        total = snd[1, :, y]
        for _, there_y in y_others:
            total = total + y_part[there_y]
        y_sum[...] = total
        copies = [
            (y_sum.at[slot, there_core], y_last.at[x], last_snd_sem.at[1], last_sem.at[1], device)
            for device, slot, there_core in x_carriers
        ]
        for copy in copies[1:]:
            send(*copy).start()
        send_or_keep(copies[:1])

    row = lax.broadcasted_iota(jnp.int32, (OCTET, 128), 0)
    names = jnp.zeros((OCTET, 128), f32)
    for k in range(2):
        for level in range(LEVELS - 1):
            names = jnp.where(row == 4 * k + level, lvl_parent[k, level].astype(f32), names)
    names_snd[...] = names
    send(names_snd, names_rcv, names_snd_sem, names_sem, sibling).start()
    for k in range(2):
        strips = [
            lvl_rhs_s[pl.ds(2 * STRIP * level + k, STRIP, stride=2), :] for level in range(LEVELS)
        ]
        strips.append(jnp.zeros((HALF - LEVELS * STRIP, COLUMNS), f32))
        extra = jnp.concatenate(strips, axis=0).T.reshape(SHARES, 2, OCTET, 128)
        right = pltpu.roll(extra[:, 1].reshape(SHARES * OCTET, 128), 64, 1)
        ride_snd[k] = extra[:, 0] + right.reshape(SHARES, OCTET, 128)
    rides = [
        (ride_snd.at[slot, index], ride_rcv.at[rows], ride_snd_sem, ride_sem, device)
        for device, index, slot in carriers
    ]
    for ride in rides[1:]:
        send(*ride).start()
    send_or_keep(rides[:1])
    local_updates(0)
    x_first()
    along_y(0)
    local_updates(1)
    y_first()
    along_y(1)
    along_y(2)
    x_then_y()

    def prepare_local(i):
        inverse = (inv_high[i], inv_rest[i])
        y_s[i] = product(y_s[i], inv_high[i], inv_rest[i], 0)
        for kind in range(2):
            high, rest = split(multiply((low_high[i, kind], low_rest[i, kind]), inverse, 0))
            low_high[i, kind] = high
            low_rest[i, kind] = rest

    to_sibling(0)
    to_far(1)

    y_then_x()
    drain(ride_rcv, ride_sem)
    parts = regroup(ride_rcv[...].reshape(2, 8, OCTET, 128))
    parts = [jnp.concatenate([part[0], part[1]], axis=1) for part in parts]
    rhs = [
        jnp.concatenate([parts[level], parts[LEVELS + level]], axis=0) for level in range(LEVELS)
    ]
    drain(names_rcv, names_sem)
    names = jnp.where(own, names_snd[...], names_rcv[...])
    parent = []
    for level in range(LEVELS - 1):
        name = jnp.where(place == 0, names[level : level + 1], names[4 + level : 5 + level])
        parent.append(jnp.broadcast_to(jnp.concatenate([name, name], axis=1), (SHARE, UNKNOWNS)))
    mine, places = place.astype(f32), [(1 - place).astype(f32), 2.0, 3.0]

    def chosen(name, at_place, value):
        return jnp.where(name == at_place, value, 0.0)

    def slot_at(index):
        return 0 if index == 0 else 1 + place

    def gathered(total, buffer, sem):
        drain(buffer, sem)
        for index in range(3):
            total = total + buffer[index]
        return total

    below = []
    take(0)
    to_sibling(1)
    drain(x_last.at[0:3], last_sem.at[0])
    above = x_sum[y]
    for _, there_y in y_others:
        above = above + x_last[there_y]
    for level in range(LEVELS):
        kinds = kinds_at(level)
        moved = rhs[level] - above
        if level + 1 < LEVELS:
            out = [thin(moved, low_at(level, kind), 1) for kind in range(kinds)]
            if level == 0:
                drain(y_last, last_sem.at[1])
                pending = (y_last[0] + y_last[1]) + (y_last[2] + y_last[3])
            else:
                pending = gathered(own_pending, up_rcv.at[level - 1, 1], up_sem.at[level - 1, 1])
            out[0] = out[0] + pending
            for kind in range(kinds):
                for index in range(3):
                    up_snd[level, kind, index] = chosen(parent[level], places[index], out[kind])
                    send(
                        up_snd.at[level, kind, index], up_rcv.at[level, kind, slot_at(index)],
                        up_snd_sem, up_sem.at[level, kind], partners[level][index],
                    ).start()
            own_pending = chosen(parent[level], mine, out[-1])
            if level == 0:
                to_far(2)
            below.append(thin(thin(moved, inv_at(level), 1), inv_at(level), 0))
            if level + 1 < TRIOS:
                take(level + 1)
            else:
                prepare_local(0)
            if level == 0:
                to_sibling(2)
            own_above = chosen(parent[level], mine, out[0])
            above = gathered(own_above, up_rcv.at[level, 0], up_sem.at[level, 0])

    def send_down(level, kind, value):
        down_snd[level, kind] = value
        for index in range(3):
            send(
                down_snd.at[level, kind], down_rcv.at[level, kind, slot_at(index)],
                down_snd_sem, down_sem.at[level, kind], partners[level][index],
            ).start()

    def pooled(level, kind, value):
        total = chosen(parent[level], mine, value)
        drain(down_rcv.at[level, kind], down_sem.at[level, kind])
        for index in range(3):
            total = total + chosen(parent[level], places[index], down_rcv[level, kind, index])
        return total

    def spread(step, landing, value):
        own_snd[step] = value.reshape(2, OCTET, UNKNOWNS)
        ring_rcv[step, y] = value[0:OCTET]
        for device, _ in y_others:
            send(
                own_snd.at[step, 0], ring_rcv.at[step, y],
                early_snd_sem.at[step], early_sem.at[step, 0], device,
            ).start()
        copies = [
            (
                own_snd.at[step, 1], landing.at[place, y, core, 1],
                early_snd_sem.at[step], early_sem.at[step, 1], device,
            )
            for device in x_holders
        ]
        for copy in copies[1:]:
            send(*copy).start()
        send_or_keep(copies[:1])

    def spread_on(step, landing):
        drain(ring_rcv.at[step, 0:3], early_sem.at[step, 0])
        copies = [
            (
                ring_rcv.at[step], landing.at[place, :, core, 0],
                late_snd_sem.at[step, 0], late_sem.at[step, 0], device,
            )
            for device in x_holders
        ]
        for copy in copies[1:]:
            send(*copy).start()
        send_or_keep(copies[:1])
        part = landing.at[:, y, :, 1]
        drain(part, early_sem.at[step, 1])
        for device, _ in y_others:
            send(part, part, late_snd_sem.at[step, 1], late_sem.at[step, 1], device).start()

    def spread_end(step, landing):
        drain(landing.at[:, :, :, 0], late_sem.at[step, 0])
        drain(landing.at[:, 0:3, :, 1], late_sem.at[step, 1])

    def whole(landing):
        return landing[...].reshape(2, COLUMNS, UNKNOWNS)

    current, current_parent = thin(moved, inv_at(LEVELS - 1), 0), None
    results = [None] * LEVELS
    results[LEVELS - 1] = current
    for level in range(LEVELS - 2, -1, -1):
        send_down(level, 0, current)
        if level == 0:
            spread(0, next_rcv, current)
            halves = []
            for octet in (slice(0, OCTET), slice(OCTET, SHARE)):
                for part in results[1:] + results[3:]:
                    halves.append(jnp.stack([part[octet, 0:HALF], part[octet, HALF:]], axis=0))
            tiles = regroup(jnp.stack(halves, axis=1))
            for m in range(8):
                for h in range(2):
                    sol_snd[8 * h + m] = tiles[m][h]
            spread_on(0, next_rcv)
            copies = [
                (sol_snd.at[device[1]], sol_rcv.at[place, share], sol_snd_sem, sol_sem, device)
                for device in holders
            ]
            for copy in copies[1:]:
                send(*copy).start()
            send_or_keep(copies[:1])
        else:
            prepare_local(LEVELS - 1 - level)
        left = below[level]
        if kinds_at(level) == 2:
            left = left - thin(pooled(level, 1, current_parent), low_at(level, 1), 0)
        current_parent = pooled(level, 0, current)
        if level > 0:
            send_down(level - 1, 1, current_parent)
        current = left - thin(current_parent, low_at(level, 0), 0)
        results[level] = current
    spread(1, x_rcv, current)

    spread_end(0, next_rcv)
    send(next_rcv, beside_rcv, beside_snd_sem, beside_sem, sibling).start()
    spread_on(1, x_rcv)
    drain(sol_rcv, sol_sem)
    for k in range(2):
        packed = sol_rcv[k].reshape(SHARES * OCTET, 128)
        right = pltpu.roll(packed, 64, 1).reshape(SHARES, OCTET, 128)
        both = jnp.stack([sol_rcv[k], right], axis=1).reshape(COLUMNS, 128)
        strips = both.T
        for level in range(1, LEVELS):
            to = pl.ds(2 * STRIP * level + k, STRIP, stride=2)
            sol_out[to, :] = strips[STRIP * (level - 1) : STRIP * level]
    drain(beside_rcv, beside_sem)
    own_next, beside_next = whole(next_rcv), whole(beside_rcv)
    for i in range(LOCALS):
        grand = None
        for at_place in range(4):
            weight = sum(
                pick[i][k] * jnp.where(lvl_parent[k, 0] == at_place, 1.0, 0.0).astype(f32)
                for k in range(2)
            )
            if at_place < 2:
                term = weight * own_next[at_place]
            else:
                term = weight * beside_next[at_place - 2]
            grand = term if grand is None else grand + term
        y_s[i] = y_s[i] - product(grand, low_high[i, 1], low_rest[i, 1], 0)
    spread_end(1, x_rcv)
    x_all = whole(x_rcv)
    for i in range(LOCALS):
        above_x = pick[i][0] * x_all[0] + pick[i][1] * x_all[1]
        loc_out[i] = (y_s[i] - product(above_x, low_high[i, 0], low_rest[i, 0], 0)).T
    here = pl.ds(pl.multiple_of(STRIP * rows, STRIP), STRIP)
    for k in range(2):
        turned_s[k] = x_all[k].T
        sol_out[pl.ds(k, STRIP, stride=2), :] = turned_s[k, here, :]

    drain(x_part.at[0:3], part_snd_sem.at[0])
    drain(y_part.at[0:3], part_snd_sem.at[1])
    drain(x_last.at[0:3], last_snd_sem.at[0])
    drain(y_last.at[0:3], last_snd_sem.at[1])
    drain(ride_rcv.at[1:], ride_snd_sem)
    drain(names_snd, names_snd_sem)
    for step in range(2):
        for _ in range(2):
            drain(ring_rcv.at[step, 0:3], early_snd_sem.at[step])
        for _ in range(3):
            drain(ring_rcv.at[step], late_snd_sem.at[step, 0])
        drain(x_rcv.at[:, 0:3, :, 1], late_snd_sem.at[step, 1])
    drain(sol_snd.at[1:], sol_snd_sem)
    drain(strips_s.at[0], strip_snd_sem)
    drain(mats.at[:, 0:3, 0], ring_snd_sem)
    drain(mats.at[:, :, 0], pair_snd_sem)
    drain(beside_rcv, beside_snd_sem)
    for level in range(LEVELS - 1):
        for kind in range(kinds_at(level)):
            drain(up_rcv.at[level, kind], up_snd_sem)
            drain(down_rcv.at[level, kind], down_snd_sem)

    @pl.when(jnp.logical_not(own))
    def _():
        drain(x_part.at[0], part_snd_sem.at[0])
        drain(y_last.at[0], last_snd_sem.at[1])
        drain(ride_rcv.at[0], ride_snd_sem)
        for step in range(2):
            drain(ring_rcv.at[step, 0], early_snd_sem.at[step])
            drain(ring_rcv.at[step], late_snd_sem.at[step, 0])
        drain(sol_snd.at[0], sol_snd_sem)
        drain(strips_s.at[0], strip_snd_sem)


def on_device(loc_rhs, loc_inv, loc_low, loc_parent, lvl_rhs, lvl_inv, lvl_low, lvl_parent):
    vmem = pl.BlockSpec(memory_space=pltpu.VMEM)
    far = pl.BlockSpec(memory_space=pltpu.HBM)
    dma = pltpu.SemaphoreType.DMA
    square = (UNKNOWNS, UNKNOWNS)
    loc_sol, sol = pl.pallas_call(
        kernel,
        out_shape=(
            jax.ShapeDtypeStruct((LOCALS, UNKNOWNS, COLUMNS), f32),
            jax.ShapeDtypeStruct((COLUMNS, 128), f32),
        ),
        in_specs=[far] * 8,
        out_specs=(vmem, vmem),
        scratch_shapes=[
            pltpu.SMEM((LOCALS,), jnp.int32),
            pltpu.SMEM((2, LEVELS - 1), jnp.int32),
            pltpu.VMEM((LOCALS, UNKNOWNS, COLUMNS), f32),
            pltpu.VMEM((LOCALS,) + square, f32),
            pltpu.VMEM((LOCALS, 2) + square, f32),
            pltpu.VMEM((LEVELS * STRIP * 2, COLUMNS), f32),
            pltpu.VMEM((LOCALS,) + square, bf16),
            pltpu.VMEM((LOCALS,) + square, bf16),
            pltpu.VMEM((LOCALS, 2) + square, bf16),
            pltpu.VMEM((LOCALS, 2) + square, bf16),
            pltpu.VMEM((LOCALS, COLUMNS, UNKNOWNS), f32),
            pltpu.VMEM((2, len(BLOCKS), STRIP, UNKNOWNS), f32),
            pltpu.VMEM((2, 2, 4, 2, SHARE, UNKNOWNS), f32),
            pltpu.VMEM((4, 4, SHARE, UNKNOWNS), f32),
            pltpu.VMEM((4, SHARE, UNKNOWNS), f32),
            pltpu.VMEM((4, 2, 2, SHARE, UNKNOWNS), f32),
            pltpu.VMEM((2, 2, SHARE, UNKNOWNS), f32),
            pltpu.VMEM((4, SHARE, UNKNOWNS), f32),
            pltpu.VMEM((4, SHARE, UNKNOWNS), f32),
            pltpu.VMEM((2, SHARES, OCTET, 128), f32),
            pltpu.VMEM((PEERS, OCTET, 128), f32),
            pltpu.VMEM((OCTET, 128), f32),
            pltpu.VMEM((OCTET, 128), f32),
            pltpu.VMEM((len(BLOCKS), 4, 2, 2 * STRIP, UNKNOWNS), f32),
            pltpu.VMEM((len(BLOCKS),) + square, bf16),
            pltpu.VMEM((len(BLOCKS),) + square, bf16),
            pltpu.VMEM((LEVELS - 1, 2, 3, SHARE, UNKNOWNS), f32),
            pltpu.VMEM((LEVELS - 1, 2, 3, SHARE, UNKNOWNS), f32),
            pltpu.VMEM((LEVELS - 1, 2, SHARE, UNKNOWNS), f32),
            pltpu.VMEM((LEVELS - 1, 2, 3, SHARE, UNKNOWNS), f32),
            pltpu.VMEM((2, 2, OCTET, UNKNOWNS), f32),
            pltpu.VMEM((2, 4, OCTET, UNKNOWNS), f32),
            pltpu.VMEM((2, 4, 2, 2, OCTET, UNKNOWNS), f32),
            pltpu.VMEM((2, 4, 2, 2, OCTET, UNKNOWNS), f32),
            pltpu.VMEM((2, 4, 2, 2, OCTET, UNKNOWNS), f32),
            pltpu.VMEM((PEERS, OCTET, 128), f32),
            pltpu.VMEM((2, SHARES, OCTET, 128), f32),
            pltpu.VMEM((2, UNKNOWNS, COLUMNS), f32),
            dma((6,)),
            dma((len(BLOCKS),)),
            dma((2,)),
            dma((2,)),
            dma((2,)),
            dma((2,)),
            dma,
            dma,
            dma,
            dma,
            dma,
            dma((TRIOS,)),
            dma,
            dma((TRIOS,)),
            dma((TRIOS,)),
            dma,
            dma((TRIOS,)),
            dma,
            dma((LEVELS - 1, 2)),
            dma,
            dma((LEVELS - 1, 2)),
            dma((2,)),
            dma((2, 2)),
            dma((2, 2)),
            dma((2, 2)),
            dma,
            dma,
            dma,
            dma,
        ],
        compiler_params=pltpu.CompilerParams(
            collective_id=0, has_side_effects=True, vmem_limit_bytes=40 * 1024 * 1024
        ),
    )(
        *(
            pltpu.with_memory_space_constraint(operand, pltpu.HBM)
            for operand in (
                loc_parent.reshape(LOCALS),
                loc_rhs.reshape(LOCALS, UNKNOWNS, COLUMNS),
                loc_inv.reshape((LOCALS,) + square),
                loc_low.reshape((LOCALS, 2) + square),
                lvl_rhs.reshape(LEVELS * STRIP * 2, COLUMNS),
                lvl_inv.reshape(LEVELS, 2, STRIP, UNKNOWNS),
                lvl_low.reshape(LEVELS - 1, 2, 2, STRIP, UNKNOWNS),
                lvl_parent.reshape(LEVELS - 1, 2).T,
            )
        )
    )
    return loc_sol[None, None], sol.reshape(1, LEVELS, STRIP, 2, COLUMNS)


def solution(mesh):
    in_specs = (
        P("leaf", "rows", None, None, None),
        P("leaf", "rows", None, None, None),
        P("leaf", "rows", None, None, None, None),
        P("leaf", "rows", None),
        P("leaf", None, "rows", None, None),
        P("leaf", None, None, "rows", None),
        P("leaf", None, None, None, "rows", None),
        P("leaf", None, None),
    )
    out_specs = (P("leaf", "rows", None, None, None), P("leaf", None, "rows", None, None))
    return jax.shard_map(
        on_device, mesh=mesh, in_specs=in_specs, out_specs=out_specs, check_vma=False
    )
```

```python
import functools

import jax
import jax.numpy as jnp
from jax import lax
from jax.experimental import pallas as pl
from jax.experimental.pallas import tpu as pltpu
from jax.sharding import PartitionSpec as P

MESH = pl.DeviceIdType.MESH
f32 = jnp.float32
bf16 = jnp.bfloat16

UNKNOWNS = 256
COLUMNS = 128
STRIP = 16
SHARE = 16
SHARES = 8
PEERS = 16
LOCALS = 3
LEVELS = 4
HALF = UNKNOWNS // 2
OCTET = 8
BLOCKS = (("inv", 0), ("low", 0, 0), ("low", 0, 1), ("inv", 1), ("low", 1, 0), ("low", 1, 1), ("inv", 2), ("low", 2, 0), ("inv", 3))
TRIOS = 3


def split(value):
    high = value.astype(bf16)
    return high, (value - high.astype(f32)).astype(bf16)


def dot(left, right, dim):
    return lax.dot_general(
        left, right, (((1,), (dim,)), ((), ())), preferred_element_type=f32
    )


def multiply(left, right, dim):
    return dot(left[0], right[0], dim) + dot(left[1], right[0], dim) + dot(left[0], right[1], dim)


def product(vectors, mat_high, mat_low, dim):
    return multiply(split(vectors), (mat_high, mat_low), dim)


def thin_product(vectors, mat_high, mat_low, dim):
    high = vectors.astype(bf16).astype(f32)
    both = jnp.concatenate([high, vectors - high], axis=0).astype(bf16)
    total = dot(both, mat_high, dim) + dot(both, mat_low, dim)
    return total[:SHARE] + total[SHARE:]


def regroup(tiles):
    group = lax.div(lax.broadcasted_iota(jnp.int32, (2, OCTET, 128), 2), STRIP)
    flat = tiles.reshape(PEERS * OCTET, 128)
    turned = [flat.reshape(2, 8, OCTET, 128)]
    for turn in range(1, 8):
        turned.append(pltpu.roll(flat, STRIP * turn, 1).reshape(2, 8, OCTET, 128))
    results = []
    for g in range(8):
        total = turned[-g % 8][:, 0]
        for m in range(1, 8):
            total = jnp.where(group == m, turned[(m - g) % 8][:, m], total)
        results.append(total)
    return results


def kinds_at(level):
    return 2 if level + 2 < LEVELS else 1


def inv_at(level):
    return BLOCKS.index(("inv", level))


def low_at(level, kind):
    return BLOCKS.index(("low", level, kind))


def trio(index):
    return slice(3 * index, 3 * index + 3)


def kernel(
    loc_names, loc_rhs, loc_inv, loc_low, lvl_rhs, lvl_inv, lvl_low, lvl_names,
    loc_out, sol_out,
    loc_parent, lvl_parent, rhs_s, inv_s, low_s, lvl_rhs_s, inv_high, inv_rest, low_high, low_rest, y_s,
    strips_s, snd, x_part, x_sum, y_part, y_sum, x_last, y_last, ride_snd, ride_rcv, names_snd, names_rcv,
    mats, mat_high, mat_rest, up_snd, up_rcv, down_snd, down_rcv,
    own_snd, ring_rcv, x_rcv, next_rcv, beside_rcv, sol_snd, sol_rcv, turned_s,
    load_sem, strips_sem, part_snd_sem, part_sem, last_snd_sem, last_sem,
    ride_snd_sem, ride_sem, names_snd_sem, names_sem, strip_snd_sem, strip_sem, ring_snd_sem, ring_sem, far_sem,
    up_snd_sem, up_sem, down_snd_sem, down_sem, early_snd_sem, early_sem, late_snd_sem, late_sem,
    sol_snd_sem, sol_sem, beside_snd_sem, beside_sem,
):
    leaf = lax.axis_index("leaf")
    rows = lax.axis_index("rows")
    z, core = lax.div(leaf, 2), lax.rem(leaf, 2)
    y, x = lax.div(rows, 4), lax.rem(rows, 4)
    x_high, parity = lax.div(x, 2), lax.rem(x, 2)
    carried = 2 * z + parity
    share = 2 * y + x_high
    own = parity == core

    def around(value):
        return [value] + [jnp.where(value + n >= 4, value + n - 4, value + n) for n in range(1, 4)]

    slots, halves = [core, 1 - core], [x_high, 1 - x_high]
    ys, xs = around(y), around(x)
    carriers = [
        ((2 * z + slot, 4 * there_y + 2 * half + core), 2 * there_y + half, slot)
        for there_y in ys
        for half in halves
        for slot in slots
    ]
    holders = [(carried, 4 * there_y + there_x) for there_y in ys for there_x in xs]
    x_carriers = [
        ((2 * z + slot, 4 * y + 2 * half + core), slot, half) for half in halves for slot in slots
    ]
    x_holders = [(carried, 4 * y + there_x) for there_x in xs]
    sibling = (2 * z + 1 - core, rows)
    z_half = lax.rem(lax.div(z, 2), 2)
    partners = [
        [sibling] + [(2 * there_z + slot, there_rows) for slot in range(2)]
        for there_z, there_rows in (
            (z, rows + 1 - 2 * parity), (z + 1 - 2 * lax.rem(z, 2), rows), (z + 2 - 4 * z_half, rows)
        )
    ]
    y_up, y_far, y_down = ys[1], ys[2], ys[3]
    up, far, down = [(leaf, 4 * there_y + x) for there_y in (y_up, y_far, y_down)]

    loads = [
        pltpu.make_async_copy(loc_rhs, rhs_s, load_sem.at[0]),
        pltpu.make_async_copy(loc_inv, inv_s, load_sem.at[1]),
        pltpu.make_async_copy(loc_low, low_s, load_sem.at[2]),
        pltpu.make_async_copy(lvl_rhs, lvl_rhs_s, load_sem.at[3]),
        pltpu.make_async_copy(loc_names, loc_parent, load_sem.at[4]),
        pltpu.make_async_copy(lvl_names, lvl_parent, load_sem.at[5]),
    ]
    strip_loads = [
        pltpu.make_async_copy(
            lvl_inv.at[level], strips_s.at[:, inv_at(level)], strips_sem.at[inv_at(level)]
        )
        for level in range(LEVELS)
    ] + [
        pltpu.make_async_copy(
            lvl_low.at[level, :, 0 : kinds_at(level)],
            strips_s.at[:, low_at(level, 0) : low_at(level, 0) + kinds_at(level)],
            strips_sem.at[low_at(level, 0)],
        )
        for level in range(LEVELS - 1)
    ]
    for load in loads + strip_loads:
        load.start()

    barrier = pltpu.get_barrier_semaphore()

    def greet(device):
        pl.semaphore_signal(barrier, inc=1, device_id=device, device_id_type=MESH)

    others = [carrier[0] for carrier in carriers[1:]] + holders[1:] + [sibling, up, far, down]
    others += [device for three in partners for device in three[1:]]
    for device in others:
        greet(device)

    @pl.when(jnp.logical_not(own))
    def _():
        greet(carriers[0][0])
        greet(holders[0])

    for load in loads[:2]:
        load.wait()
    for i in range(LOCALS):
        high, rest = split(inv_s[i])
        inv_high[i] = high
        inv_rest[i] = rest
        y_s[i] = product(rhs_s[i].T, high, rest, 1)
    pl.semaphore_wait(barrier, len(others) + jnp.where(own, 0, 2))

    def send(src, dst, send_sem, recv_sem, device):
        return pltpu.make_async_remote_copy(
            src_ref=src, dst_ref=dst, send_sem=send_sem, recv_sem=recv_sem,
            device_id=device, device_id_type=MESH,
        )

    def send_or_keep(copies):
        @pl.when(own)
        def _():
            for src, dst, send_sem, recv_sem, device in copies:
                pltpu.make_async_copy(src, dst, recv_sem).start()

        @pl.when(jnp.logical_not(own))
        def _():
            for copy in copies:
                send(*copy).start()

    def drain(ref, sem):
        pltpu.make_async_copy(ref, ref, sem).wait()

    strip = pl.ds(pl.multiple_of(STRIP * x, STRIP), STRIP)
    first, second = slice(0, 2 * STRIP), slice(2 * STRIP, 4 * STRIP)

    def along_x(index):
        copies = [
            (
                strips_s.at[slot, trio(index)], mats.at[trio(index), y, strip, :],
                strip_snd_sem, strip_sem.at[index], device,
            )
            for device, slot, _ in x_carriers
        ]
        for copy in copies[1:]:
            send(*copy).start()
        send_or_keep(copies[:1])

    def along_y(index):
        part = mats.at[trio(index), y]
        drain(part, strip_sem.at[index])
        for device in (up, down):
            send(part, part, ring_snd_sem, ring_sem.at[index], device).start()

    def to_far(index):
        drain(mats.at[trio(index), 0:2], ring_sem.at[index])
        for at_y, half_strip, device in ((y_down, first, up), (y_up, second, down)):
            part = mats.at[trio(index), at_y, half_strip, :]
            send(part, part, ring_snd_sem, far_sem.at[index], device).start()

    def take(index):
        drain(mats.at[trio(index), y_far], far_sem.at[index])
        parts = {}
        for m in range(3 * index, 3 * index + 3):
            parts[BLOCKS[m]] = split(mats[m].reshape(UNKNOWNS, UNKNOWNS))
            if BLOCKS[m][0] == "inv":
                mat_high[m], mat_rest[m] = parts[BLOCKS[m]]
        for m in range(3 * index, 3 * index + 3):
            name, level = BLOCKS[m][:2]
            if name == "low":
                mat_high[m], mat_rest[m] = split(multiply(parts[BLOCKS[m]], parts["inv", level], 0))
            elif level + 1 == LEVELS:
                turned = split(mats[m].reshape(UNKNOWNS, UNKNOWNS).T)
                mat_high[m], mat_rest[m] = split(multiply(turned, parts[BLOCKS[m]], 0))

    def thin(vectors, m, dim):
        return thin_product(vectors, mat_high[m], mat_rest[m], dim)

    for load in strip_loads:
        load.wait()
    for index in range(TRIOS):
        along_x(index)
    for load in loads[2:]:
        load.wait()
    pick = [
        [jnp.where(loc_parent[i] == slot, 1.0, 0.0).astype(f32) for slot in range(2)]
        for i in range(LOCALS)
    ]

    y_others = [(up, y_up), (far, y_far), (down, y_down)]

    def local_updates(kind):
        for i in range(LOCALS):
            high, rest = split(low_s[i, kind])
            low_high[i, kind] = high
            low_rest[i, kind] = rest
            update = product(y_s[i], high, rest, 1).reshape(4, 2, SHARE, UNKNOWNS)
            for slot in range(2):
                if i == 0:
                    snd[kind, slot] = pick[i][slot] * update
                else:
                    snd[kind, slot] += pick[i][slot] * update

    def x_first():
        copies = [
            (snd.at[0, slot, :, half], x_part.at[x], part_snd_sem.at[0], part_sem.at[0], device)
            for device, slot, half in x_carriers
        ]
        for copy in copies[1:]:
            send(*copy).start()
        send_or_keep(copies[:1])

    def x_then_y():
        drain(x_part, part_sem.at[0])
        x_sum[...] = (x_part[0] + x_part[1]) + (x_part[2] + x_part[3])
        for device, there_y in y_others:
            send(
                x_sum.at[there_y], x_last.at[y], last_snd_sem.at[0], last_sem.at[0], device
            ).start()

    def y_first():
        for device, there_y in y_others:
            send(
                snd.at[1, :, there_y], y_part.at[y], part_snd_sem.at[1], part_sem.at[1], device
            ).start()

    def y_then_x():
        drain(y_part.at[0:3], part_sem.at[1])
        total = snd[1, :, y]
        for _, there_y in y_others:
            total = total + y_part[there_y]
        y_sum[...] = total
        copies = [
            (y_sum.at[slot, half], y_last.at[x], last_snd_sem.at[1], last_sem.at[1], device)
            for device, slot, half in x_carriers
        ]
        for copy in copies[1:]:
            send(*copy).start()
        send_or_keep(copies[:1])

    row = lax.broadcasted_iota(jnp.int32, (OCTET, 128), 0)
    names = jnp.zeros((OCTET, 128), f32)
    for k in range(2):
        for level in range(LEVELS - 1):
            names = jnp.where(row == 4 * k + level, lvl_parent[k, level].astype(f32), names)
    names_snd[...] = names
    send(names_snd, names_rcv, names_snd_sem, names_sem, sibling).start()
    for k in range(2):
        strips = [
            lvl_rhs_s[pl.ds(2 * STRIP * level + k, STRIP, stride=2), :] for level in range(LEVELS)
        ]
        strips.append(jnp.zeros((HALF - LEVELS * STRIP, COLUMNS), f32))
        extra = jnp.concatenate(strips, axis=0).T.reshape(SHARES, 2, OCTET, 128)
        right = pltpu.roll(extra[:, 1].reshape(SHARES * OCTET, 128), 64, 1)
        ride_snd[k] = extra[:, 0] + right.reshape(SHARES, OCTET, 128)
    rides = [
        (ride_snd.at[slot, index], ride_rcv.at[rows], ride_snd_sem, ride_sem, device)
        for device, index, slot in carriers
    ]
    for ride in rides[1:]:
        send(*ride).start()
    send_or_keep(rides[:1])
    local_updates(0)
    x_first()
    along_y(0)
    local_updates(1)
    y_first()
    along_y(1)
    x_then_y()
    to_far(0)
    along_y(2)

    def prepare_local(i):
        inverse = (inv_high[i], inv_rest[i])
        y_s[i] = product(y_s[i], inv_high[i], inv_rest[i], 0)
        for kind in range(2):
            high, rest = split(multiply((low_high[i, kind], low_rest[i, kind]), inverse, 0))
            low_high[i, kind] = high
            low_rest[i, kind] = rest

    y_then_x()
    drain(ride_rcv, ride_sem)
    parts = regroup(ride_rcv[...].reshape(2, 8, OCTET, 128))
    parts = [jnp.concatenate([part[0], part[1]], axis=1) for part in parts]
    rhs = [
        jnp.concatenate([parts[level], parts[LEVELS + level]], axis=0) for level in range(LEVELS)
    ]
    drain(names_rcv, names_sem)
    names = jnp.where(own, names_snd[...], names_rcv[...])
    parent = []
    for level in range(LEVELS - 1):
        name = jnp.where(core == 0, names[level : level + 1], names[4 + level : 5 + level])
        parent.append(jnp.broadcast_to(jnp.concatenate([name, name], axis=1), (SHARE, UNKNOWNS)))
    mine, places = core.astype(f32), [(1 - core).astype(f32), 2.0, 3.0]

    def chosen(name, at_place, value):
        return jnp.where(name == at_place, value, 0.0)

    def slot_at(index):
        return 0 if index == 0 else 1 + core

    def gathered(total, buffer, sem):
        drain(buffer, sem)
        for index in range(3):
            total = total + buffer[index]
        return total

    below = []
    take(0)
    to_far(1)
    drain(x_last.at[0:3], last_sem.at[0])
    above = x_sum[y]
    for _, there_y in y_others:
        above = above + x_last[there_y]
    for level in range(LEVELS):
        kinds = kinds_at(level)
        moved = rhs[level] - above
        if level + 1 < LEVELS:
            out = [thin(moved, low_at(level, kind), 1) for kind in range(kinds)]
            if level == 0:
                drain(y_last, last_sem.at[1])
                pending = (y_last[0] + y_last[1]) + (y_last[2] + y_last[3])
            else:
                pending = gathered(own_pending, up_rcv.at[level - 1, 1], up_sem.at[level - 1, 1])
            out[0] = out[0] + pending
            for kind in range(kinds):
                for index in range(3):
                    up_snd[level, kind, index] = chosen(parent[level], places[index], out[kind])
                    send(
                        up_snd.at[level, kind, index], up_rcv.at[level, kind, slot_at(index)],
                        up_snd_sem, up_sem.at[level, kind], partners[level][index],
                    ).start()
            own_pending = chosen(parent[level], mine, out[-1])
            if level == 0:
                to_far(2)
            below.append(thin(thin(moved, inv_at(level), 1), inv_at(level), 0))
            if level + 1 < TRIOS:
                take(level + 1)
            else:
                prepare_local(0)
            own_above = chosen(parent[level], mine, out[0])
            above = gathered(own_above, up_rcv.at[level, 0], up_sem.at[level, 0])

    def send_down(level, kind, value):
        down_snd[level, kind] = value
        for index in range(3):
            send(
                down_snd.at[level, kind], down_rcv.at[level, kind, slot_at(index)],
                down_snd_sem, down_sem.at[level, kind], partners[level][index],
            ).start()

    def pooled(level, kind, value):
        total = chosen(parent[level], mine, value)
        drain(down_rcv.at[level, kind], down_sem.at[level, kind])
        for index in range(3):
            total = total + chosen(parent[level], places[index], down_rcv[level, kind, index])
        return total

    def spread(step, landing, value):
        own_snd[step] = value.reshape(2, OCTET, UNKNOWNS)
        ring_rcv[step, y] = value[0:OCTET]
        for device, _ in y_others:
            send(
                own_snd.at[step, 0], ring_rcv.at[step, y],
                early_snd_sem.at[step], early_sem.at[step, 0], device,
            ).start()
        copies = [
            (
                own_snd.at[step, 1], landing.at[core, y, x_high, 1],
                early_snd_sem.at[step], early_sem.at[step, 1], device,
            )
            for device in x_holders
        ]
        for copy in copies[1:]:
            send(*copy).start()
        send_or_keep(copies[:1])

    def spread_on(step, landing):
        drain(ring_rcv.at[step, 0:3], early_sem.at[step, 0])
        copies = [
            (
                ring_rcv.at[step], landing.at[core, :, x_high, 0],
                late_snd_sem.at[step, 0], late_sem.at[step, 0], device,
            )
            for device in x_holders
        ]
        for copy in copies[1:]:
            send(*copy).start()
        send_or_keep(copies[:1])
        part = landing.at[:, y, :, 1]
        drain(part, early_sem.at[step, 1])
        for device, _ in y_others:
            send(part, part, late_snd_sem.at[step, 1], late_sem.at[step, 1], device).start()

    def spread_end(step, landing):
        drain(landing.at[:, :, :, 0], late_sem.at[step, 0])
        drain(landing.at[:, 0:3, :, 1], late_sem.at[step, 1])

    def whole(landing):
        return landing[...].reshape(2, COLUMNS, UNKNOWNS)

    current, current_parent = thin(moved, inv_at(LEVELS - 1), 0), None
    results = [None] * LEVELS
    results[LEVELS - 1] = current
    for level in range(LEVELS - 2, -1, -1):
        send_down(level, 0, current)
        if level == 0:
            spread(0, next_rcv, current)
            halves = []
            for octet in (slice(0, OCTET), slice(OCTET, SHARE)):
                for part in results[1:] + results[3:]:
                    halves.append(jnp.stack([part[octet, 0:HALF], part[octet, HALF:]], axis=0))
            tiles = regroup(jnp.stack(halves, axis=1))
            for m in range(8):
                for h in range(2):
                    sol_snd[8 * h + m] = tiles[m][h]
            spread_on(0, next_rcv)
            copies = [
                (sol_snd.at[device[1]], sol_rcv.at[core, share], sol_snd_sem, sol_sem, device)
                for device in holders
            ]
            for copy in copies[1:]:
                send(*copy).start()
            send_or_keep(copies[:1])
        else:
            prepare_local(LEVELS - 1 - level)
        left = below[level]
        if kinds_at(level) == 2:
            left = left - thin(pooled(level, 1, current_parent), low_at(level, 1), 0)
        current_parent = pooled(level, 0, current)
        if level > 0:
            send_down(level - 1, 1, current_parent)
        current = left - thin(current_parent, low_at(level, 0), 0)
        results[level] = current
    spread(1, x_rcv, current)

    spread_end(0, next_rcv)
    send(next_rcv, beside_rcv, beside_snd_sem, beside_sem, sibling).start()
    spread_on(1, x_rcv)
    drain(sol_rcv, sol_sem)
    for k in range(2):
        packed = sol_rcv[k].reshape(SHARES * OCTET, 128)
        right = pltpu.roll(packed, 64, 1).reshape(SHARES, OCTET, 128)
        both = jnp.stack([sol_rcv[k], right], axis=1).reshape(COLUMNS, 128)
        strips = both.T
        for level in range(1, LEVELS):
            to = pl.ds(2 * STRIP * level + k, STRIP, stride=2)
            sol_out[to, :] = strips[STRIP * (level - 1) : STRIP * level]
    drain(beside_rcv, beside_sem)
    own_next, beside_next = whole(next_rcv), whole(beside_rcv)
    for i in range(LOCALS):
        grand = None
        for at_place in range(4):
            weight = sum(
                pick[i][k] * jnp.where(lvl_parent[k, 0] == at_place, 1.0, 0.0).astype(f32)
                for k in range(2)
            )
            if at_place < 2:
                term = weight * own_next[at_place]
            else:
                term = weight * beside_next[at_place - 2]
            grand = term if grand is None else grand + term
        y_s[i] = y_s[i] - product(grand, low_high[i, 1], low_rest[i, 1], 0)
    spread_end(1, x_rcv)
    x_all = whole(x_rcv)
    for i in range(LOCALS):
        above_x = pick[i][0] * x_all[0] + pick[i][1] * x_all[1]
        loc_out[i] = (y_s[i] - product(above_x, low_high[i, 0], low_rest[i, 0], 0)).T
    here = pl.ds(pl.multiple_of(STRIP * rows, STRIP), STRIP)
    for k in range(2):
        turned_s[k] = x_all[k].T
        sol_out[pl.ds(k, STRIP, stride=2), :] = turned_s[k, here, :]

    drain(x_part.at[0:3], part_snd_sem.at[0])
    drain(y_part.at[0:3], part_snd_sem.at[1])
    drain(x_last.at[0:3], last_snd_sem.at[0])
    drain(y_last.at[0:3], last_snd_sem.at[1])
    drain(ride_rcv.at[1:], ride_snd_sem)
    drain(names_snd, names_snd_sem)
    for step in range(2):
        for _ in range(2):
            drain(ring_rcv.at[step, 0:3], early_snd_sem.at[step])
        for _ in range(3):
            drain(ring_rcv.at[step], late_snd_sem.at[step, 0])
        drain(x_rcv.at[:, 0:3, :, 1], late_snd_sem.at[step, 1])
    drain(sol_snd.at[1:], sol_snd_sem)
    for _ in range(3):
        drain(strips_s.at[0], strip_snd_sem)
    drain(mats.at[:, 0:3], ring_snd_sem)
    drain(beside_rcv, beside_snd_sem)
    for level in range(LEVELS - 1):
        for kind in range(kinds_at(level)):
            drain(up_rcv.at[level, kind], up_snd_sem)
            drain(down_rcv.at[level, kind], down_snd_sem)

    @pl.when(jnp.logical_not(own))
    def _():
        drain(x_part.at[0], part_snd_sem.at[0])
        drain(y_last.at[0], last_snd_sem.at[1])
        drain(ride_rcv.at[0], ride_snd_sem)
        for step in range(2):
            drain(ring_rcv.at[step, 0], early_snd_sem.at[step])
            drain(ring_rcv.at[step], late_snd_sem.at[step, 0])
        drain(sol_snd.at[0], sol_snd_sem)
        drain(strips_s.at[0], strip_snd_sem)


def on_device(loc_rhs, loc_inv, loc_low, loc_parent, lvl_rhs, lvl_inv, lvl_low, lvl_parent):
    vmem = pl.BlockSpec(memory_space=pltpu.VMEM)
    far = pl.BlockSpec(memory_space=pltpu.HBM)
    dma = pltpu.SemaphoreType.DMA
    square = (UNKNOWNS, UNKNOWNS)
    loc_sol, sol = pl.pallas_call(
        kernel,
        out_shape=(
            jax.ShapeDtypeStruct((LOCALS, UNKNOWNS, COLUMNS), f32),
            jax.ShapeDtypeStruct((COLUMNS, 128), f32),
        ),
        in_specs=[far] * 8,
        out_specs=(vmem, vmem),
        scratch_shapes=[
            pltpu.SMEM((LOCALS,), jnp.int32),
            pltpu.SMEM((2, LEVELS - 1), jnp.int32),
            pltpu.VMEM((LOCALS, UNKNOWNS, COLUMNS), f32),
            pltpu.VMEM((LOCALS,) + square, f32),
            pltpu.VMEM((LOCALS, 2) + square, f32),
            pltpu.VMEM((LEVELS * STRIP * 2, COLUMNS), f32),
            pltpu.VMEM((LOCALS,) + square, bf16),
            pltpu.VMEM((LOCALS,) + square, bf16),
            pltpu.VMEM((LOCALS, 2) + square, bf16),
            pltpu.VMEM((LOCALS, 2) + square, bf16),
            pltpu.VMEM((LOCALS, COLUMNS, UNKNOWNS), f32),
            pltpu.VMEM((2, len(BLOCKS), STRIP, UNKNOWNS), f32),
            pltpu.VMEM((2, 2, 4, 2, SHARE, UNKNOWNS), f32),
            pltpu.VMEM((4, 4, SHARE, UNKNOWNS), f32),
            pltpu.VMEM((4, SHARE, UNKNOWNS), f32),
            pltpu.VMEM((4, 2, 2, SHARE, UNKNOWNS), f32),
            pltpu.VMEM((2, 2, SHARE, UNKNOWNS), f32),
            pltpu.VMEM((4, SHARE, UNKNOWNS), f32),
            pltpu.VMEM((4, SHARE, UNKNOWNS), f32),
            pltpu.VMEM((2, SHARES, OCTET, 128), f32),
            pltpu.VMEM((PEERS, OCTET, 128), f32),
            pltpu.VMEM((OCTET, 128), f32),
            pltpu.VMEM((OCTET, 128), f32),
            pltpu.VMEM((len(BLOCKS), 4, 4 * STRIP, UNKNOWNS), f32),
            pltpu.VMEM((len(BLOCKS),) + square, bf16),
            pltpu.VMEM((len(BLOCKS),) + square, bf16),
            pltpu.VMEM((LEVELS - 1, 2, 3, SHARE, UNKNOWNS), f32),
            pltpu.VMEM((LEVELS - 1, 2, 3, SHARE, UNKNOWNS), f32),
            pltpu.VMEM((LEVELS - 1, 2, SHARE, UNKNOWNS), f32),
            pltpu.VMEM((LEVELS - 1, 2, 3, SHARE, UNKNOWNS), f32),
            pltpu.VMEM((2, 2, OCTET, UNKNOWNS), f32),
            pltpu.VMEM((2, 4, OCTET, UNKNOWNS), f32),
            pltpu.VMEM((2, 4, 2, 2, OCTET, UNKNOWNS), f32),
            pltpu.VMEM((2, 4, 2, 2, OCTET, UNKNOWNS), f32),
            pltpu.VMEM((2, 4, 2, 2, OCTET, UNKNOWNS), f32),
            pltpu.VMEM((PEERS, OCTET, 128), f32),
            pltpu.VMEM((2, SHARES, OCTET, 128), f32),
            pltpu.VMEM((2, UNKNOWNS, COLUMNS), f32),
            dma((6,)),
            dma((len(BLOCKS),)),
            dma((2,)),
            dma((2,)),
            dma((2,)),
            dma((2,)),
            dma,
            dma,
            dma,
            dma,
            dma,
            dma((TRIOS,)),
            dma,
            dma((TRIOS,)),
            dma((TRIOS,)),
            dma,
            dma((LEVELS - 1, 2)),
            dma,
            dma((LEVELS - 1, 2)),
            dma((2,)),
            dma((2, 2)),
            dma((2, 2)),
            dma((2, 2)),
            dma,
            dma,
            dma,
            dma,
        ],
        compiler_params=pltpu.CompilerParams(
            collective_id=0, has_side_effects=True, vmem_limit_bytes=40 * 1024 * 1024
        ),
    )(
        *(
            pltpu.with_memory_space_constraint(operand, pltpu.HBM)
            for operand in (
                loc_parent.reshape(LOCALS),
                loc_rhs.reshape(LOCALS, UNKNOWNS, COLUMNS),
                loc_inv.reshape((LOCALS,) + square),
                loc_low.reshape((LOCALS, 2) + square),
                lvl_rhs.reshape(LEVELS * STRIP * 2, COLUMNS),
                lvl_inv.reshape(LEVELS, 2, STRIP, UNKNOWNS),
                lvl_low.reshape(LEVELS - 1, 2, 2, STRIP, UNKNOWNS),
                lvl_parent.reshape(LEVELS - 1, 2).T,
            )
        )
    )
    return loc_sol[None, None], sol.reshape(1, LEVELS, STRIP, 2, COLUMNS)


def solution(mesh):
    in_specs = (
        P("leaf", "rows", None, None, None),
        P("leaf", "rows", None, None, None),
        P("leaf", "rows", None, None, None, None),
        P("leaf", "rows", None),
        P("leaf", None, "rows", None, None),
        P("leaf", None, None, "rows", None),
        P("leaf", None, None, None, "rows", None),
        P("leaf", None, None),
    )
    out_specs = (P("leaf", "rows", None, None, None), P("leaf", None, "rows", None, None))
    return jax.shard_map(
        on_device, mesh=mesh, in_specs=in_specs, out_specs=out_specs, check_vma=False
    )
```

```python
import functools

import jax
import jax.numpy as jnp
from jax import lax
from jax.experimental import pallas as pl
from jax.experimental.pallas import tpu as pltpu
from jax.sharding import PartitionSpec as P

MESH = pl.DeviceIdType.MESH
f32 = jnp.float32
bf16 = jnp.bfloat16

UNKNOWNS = 256
COLUMNS = 128
STRIP = 16
SHARE = 16
SHARES = 8
PEERS = 16
LOCALS = 3
LEVELS = 4
HALF = UNKNOWNS // 2
OCTET = 8
BLOCKS = (("inv", 0), ("low", 0, 0), ("low", 0, 1), ("inv", 1), ("low", 1, 0), ("low", 1, 1), ("inv", 2), ("low", 2, 0), ("inv", 3))
TRIOS = 3


def split(value):
    high = value.astype(bf16)
    return high, (value - high.astype(f32)).astype(bf16)


def dot(left, right, dim):
    return lax.dot_general(
        left, right, (((1,), (dim,)), ((), ())), preferred_element_type=f32
    )


def multiply(left, right, dim):
    return dot(left[0], right[0], dim) + dot(left[1], right[0], dim) + dot(left[0], right[1], dim)


def product(vectors, mat_high, mat_low, dim):
    return multiply(split(vectors), (mat_high, mat_low), dim)


def thin_product(vectors, mat_high, mat_low, dim):
    high = vectors.astype(bf16).astype(f32)
    both = jnp.concatenate([high, vectors - high], axis=0).astype(bf16)
    total = dot(both, mat_high, dim) + dot(both, mat_low, dim)
    return total[:SHARE] + total[SHARE:]


def regroup(tiles):
    group = lax.div(lax.broadcasted_iota(jnp.int32, (2, OCTET, 128), 2), STRIP)
    flat = tiles.reshape(PEERS * OCTET, 128)
    turned = [flat.reshape(2, 8, OCTET, 128)]
    for turn in range(1, 8):
        turned.append(pltpu.roll(flat, STRIP * turn, 1).reshape(2, 8, OCTET, 128))
    results = []
    for g in range(8):
        total = turned[-g % 8][:, 0]
        for m in range(1, 8):
            total = jnp.where(group == m, turned[(m - g) % 8][:, m], total)
        results.append(total)
    return results


def kinds_at(level):
    return 2 if level + 2 < LEVELS else 1


def inv_at(level):
    return BLOCKS.index(("inv", level))


def low_at(level, kind):
    return BLOCKS.index(("low", level, kind))


def trio(index):
    return slice(3 * index, 3 * index + 3)


def kernel(
    loc_names, loc_rhs, loc_inv, loc_low, lvl_rhs, lvl_inv, lvl_low, lvl_names,
    loc_out, sol_out,
    loc_parent, lvl_parent, rhs_s, inv_s, low_s, lvl_rhs_s, inv_high, inv_rest, low_high, low_rest, y_s,
    strips_s, snd, x_part, x_sum, y_part, y_sum, x_last, y_last, ride_snd, ride_rcv, names_snd, names_rcv,
    mats, mat_high, mat_rest, up_snd, up_rcv, down_snd, down_rcv,
    own_snd, ring_rcv, x_rcv, next_rcv, beside_rcv, sol_snd, sol_rcv, turned_s,
    load_sem, strips_sem, part_snd_sem, part_sem, last_snd_sem, last_sem,
    ride_snd_sem, ride_sem, names_snd_sem, names_sem, strip_snd_sem, strip_sem, ring_snd_sem, ring_sem, far_sem,
    pair_snd_sem, pair_sem, up_snd_sem, up_sem, down_snd_sem, down_sem, early_snd_sem, early_sem, late_snd_sem, late_sem,
    sol_snd_sem, sol_sem, beside_snd_sem, beside_sem,
):
    leaf = lax.axis_index("leaf")
    rows = lax.axis_index("rows")
    z, core = lax.div(leaf, 2), lax.rem(leaf, 2)
    y, x = lax.div(rows, 4), lax.rem(rows, 4)
    x_high, parity = lax.div(x, 2), lax.rem(x, 2)
    carried = 2 * z + x_high
    place = jnp.where(x_high == 0, parity, 1 - parity)
    share = 2 * y + core
    own = x_high == core

    def x_of(odd, slot):
        return 2 * odd + jnp.where(odd == 0, slot, 1 - slot)

    def around(value):
        return [value] + [jnp.where(value + n >= 4, value + n - 4, value + n) for n in range(1, 4)]

    slots, cores = [place, 1 - place], [core, 1 - core]
    ys, xs = around(y), around(x)
    carriers = [
        ((2 * z + there_core, 4 * there_y + x_of(core, slot)), 2 * there_y + there_core, slot)
        for there_y in ys
        for slot in slots
        for there_core in cores
    ]
    holders = [(carried, 4 * there_y + there_x) for there_y in ys for there_x in xs]
    x_carriers = [
        ((2 * z + there_core, 4 * y + x_of(core, slot)), slot, there_core)
        for slot in slots
        for there_core in cores
    ]
    x_holders = [(carried, 4 * y + there_x) for there_x in xs]
    sibling = (2 * z + 1 - core, rows)
    z_half = lax.rem(lax.div(z, 2), 2)
    beside = (leaf, rows + 1 - 2 * parity)
    partners = [[beside] + [(leaf, 4 * y + x_of(1 - x_high, slot)) for slot in range(2)]]
    for there_z in (z + 1 - 2 * lax.rem(z, 2), z + 2 - 4 * z_half):
        partners.append(
            [beside] + [(2 * there_z + core, 4 * y + x_of(x_high, slot)) for slot in range(2)]
        )
    y_up, y_far, y_down = ys[1], ys[2], ys[3]
    up, far, down = [(leaf, 4 * there_y + x) for there_y in (y_up, y_far, y_down)]

    loads = [
        pltpu.make_async_copy(loc_rhs, rhs_s, load_sem.at[0]),
        pltpu.make_async_copy(loc_inv, inv_s, load_sem.at[1]),
        pltpu.make_async_copy(loc_low, low_s, load_sem.at[2]),
        pltpu.make_async_copy(lvl_rhs, lvl_rhs_s, load_sem.at[3]),
        pltpu.make_async_copy(loc_names, loc_parent, load_sem.at[4]),
        pltpu.make_async_copy(lvl_names, lvl_parent, load_sem.at[5]),
    ]
    strip_loads = [
        pltpu.make_async_copy(
            lvl_inv.at[level], strips_s.at[:, inv_at(level)], strips_sem.at[inv_at(level)]
        )
        for level in range(LEVELS)
    ] + [
        pltpu.make_async_copy(
            lvl_low.at[level, :, 0 : kinds_at(level)],
            strips_s.at[:, low_at(level, 0) : low_at(level, 0) + kinds_at(level)],
            strips_sem.at[low_at(level, 0)],
        )
        for level in range(LEVELS - 1)
    ]
    for load in loads + strip_loads:
        load.start()

    barrier = pltpu.get_barrier_semaphore()

    def greet(device):
        pl.semaphore_signal(barrier, inc=1, device_id=device, device_id_type=MESH)

    others = [carrier[0] for carrier in carriers[1:]] + holders[1:] + [sibling, beside, up, far, down]
    others += [device for three in partners for device in three[1:]]
    for device in others:
        greet(device)

    @pl.when(jnp.logical_not(own))
    def _():
        greet(carriers[0][0])
        greet(holders[0])

    for load in loads[:2]:
        load.wait()
    for i in range(LOCALS):
        high, rest = split(inv_s[i])
        inv_high[i] = high
        inv_rest[i] = rest
        y_s[i] = product(rhs_s[i].T, high, rest, 1)
    pl.semaphore_wait(barrier, len(others) + jnp.where(own, 0, 2))

    def send(src, dst, send_sem, recv_sem, device):
        return pltpu.make_async_remote_copy(
            src_ref=src, dst_ref=dst, send_sem=send_sem, recv_sem=recv_sem,
            device_id=device, device_id_type=MESH,
        )

    def send_or_keep(copies):
        @pl.when(own)
        def _():
            for src, dst, send_sem, recv_sem, device in copies:
                pltpu.make_async_copy(src, dst, recv_sem).start()

        @pl.when(jnp.logical_not(own))
        def _():
            for copy in copies:
                send(*copy).start()

    def drain(ref, sem):
        pltpu.make_async_copy(ref, ref, sem).wait()

    strip = pl.ds(pl.multiple_of(STRIP * parity, STRIP), STRIP)
    first, second = slice(0, STRIP), slice(STRIP, 2 * STRIP)

    def along_x(index):
        copies = [
            (
                strips_s.at[slot, trio(index)], mats.at[trio(index), y, x_high, strip, :],
                strip_snd_sem, strip_sem.at[index], (2 * z + x_high, 4 * y + x_of(core, slot)),
            )
            for slot in slots
        ]
        send(*copies[1]).start()
        send_or_keep(copies[:1])

    def along_y(index):
        part = mats.at[trio(index), y, core]
        drain(part, strip_sem.at[index])
        for device in (up, down):
            send(part, part, ring_snd_sem, ring_sem.at[index], device).start()
        if index == 0:
            send(part, part, ring_snd_sem, far_sem.at[index], far).start()

    def to_far(index):
        drain(mats.at[trio(index), 0:2, core], ring_sem.at[index])
        for at_y, half_strip, device in ((y_down, first, up), (y_up, second, down)):
            part = mats.at[trio(index), at_y, core, half_strip, :]
            send(part, part, ring_snd_sem, far_sem.at[index], device).start()

    def to_sibling(index):
        if index == 0:
            drain(mats.at[trio(index), 0:2, core], ring_sem.at[index])
        drain(mats.at[trio(index), y_far, core], far_sem.at[index])
        part = mats.at[trio(index), :, core]
        send(part, part, pair_snd_sem, pair_sem.at[index], sibling).start()

    def take(index):
        drain(mats.at[trio(index), :, 1 - core], pair_sem.at[index])
        parts = {}
        for m in range(3 * index, 3 * index + 3):
            parts[BLOCKS[m]] = split(mats[m].reshape(UNKNOWNS, UNKNOWNS))
            if BLOCKS[m][0] == "inv":
                mat_high[m], mat_rest[m] = parts[BLOCKS[m]]
        for m in range(3 * index, 3 * index + 3):
            name, level = BLOCKS[m][:2]
            if name == "low":
                mat_high[m], mat_rest[m] = split(multiply(parts[BLOCKS[m]], parts["inv", level], 0))
            elif level + 1 == LEVELS:
                turned = split(mats[m].reshape(UNKNOWNS, UNKNOWNS).T)
                mat_high[m], mat_rest[m] = split(multiply(turned, parts[BLOCKS[m]], 0))

    def thin(vectors, m, dim):
        return thin_product(vectors, mat_high[m], mat_rest[m], dim)

    for load in strip_loads:
        load.wait()
    along_x(0)
    for load in loads[2:]:
        load.wait()
    pick = [
        [jnp.where(loc_parent[i] == slot, 1.0, 0.0).astype(f32) for slot in range(2)]
        for i in range(LOCALS)
    ]

    y_others = [(up, y_up), (far, y_far), (down, y_down)]

    def local_updates(kind):
        for i in range(LOCALS):
            high, rest = split(low_s[i, kind])
            low_high[i, kind] = high
            low_rest[i, kind] = rest
            update = product(y_s[i], high, rest, 1).reshape(4, 2, SHARE, UNKNOWNS)
            for slot in range(2):
                if i == 0:
                    snd[kind, slot] = pick[i][slot] * update
                else:
                    snd[kind, slot] += pick[i][slot] * update

    def x_first():
        copies = [
            (snd.at[0, slot, :, there_core], x_part.at[x], part_snd_sem.at[0], part_sem.at[0], device)
            for device, slot, there_core in x_carriers
        ]
        for copy in copies[1:]:
            send(*copy).start()
        send_or_keep(copies[:1])

    def x_then_y():
        drain(x_part, part_sem.at[0])
        x_sum[...] = (x_part[0] + x_part[1]) + (x_part[2] + x_part[3])
        for device, there_y in y_others:
            send(
                x_sum.at[there_y], x_last.at[y], last_snd_sem.at[0], last_sem.at[0], device
            ).start()

    def y_first():
        for device, there_y in y_others:
            send(
                snd.at[1, :, there_y], y_part.at[y], part_snd_sem.at[1], part_sem.at[1], device
            ).start()

    def y_then_x():
        drain(y_part.at[0:3], part_sem.at[1])
        total = snd[1, :, y]
        for _, there_y in y_others:
            total = total + y_part[there_y]
        y_sum[...] = total
        copies = [
            (y_sum.at[slot, there_core], y_last.at[x], last_snd_sem.at[1], last_sem.at[1], device)
            for device, slot, there_core in x_carriers
        ]
        for copy in copies[1:]:
            send(*copy).start()
        send_or_keep(copies[:1])

    local_updates(0)
    x_first()
    along_y(0)
    along_x(1)
    along_x(2)
    local_updates(1)
    y_first()
    row = lax.broadcasted_iota(jnp.int32, (OCTET, 128), 0)
    names = jnp.zeros((OCTET, 128), f32)
    for k in range(2):
        for level in range(LEVELS - 1):
            names = jnp.where(row == 4 * k + level, lvl_parent[k, level].astype(f32), names)
    names_snd[...] = names
    send(names_snd, names_rcv, names_snd_sem, names_sem, sibling).start()
    for k in range(2):
        strips = [
            lvl_rhs_s[pl.ds(2 * STRIP * level + k, STRIP, stride=2), :] for level in range(LEVELS)
        ]
        strips.append(jnp.zeros((HALF - LEVELS * STRIP, COLUMNS), f32))
        extra = jnp.concatenate(strips, axis=0).T.reshape(SHARES, 2, OCTET, 128)
        right = pltpu.roll(extra[:, 1].reshape(SHARES * OCTET, 128), 64, 1)
        ride_snd[k] = extra[:, 0] + right.reshape(SHARES, OCTET, 128)
    rides = [
        (ride_snd.at[slot, index], ride_rcv.at[rows], ride_snd_sem, ride_sem, device)
        for device, index, slot in carriers
    ]
    for ride in rides[1:]:
        send(*ride).start()
    send_or_keep(rides[:1])
    along_y(1)
    x_then_y()
    along_y(2)

    def prepare_local(i):
        inverse = (inv_high[i], inv_rest[i])
        y_s[i] = product(y_s[i], inv_high[i], inv_rest[i], 0)
        for kind in range(2):
            high, rest = split(multiply((low_high[i, kind], low_rest[i, kind]), inverse, 0))
            low_high[i, kind] = high
            low_rest[i, kind] = rest

    to_sibling(0)
    y_then_x()
    drain(ride_rcv, ride_sem)
    parts = regroup(ride_rcv[...].reshape(2, 8, OCTET, 128))
    parts = [jnp.concatenate([part[0], part[1]], axis=1) for part in parts]
    rhs = [
        jnp.concatenate([parts[level], parts[LEVELS + level]], axis=0) for level in range(LEVELS)
    ]
    drain(names_rcv, names_sem)
    names = jnp.where(own, names_snd[...], names_rcv[...])
    parent = []
    for level in range(LEVELS - 1):
        name = jnp.where(place == 0, names[level : level + 1], names[4 + level : 5 + level])
        parent.append(jnp.broadcast_to(jnp.concatenate([name, name], axis=1), (SHARE, UNKNOWNS)))
    mine, places = place.astype(f32), [(1 - place).astype(f32), 2.0, 3.0]

    def chosen(name, at_place, value):
        return jnp.where(name == at_place, value, 0.0)

    def slot_at(index):
        return 0 if index == 0 else 1 + place

    def gathered(total, buffer, sem):
        drain(buffer, sem)
        for index in range(3):
            total = total + buffer[index]
        return total

    below = []
    take(0)
    to_far(1)
    drain(x_last.at[0:3], last_sem.at[0])
    above = x_sum[y]
    for _, there_y in y_others:
        above = above + x_last[there_y]
    for level in range(LEVELS):
        kinds = kinds_at(level)
        moved = rhs[level] - above
        if level + 1 < LEVELS:
            out = [thin(moved, low_at(level, kind), 1) for kind in range(kinds)]
            if level == 0:
                drain(y_last, last_sem.at[1])
                pending = (y_last[0] + y_last[1]) + (y_last[2] + y_last[3])
            else:
                pending = gathered(own_pending, up_rcv.at[level - 1, 1], up_sem.at[level - 1, 1])
            out[0] = out[0] + pending
            for kind in range(kinds):
                for index in range(3):
                    up_snd[level, kind, index] = chosen(parent[level], places[index], out[kind])
                    send(
                        up_snd.at[level, kind, index], up_rcv.at[level, kind, slot_at(index)],
                        up_snd_sem, up_sem.at[level, kind], partners[level][index],
                    ).start()
            own_pending = chosen(parent[level], mine, out[-1])
            if level == 0:
                to_sibling(1)
                to_far(2)
            below.append(thin(thin(moved, inv_at(level), 1), inv_at(level), 0))
            if level + 1 < TRIOS:
                take(level + 1)
            else:
                prepare_local(0)
            if level == 0:
                to_sibling(2)
            own_above = chosen(parent[level], mine, out[0])
            above = gathered(own_above, up_rcv.at[level, 0], up_sem.at[level, 0])

    def send_down(level, kind, value):
        down_snd[level, kind] = value
        for index in range(3):
            send(
                down_snd.at[level, kind], down_rcv.at[level, kind, slot_at(index)],
                down_snd_sem, down_sem.at[level, kind], partners[level][index],
            ).start()

    def pooled(level, kind, value):
        total = chosen(parent[level], mine, value)
        drain(down_rcv.at[level, kind], down_sem.at[level, kind])
        for index in range(3):
            total = total + chosen(parent[level], places[index], down_rcv[level, kind, index])
        return total

    def spread(step, landing, value):
        own_snd[step] = value.reshape(2, OCTET, UNKNOWNS)
        ring_rcv[step, y] = value[0:OCTET]
        for device, _ in y_others:
            send(
                own_snd.at[step, 0], ring_rcv.at[step, y],
                early_snd_sem.at[step], early_sem.at[step, 0], device,
            ).start()
        copies = [
            (
                own_snd.at[step, 1], landing.at[place, y, core, 1],
                early_snd_sem.at[step], early_sem.at[step, 1], device,
            )
            for device in x_holders
        ]
        for copy in copies[1:]:
            send(*copy).start()
        send_or_keep(copies[:1])

    def spread_on(step, landing):
        drain(ring_rcv.at[step, 0:3], early_sem.at[step, 0])
        copies = [
            (
                ring_rcv.at[step], landing.at[place, :, core, 0],
                late_snd_sem.at[step, 0], late_sem.at[step, 0], device,
            )
            for device in x_holders
        ]
        for copy in copies[1:]:
            send(*copy).start()
        send_or_keep(copies[:1])
        part = landing.at[:, y, :, 1]
        drain(part, early_sem.at[step, 1])
        for device, _ in y_others:
            send(part, part, late_snd_sem.at[step, 1], late_sem.at[step, 1], device).start()

    def spread_end(step, landing):
        drain(landing.at[:, :, :, 0], late_sem.at[step, 0])
        drain(landing.at[:, 0:3, :, 1], late_sem.at[step, 1])

    def whole(landing):
        return landing[...].reshape(2, COLUMNS, UNKNOWNS)

    current, current_parent = thin(moved, inv_at(LEVELS - 1), 0), None
    results = [None] * LEVELS
    results[LEVELS - 1] = current
    for level in range(LEVELS - 2, -1, -1):
        send_down(level, 0, current)
        if level == 0:
            spread(0, next_rcv, current)
            spread_on(0, next_rcv)
        else:
            prepare_local(LEVELS - 1 - level)
        left = below[level]
        if kinds_at(level) == 2:
            left = left - thin(pooled(level, 1, current_parent), low_at(level, 1), 0)
        current_parent = pooled(level, 0, current)
        if level > 0:
            send_down(level - 1, 1, current_parent)
        current = left - thin(current_parent, low_at(level, 0), 0)
        results[level] = current
    spread(1, x_rcv, current)

    spread_end(0, next_rcv)
    send(next_rcv, beside_rcv, beside_snd_sem, beside_sem, sibling).start()
    halves = []
    for octet in (slice(0, OCTET), slice(OCTET, SHARE)):
        for part in results[1:] + results[3:]:
            halves.append(jnp.stack([part[octet, 0:HALF], part[octet, HALF:]], axis=0))
    tiles = regroup(jnp.stack(halves, axis=1))
    for m in range(8):
        for h in range(2):
            sol_snd[8 * h + m] = tiles[m][h]
    spread_on(1, x_rcv)
    copies = [
        (sol_snd.at[device[1]], sol_rcv.at[place, share], sol_snd_sem, sol_sem, device)
        for device in holders
    ]
    for copy in copies[1:]:
        send(*copy).start()
    send_or_keep(copies[:1])
    drain(beside_rcv, beside_sem)
    own_next, beside_next = whole(next_rcv), whole(beside_rcv)
    for i in range(LOCALS):
        grand = None
        for at_place in range(4):
            weight = sum(
                pick[i][k] * jnp.where(lvl_parent[k, 0] == at_place, 1.0, 0.0).astype(f32)
                for k in range(2)
            )
            if at_place < 2:
                term = weight * own_next[at_place]
            else:
                term = weight * beside_next[at_place - 2]
            grand = term if grand is None else grand + term
        y_s[i] = y_s[i] - product(grand, low_high[i, 1], low_rest[i, 1], 0)
    drain(x_part.at[0:3], part_snd_sem.at[0])
    drain(y_part.at[0:3], part_snd_sem.at[1])
    drain(x_last.at[0:3], last_snd_sem.at[0])
    drain(y_last.at[0:3], last_snd_sem.at[1])
    drain(ride_rcv.at[1:], ride_snd_sem)
    drain(names_snd, names_snd_sem)
    for step in range(2):
        for _ in range(2):
            drain(ring_rcv.at[step, 0:3], early_snd_sem.at[step])
        for _ in range(3):
            drain(ring_rcv.at[step], late_snd_sem.at[step, 0])
        drain(x_rcv.at[:, 0:3, :, 1], late_snd_sem.at[step, 1])
    drain(sol_snd.at[1:], sol_snd_sem)
    drain(strips_s.at[0], strip_snd_sem)
    drain(mats.at[:, 0:3, 0], ring_snd_sem)
    drain(mats.at[:, :, 0], pair_snd_sem)
    drain(beside_rcv, beside_snd_sem)
    for level in range(LEVELS - 1):
        for kind in range(kinds_at(level)):
            drain(up_rcv.at[level, kind], up_snd_sem)
            drain(down_rcv.at[level, kind], down_snd_sem)

    @pl.when(jnp.logical_not(own))
    def _():
        drain(x_part.at[0], part_snd_sem.at[0])
        drain(y_last.at[0], last_snd_sem.at[1])
        drain(ride_rcv.at[0], ride_snd_sem)
        for step in range(2):
            drain(ring_rcv.at[step, 0], early_snd_sem.at[step])
            drain(ring_rcv.at[step], late_snd_sem.at[step, 0])
        drain(sol_snd.at[0], sol_snd_sem)
        drain(strips_s.at[0], strip_snd_sem)

    spread_end(1, x_rcv)
    x_all = whole(x_rcv)
    for i in range(LOCALS):
        above_x = pick[i][0] * x_all[0] + pick[i][1] * x_all[1]
        loc_out[i] = (y_s[i] - product(above_x, low_high[i, 0], low_rest[i, 0], 0)).T
    here = pl.ds(pl.multiple_of(STRIP * rows, STRIP), STRIP)
    for k in range(2):
        turned_s[k] = x_all[k].T
        sol_out[pl.ds(k, STRIP, stride=2), :] = turned_s[k, here, :]
    drain(sol_rcv, sol_sem)
    for k in range(2):
        packed = sol_rcv[k].reshape(SHARES * OCTET, 128)
        right = pltpu.roll(packed, 64, 1).reshape(SHARES, OCTET, 128)
        both = jnp.stack([sol_rcv[k], right], axis=1).reshape(COLUMNS, 128)
        strips = both.T
        for level in range(1, LEVELS):
            to = pl.ds(2 * STRIP * level + k, STRIP, stride=2)
            sol_out[to, :] = strips[STRIP * (level - 1) : STRIP * level]


def on_device(loc_rhs, loc_inv, loc_low, loc_parent, lvl_rhs, lvl_inv, lvl_low, lvl_parent):
    vmem = pl.BlockSpec(memory_space=pltpu.VMEM)
    far = pl.BlockSpec(memory_space=pltpu.HBM)
    dma = pltpu.SemaphoreType.DMA
    square = (UNKNOWNS, UNKNOWNS)
    loc_sol, sol = pl.pallas_call(
        kernel,
        out_shape=(
            jax.ShapeDtypeStruct((LOCALS, UNKNOWNS, COLUMNS), f32),
            jax.ShapeDtypeStruct((COLUMNS, 128), f32),
        ),
        in_specs=[far] * 8,
        out_specs=(vmem, vmem),
        scratch_shapes=[
            pltpu.SMEM((LOCALS,), jnp.int32),
            pltpu.SMEM((2, LEVELS - 1), jnp.int32),
            pltpu.VMEM((LOCALS, UNKNOWNS, COLUMNS), f32),
            pltpu.VMEM((LOCALS,) + square, f32),
            pltpu.VMEM((LOCALS, 2) + square, f32),
            pltpu.VMEM((LEVELS * STRIP * 2, COLUMNS), f32),
            pltpu.VMEM((LOCALS,) + square, bf16),
            pltpu.VMEM((LOCALS,) + square, bf16),
            pltpu.VMEM((LOCALS, 2) + square, bf16),
            pltpu.VMEM((LOCALS, 2) + square, bf16),
            pltpu.VMEM((LOCALS, COLUMNS, UNKNOWNS), f32),
            pltpu.VMEM((2, len(BLOCKS), STRIP, UNKNOWNS), f32),
            pltpu.VMEM((2, 2, 4, 2, SHARE, UNKNOWNS), f32),
            pltpu.VMEM((4, 4, SHARE, UNKNOWNS), f32),
            pltpu.VMEM((4, SHARE, UNKNOWNS), f32),
            pltpu.VMEM((4, 2, 2, SHARE, UNKNOWNS), f32),
            pltpu.VMEM((2, 2, SHARE, UNKNOWNS), f32),
            pltpu.VMEM((4, SHARE, UNKNOWNS), f32),
            pltpu.VMEM((4, SHARE, UNKNOWNS), f32),
            pltpu.VMEM((2, SHARES, OCTET, 128), f32),
            pltpu.VMEM((PEERS, OCTET, 128), f32),
            pltpu.VMEM((OCTET, 128), f32),
            pltpu.VMEM((OCTET, 128), f32),
            pltpu.VMEM((len(BLOCKS), 4, 2, 2 * STRIP, UNKNOWNS), f32),
            pltpu.VMEM((len(BLOCKS),) + square, bf16),
            pltpu.VMEM((len(BLOCKS),) + square, bf16),
            pltpu.VMEM((LEVELS - 1, 2, 3, SHARE, UNKNOWNS), f32),
            pltpu.VMEM((LEVELS - 1, 2, 3, SHARE, UNKNOWNS), f32),
            pltpu.VMEM((LEVELS - 1, 2, SHARE, UNKNOWNS), f32),
            pltpu.VMEM((LEVELS - 1, 2, 3, SHARE, UNKNOWNS), f32),
            pltpu.VMEM((2, 2, OCTET, UNKNOWNS), f32),
            pltpu.VMEM((2, 4, OCTET, UNKNOWNS), f32),
            pltpu.VMEM((2, 4, 2, 2, OCTET, UNKNOWNS), f32),
            pltpu.VMEM((2, 4, 2, 2, OCTET, UNKNOWNS), f32),
            pltpu.VMEM((2, 4, 2, 2, OCTET, UNKNOWNS), f32),
            pltpu.VMEM((PEERS, OCTET, 128), f32),
            pltpu.VMEM((2, SHARES, OCTET, 128), f32),
            pltpu.VMEM((2, UNKNOWNS, COLUMNS), f32),
            dma((6,)),
            dma((len(BLOCKS),)),
            dma((2,)),
            dma((2,)),
            dma((2,)),
            dma((2,)),
            dma,
            dma,
            dma,
            dma,
            dma,
            dma((TRIOS,)),
            dma,
            dma((TRIOS,)),
            dma((TRIOS,)),
            dma,
            dma((TRIOS,)),
            dma,
            dma((LEVELS - 1, 2)),
            dma,
            dma((LEVELS - 1, 2)),
            dma((2,)),
            dma((2, 2)),
            dma((2, 2)),
            dma((2, 2)),
            dma,
            dma,
            dma,
            dma,
        ],
        compiler_params=pltpu.CompilerParams(
            collective_id=0, has_side_effects=True, vmem_limit_bytes=40 * 1024 * 1024
        ),
    )(
        *(
            pltpu.with_memory_space_constraint(operand, pltpu.HBM)
            for operand in (
                loc_parent.reshape(LOCALS),
                loc_rhs.reshape(LOCALS, UNKNOWNS, COLUMNS),
                loc_inv.reshape((LOCALS,) + square),
                loc_low.reshape((LOCALS, 2) + square),
                lvl_rhs.reshape(LEVELS * STRIP * 2, COLUMNS),
                lvl_inv.reshape(LEVELS, 2, STRIP, UNKNOWNS),
                lvl_low.reshape(LEVELS - 1, 2, 2, STRIP, UNKNOWNS),
                lvl_parent.reshape(LEVELS - 1, 2).T,
            )
        )
    )
    return loc_sol[None, None], sol.reshape(1, LEVELS, STRIP, 2, COLUMNS)


def solution(mesh):
    in_specs = (
        P("leaf", "rows", None, None, None),
        P("leaf", "rows", None, None, None),
        P("leaf", "rows", None, None, None, None),
        P("leaf", "rows", None),
        P("leaf", None, "rows", None, None),
        P("leaf", None, None, "rows", None),
        P("leaf", None, None, None, "rows", None),
        P("leaf", None, None),
    )
    out_specs = (P("leaf", "rows", None, None, None), P("leaf", None, "rows", None, None))
    return jax.shard_map(
        on_device, mesh=mesh, in_specs=in_specs, out_specs=out_specs, check_vma=False
    )
```

```python
import functools

import jax
import jax.numpy as jnp
from jax import lax
from jax.experimental import pallas as pl
from jax.experimental.pallas import tpu as pltpu
from jax.sharding import PartitionSpec as P

MESH = pl.DeviceIdType.MESH
f32 = jnp.float32
bf16 = jnp.bfloat16

UNKNOWNS = 256
COLUMNS = 128
STRIP = 16
SHARE = 16
SHARES = 8
PEERS = 16
LOCALS = 3
LEVELS = 4
HALF = UNKNOWNS // 2
OCTET = 8
BLOCKS = (("inv", 0), ("low", 0, 0), ("low", 0, 1), ("inv", 1), ("low", 1, 0), ("low", 1, 1), ("inv", 2), ("low", 2, 0), ("inv", 3))
TRIOS = 3


def split(value):
    high = value.astype(bf16)
    return high, (value - high.astype(f32)).astype(bf16)


def dot(left, right, dim):
    return lax.dot_general(
        left, right, (((1,), (dim,)), ((), ())), preferred_element_type=f32
    )


def multiply(left, right, dim):
    return dot(left[0], right[0], dim) + dot(left[1], right[0], dim) + dot(left[0], right[1], dim)


def product(vectors, mat_high, mat_low, dim):
    return multiply(split(vectors), (mat_high, mat_low), dim)


def thin_product(vectors, mat_high, mat_low, dim):
    high = vectors.astype(bf16).astype(f32)
    both = jnp.concatenate([high, vectors - high], axis=0).astype(bf16)
    total = dot(both, mat_high, dim) + dot(both, mat_low, dim)
    return total[:SHARE] + total[SHARE:]


def regroup(tiles):
    group = lax.div(lax.broadcasted_iota(jnp.int32, (2, OCTET, 128), 2), STRIP)
    flat = tiles.reshape(PEERS * OCTET, 128)
    turned = [flat.reshape(2, 8, OCTET, 128)]
    for turn in range(1, 8):
        turned.append(pltpu.roll(flat, STRIP * turn, 1).reshape(2, 8, OCTET, 128))
    results = []
    for g in range(8):
        total = turned[-g % 8][:, 0]
        for m in range(1, 8):
            total = jnp.where(group == m, turned[(m - g) % 8][:, m], total)
        results.append(total)
    return results


def kinds_at(level):
    return 2 if level + 2 < LEVELS else 1


def inv_at(level):
    return BLOCKS.index(("inv", level))


def low_at(level, kind):
    return BLOCKS.index(("low", level, kind))


def trio(index):
    return slice(3 * index, 3 * index + 3)


def kernel(
    loc_names, loc_rhs, loc_inv, loc_low, lvl_rhs, lvl_inv, lvl_low, lvl_names,
    loc_out, sol_out,
    loc_parent, lvl_parent, rhs_s, inv_s, low_s, lvl_rhs_s, inv_high, inv_rest, low_high, low_rest, y_s,
    strips_s, snd, x_part, x_sum, x_last, y_last, ride_snd, ride_rcv, names_snd, names_rcv,
    mats, mat_high, mat_rest, up_snd, up_rcv, down_snd, down_rcv,
    own_snd, ring_rcv, x_rcv, next_rcv, beside_rcv, sol_snd, sol_rcv, turned_s,
    load_sem, strips_sem, part_snd_sem, part_sem, last_snd_sem, last_sem,
    ride_snd_sem, ride_sem, names_snd_sem, names_sem, strip_snd_sem, strip_sem, ring_snd_sem, ring_sem, far_sem,
    pair_snd_sem, pair_sem, up_snd_sem, up_sem, down_snd_sem, down_sem, early_snd_sem, early_sem, late_snd_sem, late_sem,
    sol_snd_sem, sol_sem, beside_snd_sem, beside_sem,
):
    leaf = lax.axis_index("leaf")
    rows = lax.axis_index("rows")
    z, core = lax.div(leaf, 2), lax.rem(leaf, 2)
    y, x = lax.div(rows, 4), lax.rem(rows, 4)
    x_high, parity = lax.div(x, 2), lax.rem(x, 2)
    carried = 2 * z + x_high
    place = jnp.where(x_high == 0, parity, 1 - parity)
    share = 2 * y + core
    own = x_high == core

    def x_of(odd, slot):
        return 2 * odd + jnp.where(odd == 0, slot, 1 - slot)

    def around(value):
        return [value] + [jnp.where(value + n >= 4, value + n - 4, value + n) for n in range(1, 4)]

    slots, cores = [place, 1 - place], [core, 1 - core]
    ys, xs = around(y), around(x)
    carriers = [
        ((2 * z + there_core, 4 * there_y + x_of(core, slot)), 2 * there_y + there_core, slot)
        for there_y in ys
        for slot in slots
        for there_core in cores
    ]
    carrier_shares = [(there_y, there_core) for there_y in ys for _ in slots for there_core in cores]
    holders = [(carried, 4 * there_y + there_x) for there_y in ys for there_x in xs]
    x_carriers = [
        ((2 * z + there_core, 4 * y + x_of(core, slot)), slot, there_core)
        for slot in slots
        for there_core in cores
    ]
    x_holders = [(carried, 4 * y + there_x) for there_x in xs]
    sibling = (2 * z + 1 - core, rows)
    z_half = lax.rem(lax.div(z, 2), 2)
    beside = (leaf, rows + 1 - 2 * parity)
    partners = [[beside] + [(leaf, 4 * y + x_of(1 - x_high, slot)) for slot in range(2)]]
    for there_z in (z + 1 - 2 * lax.rem(z, 2), z + 2 - 4 * z_half):
        partners.append(
            [beside] + [(2 * there_z + core, 4 * y + x_of(x_high, slot)) for slot in range(2)]
        )
    y_up, y_far, y_down = ys[1], ys[2], ys[3]
    up, far, down = [(leaf, 4 * there_y + x) for there_y in (y_up, y_far, y_down)]

    loads = [
        pltpu.make_async_copy(loc_rhs, rhs_s, load_sem.at[0]),
        pltpu.make_async_copy(loc_inv, inv_s, load_sem.at[1]),
        pltpu.make_async_copy(loc_low, low_s, load_sem.at[2]),
        pltpu.make_async_copy(lvl_rhs, lvl_rhs_s, load_sem.at[3]),
        pltpu.make_async_copy(loc_names, loc_parent, load_sem.at[4]),
        pltpu.make_async_copy(lvl_names, lvl_parent, load_sem.at[5]),
    ]
    strip_loads = [
        pltpu.make_async_copy(
            lvl_inv.at[level], strips_s.at[:, inv_at(level)], strips_sem.at[inv_at(level)]
        )
        for level in range(LEVELS)
    ] + [
        pltpu.make_async_copy(
            lvl_low.at[level, :, 0 : kinds_at(level)],
            strips_s.at[:, low_at(level, 0) : low_at(level, 0) + kinds_at(level)],
            strips_sem.at[low_at(level, 0)],
        )
        for level in range(LEVELS - 1)
    ]
    for load in loads + strip_loads:
        load.start()

    barrier = pltpu.get_barrier_semaphore()

    def greet(device):
        pl.semaphore_signal(barrier, inc=1, device_id=device, device_id_type=MESH)

    others = [carrier[0] for carrier in carriers[1:]] + holders[1:] + [sibling, beside, up, far, down]
    others += [device for three in partners for device in three[1:]]
    for device in others:
        greet(device)

    @pl.when(jnp.logical_not(own))
    def _():
        greet(carriers[0][0])
        greet(holders[0])

    for load in loads[:2]:
        load.wait()
    for i in range(LOCALS):
        high, rest = split(inv_s[i])
        inv_high[i] = high
        inv_rest[i] = rest
        y_s[i] = product(rhs_s[i].T, high, rest, 1)
    pl.semaphore_wait(barrier, len(others) + jnp.where(own, 0, 2))

    def send(src, dst, send_sem, recv_sem, device):
        return pltpu.make_async_remote_copy(
            src_ref=src, dst_ref=dst, send_sem=send_sem, recv_sem=recv_sem,
            device_id=device, device_id_type=MESH,
        )

    def send_or_keep(copies):
        @pl.when(own)
        def _():
            for src, dst, send_sem, recv_sem, device in copies:
                pltpu.make_async_copy(src, dst, recv_sem).start()

        @pl.when(jnp.logical_not(own))
        def _():
            for copy in copies:
                send(*copy).start()

    def drain(ref, sem):
        pltpu.make_async_copy(ref, ref, sem).wait()

    strip = pl.ds(pl.multiple_of(STRIP * parity, STRIP), STRIP)
    first, second = slice(0, STRIP), slice(STRIP, 2 * STRIP)

    def along_x(index):
        copies = [
            (
                strips_s.at[slot, trio(index)], mats.at[trio(index), y, x_high, strip, :],
                strip_snd_sem, strip_sem.at[index], (2 * z + x_high, 4 * y + x_of(core, slot)),
            )
            for slot in slots
        ]
        send(*copies[1]).start()
        send_or_keep(copies[:1])

    def along_y(index):
        part = mats.at[trio(index), y, core]
        drain(part, strip_sem.at[index])
        for device in (up, down):
            send(part, part, ring_snd_sem, ring_sem.at[index], device).start()
        if index == 0:
            send(part, part, ring_snd_sem, far_sem.at[index], far).start()

    def to_far(index):
        drain(mats.at[trio(index), 0:2, core], ring_sem.at[index])
        for at_y, half_strip, device in ((y_down, first, up), (y_up, second, down)):
            part = mats.at[trio(index), at_y, core, half_strip, :]
            send(part, part, ring_snd_sem, far_sem.at[index], device).start()

    def to_sibling(index):
        if index == 0:
            drain(mats.at[trio(index), 0:2, core], ring_sem.at[index])
        drain(mats.at[trio(index), y_far, core], far_sem.at[index])
        part = mats.at[trio(index), :, core]
        send(part, part, pair_snd_sem, pair_sem.at[index], sibling).start()

    def take(index):
        drain(mats.at[trio(index), :, 1 - core], pair_sem.at[index])
        parts = {}
        for m in range(3 * index, 3 * index + 3):
            parts[BLOCKS[m]] = split(mats[m].reshape(UNKNOWNS, UNKNOWNS))
            if BLOCKS[m][0] == "inv":
                mat_high[m], mat_rest[m] = parts[BLOCKS[m]]
        for m in range(3 * index, 3 * index + 3):
            name, level = BLOCKS[m][:2]
            if name == "low":
                mat_high[m], mat_rest[m] = split(multiply(parts[BLOCKS[m]], parts["inv", level], 0))
            elif level + 1 == LEVELS:
                turned = split(mats[m].reshape(UNKNOWNS, UNKNOWNS).T)
                mat_high[m], mat_rest[m] = split(multiply(turned, parts[BLOCKS[m]], 0))

    def thin(vectors, m, dim):
        return thin_product(vectors, mat_high[m], mat_rest[m], dim)

    for load in strip_loads:
        load.wait()
    along_x(0)
    for load in loads[2:]:
        load.wait()
    pick = [
        [jnp.where(loc_parent[i] == slot, 1.0, 0.0).astype(f32) for slot in range(2)]
        for i in range(LOCALS)
    ]

    y_others = [(up, y_up), (far, y_far), (down, y_down)]

    def local_updates(kind):
        for i in range(LOCALS):
            high, rest = split(low_s[i, kind])
            low_high[i, kind] = high
            low_rest[i, kind] = rest
            update = product(y_s[i], high, rest, 1).reshape(4, 2, SHARE, UNKNOWNS)
            for slot in range(2):
                if i == 0:
                    snd[kind, slot] = pick[i][slot] * update
                else:
                    snd[kind, slot] += pick[i][slot] * update

    def x_first():
        copies = [
            (snd.at[0, slot, :, there_core], x_part.at[x], part_snd_sem.at[0], part_sem.at[0], device)
            for device, slot, there_core in x_carriers
        ]
        for copy in copies[1:]:
            send(*copy).start()
        send_or_keep(copies[:1])

    def x_then_y():
        drain(x_part, part_sem.at[0])
        x_sum[...] = (x_part[0] + x_part[1]) + (x_part[2] + x_part[3])
        for device, there_y in y_others:
            send(
                x_sum.at[there_y], x_last.at[y], last_snd_sem, last_sem, device
            ).start()

    def straight():
        copies = [
            (
                snd.at[1, slot, index_y, there_core], y_last.at[rows],
                part_snd_sem.at[1], part_sem.at[1], device,
            )
            for (device, _, slot), (index_y, there_core) in zip(carriers, carrier_shares)
        ]
        for copy in copies[1:]:
            send(*copy).start()
        send_or_keep(copies[:1])

    local_updates(0)
    x_first()
    along_y(0)
    along_x(1)
    along_x(2)
    local_updates(1)
    straight()
    row = lax.broadcasted_iota(jnp.int32, (OCTET, 128), 0)
    names = jnp.zeros((OCTET, 128), f32)
    for k in range(2):
        for level in range(LEVELS - 1):
            names = jnp.where(row == 4 * k + level, lvl_parent[k, level].astype(f32), names)
    names_snd[...] = names
    send(names_snd, names_rcv, names_snd_sem, names_sem, sibling).start()
    for k in range(2):
        strips = [
            lvl_rhs_s[pl.ds(2 * STRIP * level + k, STRIP, stride=2), :] for level in range(LEVELS)
        ]
        strips.append(jnp.zeros((HALF - LEVELS * STRIP, COLUMNS), f32))
        extra = jnp.concatenate(strips, axis=0).T.reshape(SHARES, 2, OCTET, 128)
        right = pltpu.roll(extra[:, 1].reshape(SHARES * OCTET, 128), 64, 1)
        ride_snd[k] = extra[:, 0] + right.reshape(SHARES, OCTET, 128)
    rides = [
        (ride_snd.at[slot, index], ride_rcv.at[rows], ride_snd_sem, ride_sem, device)
        for device, index, slot in carriers
    ]
    for ride in rides[1:]:
        send(*ride).start()
    send_or_keep(rides[:1])
    along_y(1)
    x_then_y()
    along_y(2)

    def prepare_local(i):
        inverse = (inv_high[i], inv_rest[i])
        y_s[i] = product(y_s[i], inv_high[i], inv_rest[i], 0)
        for kind in range(2):
            both = multiply((low_high[i, kind], low_rest[i, kind]), inverse, 0)
            high, rest = split(both.T if kind == 0 else both)
            low_high[i, kind] = high
            low_rest[i, kind] = rest

    to_sibling(0)
    drain(ride_rcv, ride_sem)
    parts = regroup(ride_rcv[...].reshape(2, 8, OCTET, 128))
    parts = [jnp.concatenate([part[0], part[1]], axis=1) for part in parts]
    rhs = [
        jnp.concatenate([parts[level], parts[LEVELS + level]], axis=0) for level in range(LEVELS)
    ]
    drain(names_rcv, names_sem)
    names = jnp.where(own, names_snd[...], names_rcv[...])
    parent = []
    for level in range(LEVELS - 1):
        name = jnp.where(place == 0, names[level : level + 1], names[4 + level : 5 + level])
        parent.append(jnp.broadcast_to(jnp.concatenate([name, name], axis=1), (SHARE, UNKNOWNS)))
    mine, places = place.astype(f32), [(1 - place).astype(f32), 2.0, 3.0]

    def chosen(name, at_place, value):
        return jnp.where(name == at_place, value, 0.0)

    def slot_at(index):
        return 0 if index == 0 else 1 + place

    def gathered(total, buffer, sem):
        drain(buffer, sem)
        for index in range(3):
            total = total + buffer[index]
        return total

    below = []
    take(0)
    to_far(1)
    drain(x_last.at[0:3], last_sem)
    above = x_sum[y]
    for _, there_y in y_others:
        above = above + x_last[there_y]
    for level in range(LEVELS):
        kinds = kinds_at(level)
        moved = rhs[level] - above
        if level + 1 < LEVELS:
            out = [thin(moved, low_at(level, kind), 1) for kind in range(kinds)]
            if level == 0:
                drain(y_last, part_sem.at[1])
                pending = y_last[0]
                for source in range(1, PEERS):
                    pending = pending + y_last[source]
            else:
                pending = gathered(own_pending, up_rcv.at[level - 1, 1], up_sem.at[level - 1, 1])
            out[0] = out[0] + pending
            for kind in range(kinds):
                for index in (1, 2, 0):
                    up_snd[level, kind, index] = chosen(parent[level], places[index], out[kind])
                    send(
                        up_snd.at[level, kind, index], up_rcv.at[level, kind, slot_at(index)],
                        up_snd_sem, up_sem.at[level, kind], partners[level][index],
                    ).start()
            own_pending = chosen(parent[level], mine, out[-1])
            if level == 0:
                to_sibling(1)
                to_far(2)
            below.append(thin(thin(moved, inv_at(level), 1), inv_at(level), 0))
            if level + 1 < TRIOS:
                take(level + 1)
            else:
                prepare_local(0)
            if level == 0:
                to_sibling(2)
            own_above = chosen(parent[level], mine, out[0])
            above = gathered(own_above, up_rcv.at[level, 0], up_sem.at[level, 0])

    def send_down(level, kind, value):
        down_snd[level, kind] = value
        for index in (1, 2, 0):
            send(
                down_snd.at[level, kind], down_rcv.at[level, kind, slot_at(index)],
                down_snd_sem, down_sem.at[level, kind], partners[level][index],
            ).start()

    def pooled(level, kind, value):
        total = chosen(parent[level], mine, value)
        drain(down_rcv.at[level, kind], down_sem.at[level, kind])
        for index in range(3):
            total = total + chosen(parent[level], places[index], down_rcv[level, kind, index])
        return total

    def spread(step, landing, value):
        own_snd[step] = value.reshape(2, OCTET, UNKNOWNS)
        ring_rcv[step, y] = value[0:OCTET]
        for device, _ in y_others:
            send(
                own_snd.at[step, 0], ring_rcv.at[step, y],
                early_snd_sem.at[step], early_sem.at[step, 0], device,
            ).start()
        copies = [
            (
                own_snd.at[step, 1], landing.at[place, y, core, 1],
                early_snd_sem.at[step], early_sem.at[step, 1], device,
            )
            for device in x_holders
        ]
        for copy in copies[1:]:
            send(*copy).start()
        send_or_keep(copies[:1])

    def spread_on(step, landing):
        drain(ring_rcv.at[step, 0:3], early_sem.at[step, 0])
        copies = [
            (
                ring_rcv.at[step], landing.at[place, :, core, 0],
                late_snd_sem.at[step, 0], late_sem.at[step, 0], device,
            )
            for device in x_holders
        ]
        for copy in copies[1:]:
            send(*copy).start()
        send_or_keep(copies[:1])
        part = landing.at[:, y, :, 1]
        drain(part, early_sem.at[step, 1])
        for device, _ in y_others:
            send(part, part, late_snd_sem.at[step, 1], late_sem.at[step, 1], device).start()

    def spread_end(step, landing):
        drain(landing.at[:, :, :, 0], late_sem.at[step, 0])
        drain(landing.at[:, 0:3, :, 1], late_sem.at[step, 1])

    def whole(landing):
        return landing[...].reshape(2, COLUMNS, UNKNOWNS)

    current, current_parent = thin(moved, inv_at(LEVELS - 1), 0), None
    results = [None] * LEVELS
    results[LEVELS - 1] = current
    for level in range(LEVELS - 2, -1, -1):
        send_down(level, 0, current)
        if level == 0:
            spread(0, next_rcv, current)
            spread_on(0, next_rcv)
        else:
            prepare_local(LEVELS - 1 - level)
        left = below[level]
        if kinds_at(level) == 2:
            left = left - thin(pooled(level, 1, current_parent), low_at(level, 1), 0)
        current_parent = pooled(level, 0, current)
        if level > 0:
            send_down(level - 1, 1, current_parent)
        current = left - thin(current_parent, low_at(level, 0), 0)
        results[level] = current
    spread(1, x_rcv, current)

    spread_end(0, next_rcv)
    send(next_rcv, beside_rcv, beside_snd_sem, beside_sem, sibling).start()
    halves = []
    for octet in (slice(0, OCTET), slice(OCTET, SHARE)):
        for part in results[1:] + results[3:]:
            halves.append(jnp.stack([part[octet, 0:HALF], part[octet, HALF:]], axis=0))
    tiles = regroup(jnp.stack(halves, axis=1))
    for m in range(8):
        for h in range(2):
            sol_snd[8 * h + m] = tiles[m][h]
    spread_on(1, x_rcv)
    copies = [
        (sol_snd.at[device[1]], sol_rcv.at[place, share], sol_snd_sem, sol_sem, device)
        for device in holders
    ]
    for copy in copies[1:]:
        send(*copy).start()
    send_or_keep(copies[:1])
    drain(beside_rcv, beside_sem)
    own_next, beside_next = whole(next_rcv), whole(beside_rcv)
    for i in range(LOCALS):
        grand = None
        for at_place in range(4):
            weight = sum(
                pick[i][k] * jnp.where(lvl_parent[k, 0] == at_place, 1.0, 0.0).astype(f32)
                for k in range(2)
            )
            if at_place < 2:
                term = weight * own_next[at_place]
            else:
                term = weight * beside_next[at_place - 2]
            grand = term if grand is None else grand + term
        loc_out[i] = (y_s[i] - product(grand, low_high[i, 1], low_rest[i, 1], 0)).T
    drain(x_part.at[0:3], part_snd_sem.at[0])
    drain(y_last.at[1:], part_snd_sem.at[1])
    drain(x_last.at[0:3], last_snd_sem)
    drain(ride_rcv.at[1:], ride_snd_sem)
    drain(names_snd, names_snd_sem)
    for step in range(2):
        for _ in range(2):
            drain(ring_rcv.at[step, 0:3], early_snd_sem.at[step])
        for _ in range(3):
            drain(ring_rcv.at[step], late_snd_sem.at[step, 0])
        drain(x_rcv.at[:, 0:3, :, 1], late_snd_sem.at[step, 1])
    drain(sol_snd.at[1:], sol_snd_sem)
    drain(strips_s.at[0], strip_snd_sem)
    drain(mats.at[:, 0:3, 0], ring_snd_sem)
    drain(mats.at[:, :, 0], pair_snd_sem)
    drain(beside_rcv, beside_snd_sem)
    for level in range(LEVELS - 1):
        for kind in range(kinds_at(level)):
            drain(up_rcv.at[level, kind], up_snd_sem)
            drain(down_rcv.at[level, kind], down_snd_sem)

    @pl.when(jnp.logical_not(own))
    def _():
        drain(x_part.at[0], part_snd_sem.at[0])
        drain(y_last.at[0], part_snd_sem.at[1])
        drain(ride_rcv.at[0], ride_snd_sem)
        for step in range(2):
            drain(ring_rcv.at[step, 0], early_snd_sem.at[step])
            drain(ring_rcv.at[step], late_snd_sem.at[step, 0])
        drain(sol_snd.at[0], sol_snd_sem)
        drain(strips_s.at[0], strip_snd_sem)

    spread_end(1, x_rcv)
    x_all = whole(x_rcv)
    for i in range(LOCALS):
        above_x = pick[i][0] * x_all[0] + pick[i][1] * x_all[1]
        loc_out[i] -= multiply((low_high[i, 0], low_rest[i, 0]), split(above_x), 1)
    here = pl.ds(pl.multiple_of(STRIP * rows, STRIP), STRIP)
    for k in range(2):
        turned_s[k] = x_all[k].T
        sol_out[pl.ds(k, STRIP, stride=2), :] = turned_s[k, here, :]
    drain(sol_rcv, sol_sem)
    for k in range(2):
        packed = sol_rcv[k].reshape(SHARES * OCTET, 128)
        right = pltpu.roll(packed, 64, 1).reshape(SHARES, OCTET, 128)
        both = jnp.stack([sol_rcv[k], right], axis=1).reshape(COLUMNS, 128)
        strips = both.T
        for level in range(1, LEVELS):
            to = pl.ds(2 * STRIP * level + k, STRIP, stride=2)
            sol_out[to, :] = strips[STRIP * (level - 1) : STRIP * level]


def on_device(loc_rhs, loc_inv, loc_low, loc_parent, lvl_rhs, lvl_inv, lvl_low, lvl_parent):
    vmem = pl.BlockSpec(memory_space=pltpu.VMEM)
    far = pl.BlockSpec(memory_space=pltpu.HBM)
    dma = pltpu.SemaphoreType.DMA
    square = (UNKNOWNS, UNKNOWNS)
    loc_sol, sol = pl.pallas_call(
        kernel,
        out_shape=(
            jax.ShapeDtypeStruct((LOCALS, UNKNOWNS, COLUMNS), f32),
            jax.ShapeDtypeStruct((COLUMNS, 128), f32),
        ),
        in_specs=[far] * 8,
        out_specs=(vmem, vmem),
        scratch_shapes=[
            pltpu.SMEM((LOCALS,), jnp.int32),
            pltpu.SMEM((2, LEVELS - 1), jnp.int32),
            pltpu.VMEM((LOCALS, UNKNOWNS, COLUMNS), f32),
            pltpu.VMEM((LOCALS,) + square, f32),
            pltpu.VMEM((LOCALS, 2) + square, f32),
            pltpu.VMEM((LEVELS * STRIP * 2, COLUMNS), f32),
            pltpu.VMEM((LOCALS,) + square, bf16),
            pltpu.VMEM((LOCALS,) + square, bf16),
            pltpu.VMEM((LOCALS, 2) + square, bf16),
            pltpu.VMEM((LOCALS, 2) + square, bf16),
            pltpu.VMEM((LOCALS, COLUMNS, UNKNOWNS), f32),
            pltpu.VMEM((2, len(BLOCKS), STRIP, UNKNOWNS), f32),
            pltpu.VMEM((2, 2, 4, 2, SHARE, UNKNOWNS), f32),
            pltpu.VMEM((4, 4, SHARE, UNKNOWNS), f32),
            pltpu.VMEM((4, SHARE, UNKNOWNS), f32),
            pltpu.VMEM((4, SHARE, UNKNOWNS), f32),
            pltpu.VMEM((PEERS, SHARE, UNKNOWNS), f32),
            pltpu.VMEM((2, SHARES, OCTET, 128), f32),
            pltpu.VMEM((PEERS, OCTET, 128), f32),
            pltpu.VMEM((OCTET, 128), f32),
            pltpu.VMEM((OCTET, 128), f32),
            pltpu.VMEM((len(BLOCKS), 4, 2, 2 * STRIP, UNKNOWNS), f32),
            pltpu.VMEM((len(BLOCKS),) + square, bf16),
            pltpu.VMEM((len(BLOCKS),) + square, bf16),
            pltpu.VMEM((LEVELS - 1, 2, 3, SHARE, UNKNOWNS), f32),
            pltpu.VMEM((LEVELS - 1, 2, 3, SHARE, UNKNOWNS), f32),
            pltpu.VMEM((LEVELS - 1, 2, SHARE, UNKNOWNS), f32),
            pltpu.VMEM((LEVELS - 1, 2, 3, SHARE, UNKNOWNS), f32),
            pltpu.VMEM((2, 2, OCTET, UNKNOWNS), f32),
            pltpu.VMEM((2, 4, OCTET, UNKNOWNS), f32),
            pltpu.VMEM((2, 4, 2, 2, OCTET, UNKNOWNS), f32),
            pltpu.VMEM((2, 4, 2, 2, OCTET, UNKNOWNS), f32),
            pltpu.VMEM((2, 4, 2, 2, OCTET, UNKNOWNS), f32),
            pltpu.VMEM((PEERS, OCTET, 128), f32),
            pltpu.VMEM((2, SHARES, OCTET, 128), f32),
            pltpu.VMEM((2, UNKNOWNS, COLUMNS), f32),
            dma((6,)),
            dma((len(BLOCKS),)),
            dma((2,)),
            dma((2,)),
            dma,
            dma,
            dma,
            dma,
            dma,
            dma,
            dma,
            dma((TRIOS,)),
            dma,
            dma((TRIOS,)),
            dma((TRIOS,)),
            dma,
            dma((TRIOS,)),
            dma,
            dma((LEVELS - 1, 2)),
            dma,
            dma((LEVELS - 1, 2)),
            dma((2,)),
            dma((2, 2)),
            dma((2, 2)),
            dma((2, 2)),
            dma,
            dma,
            dma,
            dma,
        ],
        compiler_params=pltpu.CompilerParams(
            collective_id=0, has_side_effects=True, vmem_limit_bytes=40 * 1024 * 1024
        ),
    )(
        *(
            pltpu.with_memory_space_constraint(operand, pltpu.HBM)
            for operand in (
                loc_parent.reshape(LOCALS),
                loc_rhs.reshape(LOCALS, UNKNOWNS, COLUMNS),
                loc_inv.reshape((LOCALS,) + square),
                loc_low.reshape((LOCALS, 2) + square),
                lvl_rhs.reshape(LEVELS * STRIP * 2, COLUMNS),
                lvl_inv.reshape(LEVELS, 2, STRIP, UNKNOWNS),
                lvl_low.reshape(LEVELS - 1, 2, 2, STRIP, UNKNOWNS),
                lvl_parent.reshape(LEVELS - 1, 2).T,
            )
        )
    )
    return loc_sol[None, None], sol.reshape(1, LEVELS, STRIP, 2, COLUMNS)


def solution(mesh):
    in_specs = (
        P("leaf", "rows", None, None, None),
        P("leaf", "rows", None, None, None),
        P("leaf", "rows", None, None, None, None),
        P("leaf", "rows", None),
        P("leaf", None, "rows", None, None),
        P("leaf", None, None, "rows", None),
        P("leaf", None, None, None, "rows", None),
        P("leaf", None, None),
    )
    out_specs = (P("leaf", "rows", None, None, None), P("leaf", None, "rows", None, None))
    return jax.shard_map(
        on_device, mesh=mesh, in_specs=in_specs, out_specs=out_specs, check_vma=False
    )
```

```python
import functools

import jax
import jax.numpy as jnp
from jax import lax
from jax.experimental import pallas as pl
from jax.experimental.pallas import tpu as pltpu
from jax.sharding import PartitionSpec as P

MESH = pl.DeviceIdType.MESH
f32 = jnp.float32
bf16 = jnp.bfloat16

UNKNOWNS = 256
COLUMNS = 128
STRIP = 16
SHARE = 16
SHARES = 8
PEERS = 16
LOCALS = 3
LEVELS = 4
HALF = UNKNOWNS // 2
OCTET = 8
BLOCKS = (("inv", 0), ("low", 0, 0), ("low", 0, 1), ("inv", 1), ("low", 1, 0), ("low", 1, 1), ("inv", 2), ("low", 2, 0), ("inv", 3))
TRIOS = 3


def split(value):
    high = value.astype(bf16)
    return high, (value - high.astype(f32)).astype(bf16)


def dot(left, right, dim):
    return lax.dot_general(
        left, right, (((1,), (dim,)), ((), ())), preferred_element_type=f32
    )


def multiply(left, right, dim):
    return dot(left[0], right[0], dim) + dot(left[1], right[0], dim) + dot(left[0], right[1], dim)


def product(vectors, mat_high, mat_low, dim):
    return multiply(split(vectors), (mat_high, mat_low), dim)


def thin_product(vectors, mat_high, mat_low, dim):
    high = vectors.astype(bf16).astype(f32)
    both = jnp.concatenate([high, vectors - high], axis=0).astype(bf16)
    total = dot(both, mat_high, dim) + dot(both, mat_low, dim)
    return total[:SHARE] + total[SHARE:]


def regroup(tiles):
    group = lax.div(lax.broadcasted_iota(jnp.int32, (2, OCTET, 128), 2), STRIP)
    flat = tiles.reshape(PEERS * OCTET, 128)
    turned = [flat.reshape(2, 8, OCTET, 128)]
    for turn in range(1, 8):
        turned.append(pltpu.roll(flat, STRIP * turn, 1).reshape(2, 8, OCTET, 128))
    results = []
    for g in range(8):
        total = turned[-g % 8][:, 0]
        for m in range(1, 8):
            total = jnp.where(group == m, turned[(m - g) % 8][:, m], total)
        results.append(total)
    return results


def kinds_at(level):
    return 2 if level + 2 < LEVELS else 1


def inv_at(level):
    return BLOCKS.index(("inv", level))


def low_at(level, kind):
    return BLOCKS.index(("low", level, kind))


def trio(index):
    return slice(3 * index, 3 * index + 3)


def kernel(
    loc_names, loc_rhs, loc_inv, loc_low, lvl_rhs, lvl_inv, lvl_low, lvl_names,
    loc_out, sol_out,
    loc_parent, lvl_parent, rhs_s, inv_s, low_s, lvl_rhs_s, inv_high, inv_rest, low_high, low_rest, y_s, solved_s, sums_s,
    strips_s, snd, x_part, x_sum, x_last, y_last, ride_snd, ride_rcv, names_snd, names_rcv,
    mats, mat_high, mat_rest, turned_high, turned_rest, up_snd, up_rcv, down_snd, down_rcv,
    own_snd, ring_rcv, x_rcv, next_rcv, beside_rcv, sol_snd, sol_rcv, turned_s,
    load_sem, strips_sem, part_snd_sem, part_sem, last_snd_sem, last_sem,
    ride_snd_sem, ride_sem, names_snd_sem, names_sem, strip_snd_sem, strip_sem, ring_snd_sem, ring_sem, far_sem,
    pair_snd_sem, pair_sem, up_snd_sem, up_sem, down_snd_sem, down_sem, early_snd_sem, early_sem, late_snd_sem, late_sem,
    sol_snd_sem, sol_sem, beside_snd_sem, beside_sem,
):
    leaf = lax.axis_index("leaf")
    rows = lax.axis_index("rows")
    z, core = lax.div(leaf, 2), lax.rem(leaf, 2)
    y, x = lax.div(rows, 4), lax.rem(rows, 4)
    x_high, parity = lax.div(x, 2), lax.rem(x, 2)
    carried = 2 * z + x_high
    place = jnp.where(x_high == 0, parity, 1 - parity)
    share = 2 * y + core
    own = x_high == core

    def x_of(odd, slot):
        return 2 * odd + jnp.where(odd == 0, slot, 1 - slot)

    def around(value):
        return [value] + [jnp.where(value + n >= 4, value + n - 4, value + n) for n in range(1, 4)]

    slots, cores = [place, 1 - place], [core, 1 - core]
    ys, xs = around(y), around(x)
    carriers = [
        ((2 * z + there_core, 4 * there_y + x_of(core, slot)), 2 * there_y + there_core, slot)
        for there_y in ys
        for slot in slots
        for there_core in cores
    ]
    carrier_shares = [(there_y, there_core) for there_y in ys for _ in slots for there_core in cores]
    holders = [(carried, 4 * there_y + there_x) for there_y in ys for there_x in xs]
    x_carriers = [
        ((2 * z + there_core, 4 * y + x_of(core, slot)), slot, there_core)
        for slot in slots
        for there_core in cores
    ]
    x_holders = [(carried, 4 * y + there_x) for there_x in xs]
    sibling = (2 * z + 1 - core, rows)
    z_half = lax.rem(lax.div(z, 2), 2)
    beside = (leaf, rows + 1 - 2 * parity)
    partners = [[beside] + [(leaf, 4 * y + x_of(1 - x_high, slot)) for slot in range(2)]]
    for there_z in (z + 1 - 2 * lax.rem(z, 2), z + 2 - 4 * z_half):
        partners.append(
            [beside] + [(2 * there_z + core, 4 * y + x_of(x_high, slot)) for slot in range(2)]
        )
    y_up, y_far, y_down = ys[1], ys[2], ys[3]
    up, far, down = [(leaf, 4 * there_y + x) for there_y in (y_up, y_far, y_down)]

    loads = [
        pltpu.make_async_copy(loc_rhs, rhs_s, load_sem.at[0]),
        pltpu.make_async_copy(loc_inv, inv_s, load_sem.at[1]),
        pltpu.make_async_copy(loc_low, low_s, load_sem.at[2]),
        pltpu.make_async_copy(lvl_rhs, lvl_rhs_s, load_sem.at[3]),
        pltpu.make_async_copy(loc_names, loc_parent, load_sem.at[4]),
        pltpu.make_async_copy(lvl_names, lvl_parent, load_sem.at[5]),
    ]
    strip_loads = [
        pltpu.make_async_copy(
            lvl_inv.at[level], strips_s.at[:, inv_at(level)], strips_sem.at[inv_at(level)]
        )
        for level in range(LEVELS)
    ] + [
        pltpu.make_async_copy(
            lvl_low.at[level, :, 0 : kinds_at(level)],
            strips_s.at[:, low_at(level, 0) : low_at(level, 0) + kinds_at(level)],
            strips_sem.at[low_at(level, 0)],
        )
        for level in range(LEVELS - 1)
    ]
    for load in loads + strip_loads:
        load.start()

    barrier = pltpu.get_barrier_semaphore()

    def greet(device):
        pl.semaphore_signal(barrier, inc=1, device_id=device, device_id_type=MESH)

    others = [carrier[0] for carrier in carriers[1:]] + holders[1:] + [sibling, beside, up, far, down]
    others += [device for three in partners for device in three[1:]]
    for device in others:
        greet(device)

    @pl.when(jnp.logical_not(own))
    def _():
        greet(carriers[0][0])
        greet(holders[0])

    for load in loads[:2]:
        load.wait()
    for i in range(LOCALS):
        high, rest = split(inv_s[i])
        inv_high[i] = high
        inv_rest[i] = rest
        solved_s[i] = multiply((high, rest), split(rhs_s[i]), 0)
    pl.semaphore_wait(barrier, len(others) + jnp.where(own, 0, 2))

    def send(src, dst, send_sem, recv_sem, device):
        return pltpu.make_async_remote_copy(
            src_ref=src, dst_ref=dst, send_sem=send_sem, recv_sem=recv_sem,
            device_id=device, device_id_type=MESH,
        )

    def send_or_keep(copies):
        @pl.when(own)
        def _():
            for src, dst, send_sem, recv_sem, device in copies:
                pltpu.make_async_copy(src, dst, recv_sem).start()

        @pl.when(jnp.logical_not(own))
        def _():
            for copy in copies:
                send(*copy).start()

    def drain(ref, sem):
        pltpu.make_async_copy(ref, ref, sem).wait()

    strip = pl.ds(pl.multiple_of(STRIP * parity, STRIP), STRIP)
    first, second = slice(0, STRIP), slice(STRIP, 2 * STRIP)

    def along_x(index):
        copies = [
            (
                strips_s.at[slot, trio(index)], mats.at[trio(index), y, x_high, strip, :],
                strip_snd_sem, strip_sem.at[index], (2 * z + x_high, 4 * y + x_of(core, slot)),
            )
            for slot in slots
        ]
        send(*copies[1]).start()
        send_or_keep(copies[:1])

    def along_y(index):
        part = mats.at[trio(index), y, core]
        drain(part, strip_sem.at[index])
        for device in (up, down):
            send(part, part, ring_snd_sem, ring_sem.at[index], device).start()
        if index == 0:
            send(part, part, ring_snd_sem, far_sem.at[index], far).start()

    def to_far(index):
        drain(mats.at[trio(index), 0:2, core], ring_sem.at[index])
        for at_y, half_strip, device in ((y_down, first, up), (y_up, second, down)):
            part = mats.at[trio(index), at_y, core, half_strip, :]
            send(part, part, ring_snd_sem, far_sem.at[index], device).start()

    def to_sibling(index):
        if index == 0:
            drain(mats.at[trio(index), 0:2, core], ring_sem.at[index])
        drain(mats.at[trio(index), y_far, core], far_sem.at[index])
        part = mats.at[trio(index), :, core]
        send(part, part, pair_snd_sem, pair_sem.at[index], sibling).start()

    def take(index):
        drain(mats.at[trio(index), :, 1 - core], pair_sem.at[index])
        parts = {}
        for m in range(3 * index, 3 * index + 3):
            parts[BLOCKS[m]] = split(mats[m].reshape(UNKNOWNS, UNKNOWNS))
            if BLOCKS[m][0] == "inv":
                mat_high[m], mat_rest[m] = parts[BLOCKS[m]]
        for m in range(3 * index, 3 * index + 3):
            name, level = BLOCKS[m][:2]
            if name == "low":
                both = multiply(parts[BLOCKS[m]], parts["inv", level], 0)
                mat_high[m], mat_rest[m] = split(both)
                if index > 0:
                    turned_high[m], turned_rest[m] = split(both.T)
            elif level + 1 == LEVELS:
                turned = split(mats[m].reshape(UNKNOWNS, UNKNOWNS).T)
                mat_high[m], mat_rest[m] = split(multiply(turned, parts[BLOCKS[m]], 0))

    def thin_up(vectors, m):
        if m < 3:
            return thin(vectors, m, 1)
        return thin_product(vectors, turned_high[m], turned_rest[m], 0)

    def thin(vectors, m, dim):
        return thin_product(vectors, mat_high[m], mat_rest[m], dim)

    for load in strip_loads:
        load.wait()
    along_x(0)
    for load in loads[2:]:
        load.wait()
    pick = [
        [jnp.where(loc_parent[i] == slot, 1.0, 0.0).astype(f32) for slot in range(2)]
        for i in range(LOCALS)
    ]

    y_others = [(up, y_up), (far, y_far), (down, y_down)]

    def local_updates(kind):
        for i in range(LOCALS):
            high, rest = split(low_s[i, kind])
            low_high[i, kind] = high
            low_rest[i, kind] = rest
            update = multiply((high, rest), split(solved_s[i]), 0)
            for slot in range(2):
                if i == 0:
                    sums_s[slot] = pick[i][slot] * update
                else:
                    sums_s[slot] += pick[i][slot] * update
        for slot in range(2):
            snd[kind, slot] = sums_s[slot].T.reshape(4, 2, SHARE, UNKNOWNS)

    def x_first():
        copies = [
            (snd.at[0, slot, :, there_core], x_part.at[x], part_snd_sem.at[0], part_sem.at[0], device)
            for device, slot, there_core in x_carriers
        ]
        for copy in copies[1:]:
            send(*copy).start()
        send_or_keep(copies[:1])

    def x_then_y():
        drain(x_part, part_sem.at[0])
        x_sum[...] = (x_part[0] + x_part[1]) + (x_part[2] + x_part[3])
        for device, there_y in y_others:
            send(
                x_sum.at[there_y], x_last.at[y], last_snd_sem, last_sem, device
            ).start()

    def straight():
        copies = [
            (
                snd.at[1, slot, index_y, there_core], y_last.at[rows],
                part_snd_sem.at[1], part_sem.at[1], device,
            )
            for (device, _, slot), (index_y, there_core) in zip(carriers, carrier_shares)
        ]
        for copy in copies[1:]:
            send(*copy).start()
        send_or_keep(copies[:1])

    local_updates(0)
    x_first()
    along_y(0)
    along_x(1)
    along_x(2)
    local_updates(1)
    straight()
    row = lax.broadcasted_iota(jnp.int32, (OCTET, 128), 0)
    names = jnp.zeros((OCTET, 128), f32)
    for k in range(2):
        for level in range(LEVELS - 1):
            names = jnp.where(row == 4 * k + level, lvl_parent[k, level].astype(f32), names)
    names_snd[...] = names
    send(names_snd, names_rcv, names_snd_sem, names_sem, sibling).start()
    for k in range(2):
        strips = [
            lvl_rhs_s[pl.ds(2 * STRIP * level + k, STRIP, stride=2), :] for level in range(LEVELS)
        ]
        strips.append(jnp.zeros((HALF - LEVELS * STRIP, COLUMNS), f32))
        extra = jnp.concatenate(strips, axis=0).T.reshape(SHARES, 2, OCTET, 128)
        right = pltpu.roll(extra[:, 1].reshape(SHARES * OCTET, 128), 64, 1)
        ride_snd[k] = extra[:, 0] + right.reshape(SHARES, OCTET, 128)
    rides = [
        (ride_snd.at[slot, index], ride_rcv.at[rows], ride_snd_sem, ride_sem, device)
        for device, index, slot in carriers
    ]
    for ride in rides[1:]:
        send(*ride).start()
    send_or_keep(rides[:1])
    along_y(1)
    x_then_y()
    along_y(2)

    def prepare_local(i):
        inverse = (inv_high[i], inv_rest[i])
        y_s[i] = product(solved_s[i].T, inv_high[i], inv_rest[i], 0)
        for kind in range(2):
            both = multiply((low_high[i, kind], low_rest[i, kind]), inverse, 0)
            high, rest = split(both.T if kind == 0 else both)
            low_high[i, kind] = high
            low_rest[i, kind] = rest

    to_sibling(0)
    drain(ride_rcv, ride_sem)
    parts = regroup(ride_rcv[...].reshape(2, 8, OCTET, 128))
    parts = [jnp.concatenate([part[0], part[1]], axis=1) for part in parts]
    rhs = [
        jnp.concatenate([parts[level], parts[LEVELS + level]], axis=0) for level in range(LEVELS)
    ]
    drain(names_rcv, names_sem)
    names = jnp.where(own, names_snd[...], names_rcv[...])
    parent = []
    for level in range(LEVELS - 1):
        name = jnp.where(place == 0, names[level : level + 1], names[4 + level : 5 + level])
        parent.append(jnp.broadcast_to(jnp.concatenate([name, name], axis=1), (SHARE, UNKNOWNS)))
    mine, places = place.astype(f32), [(1 - place).astype(f32), 2.0, 3.0]

    def chosen(name, at_place, value):
        return jnp.where(name == at_place, value, 0.0)

    def slot_at(index):
        return 0 if index == 0 else 1 + place

    def gathered(total, buffer, sem):
        drain(buffer, sem)
        for index in range(3):
            total = total + buffer[index]
        return total

    below = []
    take(0)
    to_far(1)
    drain(x_last.at[0:3], last_sem)
    above = x_sum[y]
    for _, there_y in y_others:
        above = above + x_last[there_y]
    for level in range(LEVELS):
        kinds = kinds_at(level)
        moved = rhs[level] - above
        if level + 1 < LEVELS:
            out = [thin_up(moved, low_at(level, kind)) for kind in range(kinds)]
            if level == 0:
                drain(y_last, part_sem.at[1])
                pending = y_last[0]
                for source in range(1, PEERS):
                    pending = pending + y_last[source]
            else:
                pending = gathered(own_pending, up_rcv.at[level - 1, 1], up_sem.at[level - 1, 1])
            out[0] = out[0] + pending
            for kind in range(kinds):
                for index in (1, 2, 0):
                    up_snd[level, kind, index] = chosen(parent[level], places[index], out[kind])
                    send(
                        up_snd.at[level, kind, index], up_rcv.at[level, kind, slot_at(index)],
                        up_snd_sem, up_sem.at[level, kind], partners[level][index],
                    ).start()
            own_pending = chosen(parent[level], mine, out[-1])
            if level == 0:
                to_sibling(1)
                to_far(2)
            below.append(thin(thin(moved, inv_at(level), 1), inv_at(level), 0))
            if level + 1 < TRIOS:
                take(level + 1)
            else:
                prepare_local(0)
            if level == 0:
                to_sibling(2)
            own_above = chosen(parent[level], mine, out[0])
            above = gathered(own_above, up_rcv.at[level, 0], up_sem.at[level, 0])

    def send_down(level, kind, value):
        down_snd[level, kind] = value
        for index in (1, 2, 0):
            send(
                down_snd.at[level, kind], down_rcv.at[level, kind, slot_at(index)],
                down_snd_sem, down_sem.at[level, kind], partners[level][index],
            ).start()

    def pooled(level, kind, value):
        total = chosen(parent[level], mine, value)
        drain(down_rcv.at[level, kind], down_sem.at[level, kind])
        for index in range(3):
            total = total + chosen(parent[level], places[index], down_rcv[level, kind, index])
        return total

    def spread(step, landing, value):
        own_snd[step] = value.reshape(2, OCTET, UNKNOWNS)
        ring_rcv[step, y] = value[0:OCTET]
        for device, _ in y_others:
            send(
                own_snd.at[step, 0], ring_rcv.at[step, y],
                early_snd_sem.at[step], early_sem.at[step, 0], device,
            ).start()
        copies = [
            (
                own_snd.at[step, 1], landing.at[place, y, core, 1],
                early_snd_sem.at[step], early_sem.at[step, 1], device,
            )
            for device in x_holders
        ]
        for copy in copies[1:]:
            send(*copy).start()
        send_or_keep(copies[:1])

    def spread_on(step, landing):
        drain(ring_rcv.at[step, 0:3], early_sem.at[step, 0])
        copies = [
            (
                ring_rcv.at[step], landing.at[place, :, core, 0],
                late_snd_sem.at[step, 0], late_sem.at[step, 0], device,
            )
            for device in x_holders
        ]
        for copy in copies[1:]:
            send(*copy).start()
        send_or_keep(copies[:1])
        part = landing.at[:, y, :, 1]
        drain(part, early_sem.at[step, 1])
        for device, _ in y_others:
            send(part, part, late_snd_sem.at[step, 1], late_sem.at[step, 1], device).start()

    def spread_end(step, landing):
        drain(landing.at[:, :, :, 0], late_sem.at[step, 0])
        drain(landing.at[:, 0:3, :, 1], late_sem.at[step, 1])

    def whole(landing):
        return landing[...].reshape(2, COLUMNS, UNKNOWNS)

    current, current_parent = thin(moved, inv_at(LEVELS - 1), 0), None
    results = [None] * LEVELS
    results[LEVELS - 1] = current
    for level in range(LEVELS - 2, -1, -1):
        send_down(level, 0, current)
        if level == 0:
            spread(0, next_rcv, current)
            spread_on(0, next_rcv)
        else:
            prepare_local(LEVELS - 1 - level)
        left = below[level]
        if kinds_at(level) == 2:
            left = left - thin(pooled(level, 1, current_parent), low_at(level, 1), 0)
        current_parent = pooled(level, 0, current)
        if level > 0:
            send_down(level - 1, 1, current_parent)
        current = left - thin(current_parent, low_at(level, 0), 0)
        results[level] = current
    spread(1, x_rcv, current)

    spread_end(0, next_rcv)
    send(next_rcv, beside_rcv, beside_snd_sem, beside_sem, sibling).start()
    halves = []
    for octet in (slice(0, OCTET), slice(OCTET, SHARE)):
        for part in results[1:] + results[3:]:
            halves.append(jnp.stack([part[octet, 0:HALF], part[octet, HALF:]], axis=0))
    tiles = regroup(jnp.stack(halves, axis=1))
    for m in range(8):
        for h in range(2):
            sol_snd[8 * h + m] = tiles[m][h]
    spread_on(1, x_rcv)
    copies = [
        (sol_snd.at[device[1]], sol_rcv.at[place, share], sol_snd_sem, sol_sem, device)
        for device in holders
    ]
    for copy in copies[1:]:
        send(*copy).start()
    send_or_keep(copies[:1])
    drain(beside_rcv, beside_sem)
    own_next, beside_next = whole(next_rcv), whole(beside_rcv)
    for i in range(LOCALS):
        grand = None
        for at_place in range(4):
            weight = sum(
                pick[i][k] * jnp.where(lvl_parent[k, 0] == at_place, 1.0, 0.0).astype(f32)
                for k in range(2)
            )
            if at_place < 2:
                term = weight * own_next[at_place]
            else:
                term = weight * beside_next[at_place - 2]
            grand = term if grand is None else grand + term
        loc_out[i] = (y_s[i] - product(grand, low_high[i, 1], low_rest[i, 1], 0)).T
    drain(x_part.at[0:3], part_snd_sem.at[0])
    drain(y_last.at[1:], part_snd_sem.at[1])
    drain(x_last.at[0:3], last_snd_sem)
    drain(ride_rcv.at[1:], ride_snd_sem)
    drain(names_snd, names_snd_sem)
    for step in range(2):
        for _ in range(2):
            drain(ring_rcv.at[step, 0:3], early_snd_sem.at[step])
        for _ in range(3):
            drain(ring_rcv.at[step], late_snd_sem.at[step, 0])
        drain(x_rcv.at[:, 0:3, :, 1], late_snd_sem.at[step, 1])
    drain(sol_snd.at[1:], sol_snd_sem)
    drain(strips_s.at[0], strip_snd_sem)
    drain(mats.at[:, 0:3, 0], ring_snd_sem)
    drain(mats.at[:, :, 0], pair_snd_sem)
    drain(beside_rcv, beside_snd_sem)
    for level in range(LEVELS - 1):
        for kind in range(kinds_at(level)):
            drain(up_rcv.at[level, kind], up_snd_sem)
            drain(down_rcv.at[level, kind], down_snd_sem)

    @pl.when(jnp.logical_not(own))
    def _():
        drain(x_part.at[0], part_snd_sem.at[0])
        drain(y_last.at[0], part_snd_sem.at[1])
        drain(ride_rcv.at[0], ride_snd_sem)
        for step in range(2):
            drain(ring_rcv.at[step, 0], early_snd_sem.at[step])
            drain(ring_rcv.at[step], late_snd_sem.at[step, 0])
        drain(sol_snd.at[0], sol_snd_sem)
        drain(strips_s.at[0], strip_snd_sem)

    spread_end(1, x_rcv)
    x_all = whole(x_rcv)
    for i in range(LOCALS):
        above_x = pick[i][0] * x_all[0] + pick[i][1] * x_all[1]
        loc_out[i] -= multiply((low_high[i, 0], low_rest[i, 0]), split(above_x), 1)
    here = pl.ds(pl.multiple_of(STRIP * rows, STRIP), STRIP)
    for k in range(2):
        turned_s[k] = x_all[k].T
        sol_out[pl.ds(k, STRIP, stride=2), :] = turned_s[k, here, :]
    drain(sol_rcv, sol_sem)
    for k in range(2):
        packed = sol_rcv[k].reshape(SHARES * OCTET, 128)
        right = pltpu.roll(packed, 64, 1).reshape(SHARES, OCTET, 128)
        both = jnp.stack([sol_rcv[k], right], axis=1).reshape(COLUMNS, 128)
        strips = both.T
        for level in range(1, LEVELS):
            to = pl.ds(2 * STRIP * level + k, STRIP, stride=2)
            sol_out[to, :] = strips[STRIP * (level - 1) : STRIP * level]


def on_device(loc_rhs, loc_inv, loc_low, loc_parent, lvl_rhs, lvl_inv, lvl_low, lvl_parent):
    vmem = pl.BlockSpec(memory_space=pltpu.VMEM)
    far = pl.BlockSpec(memory_space=pltpu.HBM)
    dma = pltpu.SemaphoreType.DMA
    square = (UNKNOWNS, UNKNOWNS)
    loc_sol, sol = pl.pallas_call(
        kernel,
        out_shape=(
            jax.ShapeDtypeStruct((LOCALS, UNKNOWNS, COLUMNS), f32),
            jax.ShapeDtypeStruct((COLUMNS, 128), f32),
        ),
        in_specs=[far] * 8,
        out_specs=(vmem, vmem),
        scratch_shapes=[
            pltpu.SMEM((LOCALS,), jnp.int32),
            pltpu.SMEM((2, LEVELS - 1), jnp.int32),
            pltpu.VMEM((LOCALS, UNKNOWNS, COLUMNS), f32),
            pltpu.VMEM((LOCALS,) + square, f32),
            pltpu.VMEM((LOCALS, 2) + square, f32),
            pltpu.VMEM((LEVELS * STRIP * 2, COLUMNS), f32),
            pltpu.VMEM((LOCALS,) + square, bf16),
            pltpu.VMEM((LOCALS,) + square, bf16),
            pltpu.VMEM((LOCALS, 2) + square, bf16),
            pltpu.VMEM((LOCALS, 2) + square, bf16),
            pltpu.VMEM((LOCALS, COLUMNS, UNKNOWNS), f32),
            pltpu.VMEM((LOCALS, UNKNOWNS, COLUMNS), f32),
            pltpu.VMEM((2, UNKNOWNS, COLUMNS), f32),
            pltpu.VMEM((2, len(BLOCKS), STRIP, UNKNOWNS), f32),
            pltpu.VMEM((2, 2, 4, 2, SHARE, UNKNOWNS), f32),
            pltpu.VMEM((4, 4, SHARE, UNKNOWNS), f32),
            pltpu.VMEM((4, SHARE, UNKNOWNS), f32),
            pltpu.VMEM((4, SHARE, UNKNOWNS), f32),
            pltpu.VMEM((PEERS, SHARE, UNKNOWNS), f32),
            pltpu.VMEM((2, SHARES, OCTET, 128), f32),
            pltpu.VMEM((PEERS, OCTET, 128), f32),
            pltpu.VMEM((OCTET, 128), f32),
            pltpu.VMEM((OCTET, 128), f32),
            pltpu.VMEM((len(BLOCKS), 4, 2, 2 * STRIP, UNKNOWNS), f32),
            pltpu.VMEM((len(BLOCKS),) + square, bf16),
            pltpu.VMEM((len(BLOCKS),) + square, bf16),
            pltpu.VMEM((len(BLOCKS),) + square, bf16),
            pltpu.VMEM((len(BLOCKS),) + square, bf16),
            pltpu.VMEM((LEVELS - 1, 2, 3, SHARE, UNKNOWNS), f32),
            pltpu.VMEM((LEVELS - 1, 2, 3, SHARE, UNKNOWNS), f32),
            pltpu.VMEM((LEVELS - 1, 2, SHARE, UNKNOWNS), f32),
            pltpu.VMEM((LEVELS - 1, 2, 3, SHARE, UNKNOWNS), f32),
            pltpu.VMEM((2, 2, OCTET, UNKNOWNS), f32),
            pltpu.VMEM((2, 4, OCTET, UNKNOWNS), f32),
            pltpu.VMEM((2, 4, 2, 2, OCTET, UNKNOWNS), f32),
            pltpu.VMEM((2, 4, 2, 2, OCTET, UNKNOWNS), f32),
            pltpu.VMEM((2, 4, 2, 2, OCTET, UNKNOWNS), f32),
            pltpu.VMEM((PEERS, OCTET, 128), f32),
            pltpu.VMEM((2, SHARES, OCTET, 128), f32),
            pltpu.VMEM((2, UNKNOWNS, COLUMNS), f32),
            dma((6,)),
            dma((len(BLOCKS),)),
            dma((2,)),
            dma((2,)),
            dma,
            dma,
            dma,
            dma,
            dma,
            dma,
            dma,
            dma((TRIOS,)),
            dma,
            dma((TRIOS,)),
            dma((TRIOS,)),
            dma,
            dma((TRIOS,)),
            dma,
            dma((LEVELS - 1, 2)),
            dma,
            dma((LEVELS - 1, 2)),
            dma((2,)),
            dma((2, 2)),
            dma((2, 2)),
            dma((2, 2)),
            dma,
            dma,
            dma,
            dma,
        ],
        compiler_params=pltpu.CompilerParams(
            collective_id=0, has_side_effects=True, vmem_limit_bytes=40 * 1024 * 1024
        ),
    )(
        *(
            pltpu.with_memory_space_constraint(operand, pltpu.HBM)
            for operand in (
                loc_parent.reshape(LOCALS),
                loc_rhs.reshape(LOCALS, UNKNOWNS, COLUMNS),
                loc_inv.reshape((LOCALS,) + square),
                loc_low.reshape((LOCALS, 2) + square),
                lvl_rhs.reshape(LEVELS * STRIP * 2, COLUMNS),
                lvl_inv.reshape(LEVELS, 2, STRIP, UNKNOWNS),
                lvl_low.reshape(LEVELS - 1, 2, 2, STRIP, UNKNOWNS),
                lvl_parent.reshape(LEVELS - 1, 2).T,
            )
        )
    )
    return loc_sol[None, None], sol.reshape(1, LEVELS, STRIP, 2, COLUMNS)


def solution(mesh):
    in_specs = (
        P("leaf", "rows", None, None, None),
        P("leaf", "rows", None, None, None),
        P("leaf", "rows", None, None, None, None),
        P("leaf", "rows", None),
        P("leaf", None, "rows", None, None),
        P("leaf", None, None, "rows", None),
        P("leaf", None, None, None, "rows", None),
        P("leaf", None, None),
    )
    out_specs = (P("leaf", "rows", None, None, None), P("leaf", None, "rows", None, None))
    return jax.shard_map(
        on_device, mesh=mesh, in_specs=in_specs, out_specs=out_specs, check_vma=False
    )
```

```python
import functools

import jax
import jax.numpy as jnp
from jax import lax
from jax.experimental import pallas as pl
from jax.experimental.pallas import tpu as pltpu
from jax.sharding import PartitionSpec as P

MESH = pl.DeviceIdType.MESH
f32 = jnp.float32
bf16 = jnp.bfloat16

UNKNOWNS = 256
COLUMNS = 128
STRIP = 16
SHARE = 16
SHARES = 8
PEERS = 16
LOCALS = 3
LEVELS = 4
HALF = UNKNOWNS // 2
OCTET = 8
BLOCKS = (("inv", 0), ("low", 0, 0), ("low", 0, 1), ("inv", 1), ("low", 1, 0), ("low", 1, 1), ("inv", 2), ("low", 2, 0), ("inv", 3))
TRIOS = 3


def split(value):
    high = value.astype(bf16)
    return high, (value - high.astype(f32)).astype(bf16)


def dot(left, right, dim):
    return lax.dot_general(
        left, right, (((1,), (dim,)), ((), ())), preferred_element_type=f32
    )


def multiply(left, right, dim):
    return dot(left[0], right[0], dim) + dot(left[1], right[0], dim) + dot(left[0], right[1], dim)


def product(vectors, mat_high, mat_low, dim):
    return multiply(split(vectors), (mat_high, mat_low), dim)


def thin_product(vectors, mat_high, mat_low, dim):
    high = vectors.astype(bf16).astype(f32)
    both = jnp.concatenate([high, vectors - high], axis=0).astype(bf16)
    total = dot(both, mat_high, dim) + dot(both, mat_low, dim)
    return total[:SHARE] + total[SHARE:]


def regroup(tiles):
    group = lax.div(lax.broadcasted_iota(jnp.int32, (2, OCTET, 128), 2), STRIP)
    flat = tiles.reshape(PEERS * OCTET, 128)
    turned = [flat.reshape(2, 8, OCTET, 128)]
    for turn in range(1, 8):
        turned.append(pltpu.roll(flat, STRIP * turn, 1).reshape(2, 8, OCTET, 128))
    results = []
    for g in range(8):
        total = turned[-g % 8][:, 0]
        for m in range(1, 8):
            total = jnp.where(group == m, turned[(m - g) % 8][:, m], total)
        results.append(total)
    return results


def kinds_at(level):
    return 2 if level + 2 < LEVELS else 1


def inv_at(level):
    return BLOCKS.index(("inv", level))


def low_at(level, kind):
    return BLOCKS.index(("low", level, kind))


def trio(index):
    return slice(3 * index, 3 * index + 3)


def pieces(index, upper):
    if not upper:
        return [(trio(index), slice(0, UNKNOWNS))]
    found = []
    for m in range(3 * index, 3 * index + 3):
        lanes = slice(0, HALF if BLOCKS[m][0] == "inv" else UNKNOWNS)
        if found and found[-1][1] == lanes:
            found[-1] = (slice(found[-1][0].start, m + 1), lanes)
        else:
            found.append((slice(m, m + 1), lanes))
    return found


def kernel(
    loc_names, loc_rhs, loc_inv, loc_low, lvl_rhs, lvl_inv, lvl_low, lvl_names,
    loc_out, sol_out,
    loc_parent, lvl_parent, rhs_s, inv_s, low_s, lvl_rhs_s, inv_high, inv_rest, low_high, low_rest, y_s, solved_s, sums_s,
    strips_s, snd, x_part, x_sum, x_last, y_last, ride_snd, ride_rcv, names_snd, names_rcv,
    mats, mat_high, mat_rest, turned_high, turned_rest, up_snd, up_rcv, down_snd, down_rcv,
    own_snd, ring_rcv, x_rcv, next_rcv, beside_rcv, sol_snd, sol_rcv, turned_s,
    load_sem, strips_sem, part_snd_sem, part_sem, last_snd_sem, last_sem,
    ride_snd_sem, ride_sem, names_snd_sem, names_sem, strip_snd_sem, strip_sem, ring_snd_sem, ring_sem, far_sem,
    pair_snd_sem, pair_sem, up_snd_sem, up_sem, down_snd_sem, down_sem, early_snd_sem, early_sem, late_snd_sem, late_sem,
    sol_snd_sem, sol_sem, beside_snd_sem, beside_sem,
):
    leaf = lax.axis_index("leaf")
    rows = lax.axis_index("rows")
    z, core = lax.div(leaf, 2), lax.rem(leaf, 2)
    y, x = lax.div(rows, 4), lax.rem(rows, 4)
    x_high, parity = lax.div(x, 2), lax.rem(x, 2)
    carried = 2 * z + x_high
    place = jnp.where(x_high == 0, parity, 1 - parity)
    share = 2 * y + core
    own = x_high == core

    def x_of(odd, slot):
        return 2 * odd + jnp.where(odd == 0, slot, 1 - slot)

    def around(value):
        return [value] + [jnp.where(value + n >= 4, value + n - 4, value + n) for n in range(1, 4)]

    slots, cores = [place, 1 - place], [core, 1 - core]
    ys, xs = around(y), around(x)
    carriers = [
        ((2 * z + there_core, 4 * there_y + x_of(core, slot)), 2 * there_y + there_core, slot)
        for there_y in ys
        for slot in slots
        for there_core in cores
    ]
    carrier_shares = [(there_y, there_core) for there_y in ys for _ in slots for there_core in cores]
    holders = [(carried, 4 * there_y + there_x) for there_y in ys for there_x in xs]
    x_carriers = [
        ((2 * z + there_core, 4 * y + x_of(core, slot)), slot, there_core)
        for slot in slots
        for there_core in cores
    ]
    x_holders = [(carried, 4 * y + there_x) for there_x in xs]
    sibling = (2 * z + 1 - core, rows)
    z_half = lax.rem(lax.div(z, 2), 2)
    beside = (leaf, rows + 1 - 2 * parity)
    partners = [[beside] + [(leaf, 4 * y + x_of(1 - x_high, slot)) for slot in range(2)]]
    for there_z in (z + 1 - 2 * lax.rem(z, 2), z + 2 - 4 * z_half):
        partners.append(
            [beside] + [(2 * there_z + core, 4 * y + x_of(x_high, slot)) for slot in range(2)]
        )
    y_up, y_far, y_down = ys[1], ys[2], ys[3]
    up, far, down = [(leaf, 4 * there_y + x) for there_y in (y_up, y_far, y_down)]

    loads = [
        pltpu.make_async_copy(loc_rhs, rhs_s, load_sem.at[0]),
        pltpu.make_async_copy(loc_inv, inv_s, load_sem.at[1]),
        pltpu.make_async_copy(loc_low, low_s, load_sem.at[2]),
        pltpu.make_async_copy(lvl_rhs, lvl_rhs_s, load_sem.at[3]),
        pltpu.make_async_copy(loc_names, loc_parent, load_sem.at[4]),
        pltpu.make_async_copy(lvl_names, lvl_parent, load_sem.at[5]),
    ]
    strip_loads = [
        pltpu.make_async_copy(
            lvl_inv.at[level], strips_s.at[:, inv_at(level)], strips_sem.at[inv_at(level)]
        )
        for level in range(LEVELS)
    ] + [
        pltpu.make_async_copy(
            lvl_low.at[level, :, 0 : kinds_at(level)],
            strips_s.at[:, low_at(level, 0) : low_at(level, 0) + kinds_at(level)],
            strips_sem.at[low_at(level, 0)],
        )
        for level in range(LEVELS - 1)
    ]
    for load in loads + strip_loads:
        load.start()

    for level in range(LEVELS):
        mats[inv_at(level), 0:2, :, :, HALF:] = jnp.zeros((2, 2, 2 * STRIP, HALF), f32)

    barrier = pltpu.get_barrier_semaphore()

    def greet(device):
        pl.semaphore_signal(barrier, inc=1, device_id=device, device_id_type=MESH)

    others = [carrier[0] for carrier in carriers[1:]] + holders[1:] + [sibling, beside, up, far, down]
    others += [device for three in partners for device in three[1:]]
    for device in others:
        greet(device)

    @pl.when(jnp.logical_not(own))
    def _():
        greet(carriers[0][0])
        greet(holders[0])

    for load in loads[:2]:
        load.wait()
    for i in range(LOCALS):
        high, rest = split(inv_s[i])
        inv_high[i] = high
        inv_rest[i] = rest
        solved_s[i] = multiply((high, rest), split(rhs_s[i]), 0)
    pl.semaphore_wait(barrier, len(others) + jnp.where(own, 0, 2))

    def send(src, dst, send_sem, recv_sem, device):
        return pltpu.make_async_remote_copy(
            src_ref=src, dst_ref=dst, send_sem=send_sem, recv_sem=recv_sem,
            device_id=device, device_id_type=MESH,
        )

    def send_or_keep(copies):
        @pl.when(own)
        def _():
            for src, dst, send_sem, recv_sem, device in copies:
                pltpu.make_async_copy(src, dst, recv_sem).start()

        @pl.when(jnp.logical_not(own))
        def _():
            for copy in copies:
                send(*copy).start()

    def drain(ref, sem):
        pltpu.make_async_copy(ref, ref, sem).wait()

    strip = pl.ds(pl.multiple_of(STRIP * parity, STRIP), STRIP)
    first, second = slice(0, STRIP), slice(STRIP, 2 * STRIP)

    def by_rows(at_y, index, act):
        for upper in (True, False):

            @pl.when((at_y < 2) if upper else (at_y >= 2))
            def _():
                for blocks, lanes in pieces(index, upper):
                    act(blocks, lanes)

    def along_x(index):
        def start(blocks, lanes):
            copies = [
                (
                    strips_s.at[slot, blocks, :, lanes],
                    mats.at[blocks, y, x_high, strip, lanes],
                    strip_snd_sem, strip_sem.at[index], (2 * z + x_high, 4 * y + x_of(core, slot)),
                )
                for slot in slots
            ]
            send(*copies[1]).start()
            send_or_keep(copies[:1])

        by_rows(y, index, start)

    def rows_of(at_y, part):
        return lambda blocks, lanes: mats.at[blocks, at_y, core, part, lanes]

    def wait_rows(at_y, index, part, sem):
        by_rows(at_y, index, lambda blocks, lanes: drain(rows_of(at_y, part)(blocks, lanes), sem))

    def units(index, upper):
        return sum(
            (blocks.stop - blocks.start) * (lanes.stop // HALF) for blocks, lanes in pieces(index, upper)
        )

    def wait_all(at_y, index, sem):
        for upper in (True, False):

            @pl.when((at_y < 2) if upper else (at_y >= 2))
            def _():
                drain(y_last.at[0 : units(index, upper)], sem)

    def send_rows(at_y, index, part, sem, device):
        def start(blocks, lanes):
            ref = rows_of(at_y, part)(blocks, lanes)
            send(ref, ref, ring_snd_sem, sem, device).start()

        by_rows(at_y, index, start)

    every = slice(0, 2 * STRIP)

    def along_y(index):
        wait_all(y, index, strip_sem.at[index])
        for device in (up, down):
            send_rows(y, index, every, ring_sem.at[index], device)
        if index == 0:
            send_rows(y, index, every, far_sem.at[index], far)

    def wait_ring(index):
        drain(y_last.at[0 : units(index, True) + units(index, False)], ring_sem.at[index])

    def to_far(index):
        wait_ring(index)
        for at_y, half_strip, device in ((y_down, first, up), (y_up, second, down)):
            send_rows(at_y, index, half_strip, far_sem.at[index], device)

    def pair_parts(index, collector):
        return [
            mats.at[blocks, 0:2, collector, :, lanes] for blocks, lanes in pieces(index, True)
        ] + [mats.at[trio(index), 2:4, collector]]

    def to_sibling(index):
        if index == 0:
            wait_ring(index)
        wait_all(y_far, index, far_sem.at[index])
        for n, part in enumerate(pair_parts(index, core)):
            send(part, part, pair_snd_sem, pair_sem.at[index, n], sibling).start()

    def take(index):
        for n, part in enumerate(pair_parts(index, 1 - core)):
            drain(part, pair_sem.at[index, n])
        parts = {}
        for m in range(3 * index, 3 * index + 3):
            parts[BLOCKS[m]] = split(mats[m].reshape(UNKNOWNS, UNKNOWNS))
            if BLOCKS[m][0] == "inv":
                mat_high[m], mat_rest[m] = parts[BLOCKS[m]]
        for m in range(3 * index, 3 * index + 3):
            name, level = BLOCKS[m][:2]
            if name == "low":
                both = multiply(parts[BLOCKS[m]], parts["inv", level], 0)
                mat_high[m], mat_rest[m] = split(both)
                if index > 0:
                    turned_high[m], turned_rest[m] = split(both.T)
            elif level + 1 == LEVELS:
                turned = split(mats[m].reshape(UNKNOWNS, UNKNOWNS).T)
                mat_high[m], mat_rest[m] = split(multiply(turned, parts[BLOCKS[m]], 0))

    def thin_up(vectors, m):
        if m < 3:
            return thin(vectors, m, 1)
        return thin_product(vectors, turned_high[m], turned_rest[m], 0)

    def thin(vectors, m, dim):
        return thin_product(vectors, mat_high[m], mat_rest[m], dim)

    for load in strip_loads:
        load.wait()
    along_x(0)
    for load in loads[2:]:
        load.wait()
    pick = [
        [jnp.where(loc_parent[i] == slot, 1.0, 0.0).astype(f32) for slot in range(2)]
        for i in range(LOCALS)
    ]

    y_others = [(up, y_up), (far, y_far), (down, y_down)]

    def local_updates(kind):
        for i in range(LOCALS):
            high, rest = split(low_s[i, kind])
            low_high[i, kind] = high
            low_rest[i, kind] = rest
            update = multiply((high, rest), split(solved_s[i]), 0)
            for slot in range(2):
                if i == 0:
                    sums_s[slot] = pick[i][slot] * update
                else:
                    sums_s[slot] += pick[i][slot] * update
        for slot in range(2):
            snd[kind, slot] = sums_s[slot].T.reshape(4, 2, SHARE, UNKNOWNS)

    def x_first():
        copies = [
            (snd.at[0, slot, :, there_core], x_part.at[x], part_snd_sem.at[0], part_sem.at[0], device)
            for device, slot, there_core in x_carriers
        ]
        for copy in copies[1:]:
            send(*copy).start()
        send_or_keep(copies[:1])

    def x_then_y():
        drain(x_part, part_sem.at[0])
        x_sum[...] = (x_part[0] + x_part[1]) + (x_part[2] + x_part[3])
        for device, there_y in y_others:
            send(
                x_sum.at[there_y], x_last.at[y], last_snd_sem, last_sem, device
            ).start()

    def straight():
        copies = [
            (
                snd.at[1, slot, index_y, there_core], y_last.at[rows],
                part_snd_sem.at[1], part_sem.at[1], device,
            )
            for (device, _, slot), (index_y, there_core) in zip(carriers, carrier_shares)
        ]
        for copy in copies[1:]:
            send(*copy).start()
        send_or_keep(copies[:1])

    local_updates(0)
    x_first()
    along_y(0)
    along_x(1)
    along_x(2)
    local_updates(1)
    straight()
    row = lax.broadcasted_iota(jnp.int32, (OCTET, 128), 0)
    names = jnp.zeros((OCTET, 128), f32)
    for k in range(2):
        for level in range(LEVELS - 1):
            names = jnp.where(row == 4 * k + level, lvl_parent[k, level].astype(f32), names)
    names_snd[...] = names
    send(names_snd, names_rcv, names_snd_sem, names_sem, sibling).start()
    for k in range(2):
        strips = [
            lvl_rhs_s[pl.ds(2 * STRIP * level + k, STRIP, stride=2), :] for level in range(LEVELS)
        ]
        strips.append(jnp.zeros((HALF - LEVELS * STRIP, COLUMNS), f32))
        extra = jnp.concatenate(strips, axis=0).T.reshape(SHARES, 2, OCTET, 128)
        right = pltpu.roll(extra[:, 1].reshape(SHARES * OCTET, 128), 64, 1)
        ride_snd[k] = extra[:, 0] + right.reshape(SHARES, OCTET, 128)
    rides = [
        (ride_snd.at[slot, index], ride_rcv.at[rows], ride_snd_sem, ride_sem, device)
        for device, index, slot in carriers
    ]
    for ride in rides[1:]:
        send(*ride).start()
    send_or_keep(rides[:1])
    along_y(1)
    x_then_y()
    along_y(2)

    def prepare_local(i):
        inverse = (inv_high[i], inv_rest[i])
        y_s[i] = product(solved_s[i].T, inv_high[i], inv_rest[i], 0)
        for kind in range(2):
            both = multiply((low_high[i, kind], low_rest[i, kind]), inverse, 0)
            high, rest = split(both.T if kind == 0 else both)
            low_high[i, kind] = high
            low_rest[i, kind] = rest

    to_sibling(0)
    drain(ride_rcv, ride_sem)
    parts = regroup(ride_rcv[...].reshape(2, 8, OCTET, 128))
    parts = [jnp.concatenate([part[0], part[1]], axis=1) for part in parts]
    rhs = [
        jnp.concatenate([parts[level], parts[LEVELS + level]], axis=0) for level in range(LEVELS)
    ]
    drain(names_rcv, names_sem)
    names = jnp.where(own, names_snd[...], names_rcv[...])
    parent = []
    for level in range(LEVELS - 1):
        name = jnp.where(place == 0, names[level : level + 1], names[4 + level : 5 + level])
        parent.append(jnp.broadcast_to(jnp.concatenate([name, name], axis=1), (SHARE, UNKNOWNS)))
    mine, places = place.astype(f32), [(1 - place).astype(f32), 2.0, 3.0]

    def chosen(name, at_place, value):
        return jnp.where(name == at_place, value, 0.0)

    def slot_at(index):
        return 0 if index == 0 else 1 + place

    def gathered(total, buffer, sem):
        drain(buffer, sem)
        for index in range(3):
            total = total + buffer[index]
        return total

    below = []
    take(0)
    to_far(1)
    drain(x_last.at[0:3], last_sem)
    above = x_sum[y]
    for _, there_y in y_others:
        above = above + x_last[there_y]
    for level in range(LEVELS):
        kinds = kinds_at(level)
        moved = rhs[level] - above
        if level + 1 < LEVELS:
            out = [thin_up(moved, low_at(level, kind)) for kind in range(kinds)]
            if level == 0:
                drain(y_last, part_sem.at[1])
                pending = y_last[0]
                for source in range(1, PEERS):
                    pending = pending + y_last[source]
            else:
                pending = gathered(own_pending, up_rcv.at[level - 1, 1], up_sem.at[level - 1, 1])
            out[0] = out[0] + pending
            for kind in range(kinds):
                for index in (1, 2, 0):
                    up_snd[level, kind, index] = chosen(parent[level], places[index], out[kind])
                    send(
                        up_snd.at[level, kind, index], up_rcv.at[level, kind, slot_at(index)],
                        up_snd_sem, up_sem.at[level, kind], partners[level][index],
                    ).start()
            own_pending = chosen(parent[level], mine, out[-1])
            if level == 0:
                to_sibling(1)
                to_far(2)
            below.append(thin(thin(moved, inv_at(level), 1), inv_at(level), 0))
            if level + 1 < TRIOS:
                take(level + 1)
            else:
                prepare_local(0)
            if level == 0:
                to_sibling(2)
            own_above = chosen(parent[level], mine, out[0])
            above = gathered(own_above, up_rcv.at[level, 0], up_sem.at[level, 0])

    def send_down(level, kind, value):
        down_snd[level, kind] = value
        for index in (1, 2, 0):
            send(
                down_snd.at[level, kind], down_rcv.at[level, kind, slot_at(index)],
                down_snd_sem, down_sem.at[level, kind], partners[level][index],
            ).start()

    def pooled(level, kind, value):
        total = chosen(parent[level], mine, value)
        drain(down_rcv.at[level, kind], down_sem.at[level, kind])
        for index in range(3):
            total = total + chosen(parent[level], places[index], down_rcv[level, kind, index])
        return total

    def spread(step, landing, value):
        own_snd[step] = value.reshape(2, OCTET, UNKNOWNS)
        ring_rcv[step, y] = value[0:OCTET]
        for device, _ in y_others:
            send(
                own_snd.at[step, 0], ring_rcv.at[step, y],
                early_snd_sem.at[step], early_sem.at[step, 0], device,
            ).start()
        copies = [
            (
                own_snd.at[step, 1], landing.at[place, y, core, 1],
                early_snd_sem.at[step], early_sem.at[step, 1], device,
            )
            for device in x_holders
        ]
        for copy in copies[1:]:
            send(*copy).start()
        send_or_keep(copies[:1])

    def spread_on(step, landing):
        drain(ring_rcv.at[step, 0:3], early_sem.at[step, 0])
        copies = [
            (
                ring_rcv.at[step], landing.at[place, :, core, 0],
                late_snd_sem.at[step, 0], late_sem.at[step, 0], device,
            )
            for device in x_holders
        ]
        for copy in copies[1:]:
            send(*copy).start()
        send_or_keep(copies[:1])
        part = landing.at[:, y, :, 1]
        drain(part, early_sem.at[step, 1])
        for device, _ in y_others:
            send(part, part, late_snd_sem.at[step, 1], late_sem.at[step, 1], device).start()

    def spread_end(step, landing):
        drain(landing.at[:, :, :, 0], late_sem.at[step, 0])
        drain(landing.at[:, 0:3, :, 1], late_sem.at[step, 1])

    def whole(landing):
        return landing[...].reshape(2, COLUMNS, UNKNOWNS)

    current, current_parent = thin(moved, inv_at(LEVELS - 1), 0), None
    results = [None] * LEVELS
    results[LEVELS - 1] = current
    for level in range(LEVELS - 2, -1, -1):
        send_down(level, 0, current)
        if level == 0:
            spread(0, next_rcv, current)
            spread_on(0, next_rcv)
        else:
            prepare_local(LEVELS - 1 - level)
        left = below[level]
        if kinds_at(level) == 2:
            left = left - thin(pooled(level, 1, current_parent), low_at(level, 1), 0)
        current_parent = pooled(level, 0, current)
        if level > 0:
            send_down(level - 1, 1, current_parent)
        current = left - thin(current_parent, low_at(level, 0), 0)
        results[level] = current
    spread(1, x_rcv, current)

    spread_end(0, next_rcv)
    send(next_rcv, beside_rcv, beside_snd_sem, beside_sem, sibling).start()
    halves = []
    for octet in (slice(0, OCTET), slice(OCTET, SHARE)):
        for part in results[1:] + results[3:]:
            halves.append(jnp.stack([part[octet, 0:HALF], part[octet, HALF:]], axis=0))
    tiles = regroup(jnp.stack(halves, axis=1))
    for m in range(8):
        for h in range(2):
            sol_snd[8 * h + m] = tiles[m][h]
    spread_on(1, x_rcv)
    copies = [
        (sol_snd.at[device[1]], sol_rcv.at[place, share], sol_snd_sem, sol_sem, device)
        for device in holders
    ]
    for copy in copies[1:]:
        send(*copy).start()
    send_or_keep(copies[:1])
    drain(beside_rcv, beside_sem)
    own_next, beside_next = whole(next_rcv), whole(beside_rcv)
    for i in range(LOCALS):
        grand = None
        for at_place in range(4):
            weight = sum(
                pick[i][k] * jnp.where(lvl_parent[k, 0] == at_place, 1.0, 0.0).astype(f32)
                for k in range(2)
            )
            if at_place < 2:
                term = weight * own_next[at_place]
            else:
                term = weight * beside_next[at_place - 2]
            grand = term if grand is None else grand + term
        loc_out[i] = (y_s[i] - product(grand, low_high[i, 1], low_rest[i, 1], 0)).T
    drain(x_part.at[0:3], part_snd_sem.at[0])
    drain(y_last.at[1:], part_snd_sem.at[1])
    drain(x_last.at[0:3], last_snd_sem)
    drain(ride_rcv.at[1:], ride_snd_sem)
    drain(names_snd, names_snd_sem)
    for step in range(2):
        for _ in range(2):
            drain(ring_rcv.at[step, 0:3], early_snd_sem.at[step])
        for _ in range(3):
            drain(ring_rcv.at[step], late_snd_sem.at[step, 0])
        drain(x_rcv.at[:, 0:3, :, 1], late_snd_sem.at[step, 1])
    drain(sol_snd.at[1:], sol_snd_sem)
    def strips_sent():
        for index in range(TRIOS):
            by_rows(
                y, index,
                lambda blocks, lanes: drain(strips_s.at[0, blocks, :, lanes], strip_snd_sem),
            )

    strips_sent()
    for index in range(TRIOS):
        for _ in range(3 if index == 0 else 2):
            wait_rows(y, index, every, ring_snd_sem)
        if index > 0:
            wait_rows(y_down, index, first, ring_snd_sem)
            wait_rows(y_up, index, second, ring_snd_sem)
        for part in pair_parts(index, core):
            drain(part, pair_snd_sem)
    drain(beside_rcv, beside_snd_sem)
    for level in range(LEVELS - 1):
        for kind in range(kinds_at(level)):
            drain(up_rcv.at[level, kind], up_snd_sem)
            drain(down_rcv.at[level, kind], down_snd_sem)

    @pl.when(jnp.logical_not(own))
    def _():
        drain(x_part.at[0], part_snd_sem.at[0])
        drain(y_last.at[0], part_snd_sem.at[1])
        drain(ride_rcv.at[0], ride_snd_sem)
        for step in range(2):
            drain(ring_rcv.at[step, 0], early_snd_sem.at[step])
            drain(ring_rcv.at[step], late_snd_sem.at[step, 0])
        drain(sol_snd.at[0], sol_snd_sem)
        strips_sent()

    spread_end(1, x_rcv)
    x_all = whole(x_rcv)
    for i in range(LOCALS):
        above_x = pick[i][0] * x_all[0] + pick[i][1] * x_all[1]
        loc_out[i] -= multiply((low_high[i, 0], low_rest[i, 0]), split(above_x), 1)
    here = pl.ds(pl.multiple_of(STRIP * rows, STRIP), STRIP)
    for k in range(2):
        turned_s[k] = x_all[k].T
        sol_out[pl.ds(k, STRIP, stride=2), :] = turned_s[k, here, :]
    drain(sol_rcv, sol_sem)
    for k in range(2):
        packed = sol_rcv[k].reshape(SHARES * OCTET, 128)
        right = pltpu.roll(packed, 64, 1).reshape(SHARES, OCTET, 128)
        both = jnp.stack([sol_rcv[k], right], axis=1).reshape(COLUMNS, 128)
        strips = both.T
        for level in range(1, LEVELS):
            to = pl.ds(2 * STRIP * level + k, STRIP, stride=2)
            sol_out[to, :] = strips[STRIP * (level - 1) : STRIP * level]


def on_device(loc_rhs, loc_inv, loc_low, loc_parent, lvl_rhs, lvl_inv, lvl_low, lvl_parent):
    vmem = pl.BlockSpec(memory_space=pltpu.VMEM)
    far = pl.BlockSpec(memory_space=pltpu.HBM)
    dma = pltpu.SemaphoreType.DMA
    square = (UNKNOWNS, UNKNOWNS)
    loc_sol, sol = pl.pallas_call(
        kernel,
        out_shape=(
            jax.ShapeDtypeStruct((LOCALS, UNKNOWNS, COLUMNS), f32),
            jax.ShapeDtypeStruct((COLUMNS, 128), f32),
        ),
        in_specs=[far] * 8,
        out_specs=(vmem, vmem),
        scratch_shapes=[
            pltpu.SMEM((LOCALS,), jnp.int32),
            pltpu.SMEM((2, LEVELS - 1), jnp.int32),
            pltpu.VMEM((LOCALS, UNKNOWNS, COLUMNS), f32),
            pltpu.VMEM((LOCALS,) + square, f32),
            pltpu.VMEM((LOCALS, 2) + square, f32),
            pltpu.VMEM((LEVELS * STRIP * 2, COLUMNS), f32),
            pltpu.VMEM((LOCALS,) + square, bf16),
            pltpu.VMEM((LOCALS,) + square, bf16),
            pltpu.VMEM((LOCALS, 2) + square, bf16),
            pltpu.VMEM((LOCALS, 2) + square, bf16),
            pltpu.VMEM((LOCALS, COLUMNS, UNKNOWNS), f32),
            pltpu.VMEM((LOCALS, UNKNOWNS, COLUMNS), f32),
            pltpu.VMEM((2, UNKNOWNS, COLUMNS), f32),
            pltpu.VMEM((2, len(BLOCKS), STRIP, UNKNOWNS), f32),
            pltpu.VMEM((2, 2, 4, 2, SHARE, UNKNOWNS), f32),
            pltpu.VMEM((4, 4, SHARE, UNKNOWNS), f32),
            pltpu.VMEM((4, SHARE, UNKNOWNS), f32),
            pltpu.VMEM((4, SHARE, UNKNOWNS), f32),
            pltpu.VMEM((PEERS, SHARE, UNKNOWNS), f32),
            pltpu.VMEM((2, SHARES, OCTET, 128), f32),
            pltpu.VMEM((PEERS, OCTET, 128), f32),
            pltpu.VMEM((OCTET, 128), f32),
            pltpu.VMEM((OCTET, 128), f32),
            pltpu.VMEM((len(BLOCKS), 4, 2, 2 * STRIP, UNKNOWNS), f32),
            pltpu.VMEM((len(BLOCKS),) + square, bf16),
            pltpu.VMEM((len(BLOCKS),) + square, bf16),
            pltpu.VMEM((len(BLOCKS),) + square, bf16),
            pltpu.VMEM((len(BLOCKS),) + square, bf16),
            pltpu.VMEM((LEVELS - 1, 2, 3, SHARE, UNKNOWNS), f32),
            pltpu.VMEM((LEVELS - 1, 2, 3, SHARE, UNKNOWNS), f32),
            pltpu.VMEM((LEVELS - 1, 2, SHARE, UNKNOWNS), f32),
            pltpu.VMEM((LEVELS - 1, 2, 3, SHARE, UNKNOWNS), f32),
            pltpu.VMEM((2, 2, OCTET, UNKNOWNS), f32),
            pltpu.VMEM((2, 4, OCTET, UNKNOWNS), f32),
            pltpu.VMEM((2, 4, 2, 2, OCTET, UNKNOWNS), f32),
            pltpu.VMEM((2, 4, 2, 2, OCTET, UNKNOWNS), f32),
            pltpu.VMEM((2, 4, 2, 2, OCTET, UNKNOWNS), f32),
            pltpu.VMEM((PEERS, OCTET, 128), f32),
            pltpu.VMEM((2, SHARES, OCTET, 128), f32),
            pltpu.VMEM((2, UNKNOWNS, COLUMNS), f32),
            dma((6,)),
            dma((len(BLOCKS),)),
            dma((2,)),
            dma((2,)),
            dma,
            dma,
            dma,
            dma,
            dma,
            dma,
            dma,
            dma((TRIOS,)),
            dma,
            dma((TRIOS,)),
            dma((TRIOS,)),
            dma,
            dma((TRIOS, 4)),
            dma,
            dma((LEVELS - 1, 2)),
            dma,
            dma((LEVELS - 1, 2)),
            dma((2,)),
            dma((2, 2)),
            dma((2, 2)),
            dma((2, 2)),
            dma,
            dma,
            dma,
            dma,
        ],
        compiler_params=pltpu.CompilerParams(
            collective_id=0, has_side_effects=True, vmem_limit_bytes=40 * 1024 * 1024
        ),
    )(
        *(
            pltpu.with_memory_space_constraint(operand, pltpu.HBM)
            for operand in (
                loc_parent.reshape(LOCALS),
                loc_rhs.reshape(LOCALS, UNKNOWNS, COLUMNS),
                loc_inv.reshape((LOCALS,) + square),
                loc_low.reshape((LOCALS, 2) + square),
                lvl_rhs.reshape(LEVELS * STRIP * 2, COLUMNS),
                lvl_inv.reshape(LEVELS, 2, STRIP, UNKNOWNS),
                lvl_low.reshape(LEVELS - 1, 2, 2, STRIP, UNKNOWNS),
                lvl_parent.reshape(LEVELS - 1, 2).T,
            )
        )
    )
    return loc_sol[None, None], sol.reshape(1, LEVELS, STRIP, 2, COLUMNS)


def solution(mesh):
    in_specs = (
        P("leaf", "rows", None, None, None),
        P("leaf", "rows", None, None, None),
        P("leaf", "rows", None, None, None, None),
        P("leaf", "rows", None),
        P("leaf", None, "rows", None, None),
        P("leaf", None, None, "rows", None),
        P("leaf", None, None, None, "rows", None),
        P("leaf", None, None),
    )
    out_specs = (P("leaf", "rows", None, None, None), P("leaf", None, "rows", None, None))
    return jax.shard_map(
        on_device, mesh=mesh, in_specs=in_specs, out_specs=out_specs, check_vma=False
    )
```

```python
import functools

import jax
import jax.numpy as jnp
from jax import lax
from jax.experimental import pallas as pl
from jax.experimental.pallas import tpu as pltpu
from jax.sharding import PartitionSpec as P

MESH = pl.DeviceIdType.MESH
f32 = jnp.float32
bf16 = jnp.bfloat16

UNKNOWNS = 256
COLUMNS = 128
STRIP = 16
SHARE = 16
SHARES = 8
PEERS = 16
LOCALS = 3
LEVELS = 4
HALF = UNKNOWNS // 2
OCTET = 8
BLOCKS = (("inv", 0), ("low", 0, 0), ("low", 0, 1), ("inv", 1), ("low", 1, 0), ("low", 1, 1), ("inv", 2), ("low", 2, 0), ("inv", 3))
TRIOS = 3


def split(value):
    high = value.astype(bf16)
    return high, (value - high.astype(f32)).astype(bf16)


def dot(left, right, dim):
    return lax.dot_general(
        left, right, (((1,), (dim,)), ((), ())), preferred_element_type=f32
    )


def multiply(left, right, dim):
    return dot(left[0], right[0], dim) + dot(left[1], right[0], dim) + dot(left[0], right[1], dim)


def product(vectors, mat_high, mat_low, dim):
    return multiply(split(vectors), (mat_high, mat_low), dim)


def thin_product(vectors, mat_high, mat_low, dim):
    high = vectors.astype(bf16).astype(f32)
    both = jnp.concatenate([high, vectors - high], axis=0).astype(bf16)
    total = dot(both, mat_high, dim) + dot(both, mat_low, dim)
    return total[:SHARE] + total[SHARE:]


def regroup(tiles):
    group = lax.div(lax.broadcasted_iota(jnp.int32, (2, OCTET, 128), 2), STRIP)
    flat = tiles.reshape(PEERS * OCTET, 128)
    turned = [flat.reshape(2, 8, OCTET, 128)]
    for turn in range(1, 8):
        turned.append(pltpu.roll(flat, STRIP * turn, 1).reshape(2, 8, OCTET, 128))
    results = []
    for g in range(8):
        total = turned[-g % 8][:, 0]
        for m in range(1, 8):
            total = jnp.where(group == m, turned[(m - g) % 8][:, m], total)
        results.append(total)
    return results


def kinds_at(level):
    return 2 if level + 2 < LEVELS else 1


def inv_at(level):
    return BLOCKS.index(("inv", level))


def low_at(level, kind):
    return BLOCKS.index(("low", level, kind))


def trio(index):
    return slice(3 * index, 3 * index + 3)


def kernel(
    loc_names, loc_rhs, loc_inv, loc_low, lvl_rhs, lvl_inv, lvl_low, lvl_names,
    loc_out, sol_out,
    loc_parent, lvl_parent, rhs_s, inv_s, low_s, lvl_rhs_s, inv_high, inv_rest, low_high, low_rest, y_s, solved_s, sums_s,
    strips_s, snd, x_part, x_sum, x_last, y_last, ride_snd, ride_rcv, names_snd, names_rcv,
    mats, mat_high, mat_rest, up_snd, up_rcv, down_snd, down_rcv,
    own_snd, ring_rcv, x_rcv, next_rcv, beside_rcv, sol_snd, sol_rcv, turned_s,
    load_sem, strips_sem, part_snd_sem, part_sem, last_snd_sem, last_sem,
    ride_snd_sem, ride_sem, names_snd_sem, names_sem, strip_snd_sem, strip_sem, ring_snd_sem, ring_sem, far_sem,
    pair_snd_sem, pair_sem, up_snd_sem, up_sem, down_snd_sem, down_sem, early_snd_sem, early_sem, late_snd_sem, late_sem,
    sol_snd_sem, sol_sem, beside_snd_sem, beside_sem,
):
    leaf = lax.axis_index("leaf")
    rows = lax.axis_index("rows")
    z, core = lax.div(leaf, 2), lax.rem(leaf, 2)
    y, x = lax.div(rows, 4), lax.rem(rows, 4)
    x_high, parity = lax.div(x, 2), lax.rem(x, 2)
    carried = 2 * z + x_high
    place = jnp.where(x_high == 0, parity, 1 - parity)
    share = 2 * y + core
    own = x_high == core

    def x_of(odd, slot):
        return 2 * odd + jnp.where(odd == 0, slot, 1 - slot)

    def around(value):
        return [value] + [jnp.where(value + n >= 4, value + n - 4, value + n) for n in range(1, 4)]

    slots, cores = [place, 1 - place], [core, 1 - core]
    ys, xs = around(y), around(x)
    carriers = [
        ((2 * z + there_core, 4 * there_y + x_of(core, slot)), 2 * there_y + there_core, slot)
        for there_y in ys
        for slot in slots
        for there_core in cores
    ]
    carrier_shares = [(there_y, there_core) for there_y in ys for _ in slots for there_core in cores]
    holders = [(carried, 4 * there_y + there_x) for there_y in ys for there_x in xs]
    x_carriers = [
        ((2 * z + there_core, 4 * y + x_of(core, slot)), slot, there_core)
        for slot in slots
        for there_core in cores
    ]
    x_holders = [(carried, 4 * y + there_x) for there_x in xs]
    sibling = (2 * z + 1 - core, rows)
    z_half = lax.rem(lax.div(z, 2), 2)
    beside = (leaf, rows + 1 - 2 * parity)
    partners = [[beside] + [(leaf, 4 * y + x_of(1 - x_high, slot)) for slot in range(2)]]
    for there_z in (z + 1 - 2 * lax.rem(z, 2), z + 2 - 4 * z_half):
        partners.append(
            [beside] + [(2 * there_z + core, 4 * y + x_of(x_high, slot)) for slot in range(2)]
        )
    y_up, y_far, y_down = ys[1], ys[2], ys[3]
    up, far, down = [(leaf, 4 * there_y + x) for there_y in (y_up, y_far, y_down)]

    loads = [
        pltpu.make_async_copy(loc_rhs, rhs_s, load_sem.at[0]),
        pltpu.make_async_copy(loc_inv, inv_s, load_sem.at[1]),
        pltpu.make_async_copy(loc_low, low_s, load_sem.at[2]),
        pltpu.make_async_copy(lvl_rhs, lvl_rhs_s, load_sem.at[3]),
        pltpu.make_async_copy(loc_names, loc_parent, load_sem.at[4]),
        pltpu.make_async_copy(lvl_names, lvl_parent, load_sem.at[5]),
    ]
    strip_loads = [
        pltpu.make_async_copy(
            lvl_inv.at[level], strips_s.at[:, inv_at(level)], strips_sem.at[inv_at(level)]
        )
        for level in range(LEVELS)
    ] + [
        pltpu.make_async_copy(
            lvl_low.at[level, :, 0 : kinds_at(level)],
            strips_s.at[:, low_at(level, 0) : low_at(level, 0) + kinds_at(level)],
            strips_sem.at[low_at(level, 0)],
        )
        for level in range(LEVELS - 1)
    ]
    for load in loads + strip_loads:
        load.start()

    barrier = pltpu.get_barrier_semaphore()

    def greet(device):
        pl.semaphore_signal(barrier, inc=1, device_id=device, device_id_type=MESH)

    others = [carrier[0] for carrier in carriers[1:]] + holders[1:] + [sibling, beside, up, far, down]
    others += [device for three in partners for device in three[1:]]
    for device in others:
        greet(device)

    @pl.when(jnp.logical_not(own))
    def _():
        greet(carriers[0][0])
        greet(holders[0])

    for load in loads[:2]:
        load.wait()
    for i in range(LOCALS):
        high, rest = split(inv_s[i])
        inv_high[i] = high
        inv_rest[i] = rest
        solved_s[i] = multiply((high, rest), split(rhs_s[i]), 0)
    pl.semaphore_wait(barrier, len(others) + jnp.where(own, 0, 2))

    def send(src, dst, send_sem, recv_sem, device):
        return pltpu.make_async_remote_copy(
            src_ref=src, dst_ref=dst, send_sem=send_sem, recv_sem=recv_sem,
            device_id=device, device_id_type=MESH,
        )

    def send_or_keep(copies):
        @pl.when(own)
        def _():
            for src, dst, send_sem, recv_sem, device in copies:
                pltpu.make_async_copy(src, dst, recv_sem).start()

        @pl.when(jnp.logical_not(own))
        def _():
            for copy in copies:
                send(*copy).start()

    def drain(ref, sem):
        pltpu.make_async_copy(ref, ref, sem).wait()

    strip = pl.ds(pl.multiple_of(STRIP * parity, STRIP), STRIP)
    first, second = slice(0, STRIP), slice(STRIP, 2 * STRIP)

    def along_x(index):
        copies = [
            (
                strips_s.at[slot, trio(index)], mats.at[trio(index), y, x_high, strip, :],
                strip_snd_sem, strip_sem.at[index], (2 * z + x_high, 4 * y + x_of(core, slot)),
            )
            for slot in slots
        ]
        send(*copies[1]).start()
        send_or_keep(copies[:1])

    def along_y(index):
        part = mats.at[trio(index), y, core]
        drain(part, strip_sem.at[index])
        for device in (up, down):
            send(part, part, ring_snd_sem, ring_sem.at[index], device).start()
        if index == 0:
            send(part, part, ring_snd_sem, far_sem.at[index], far).start()

    def to_far(index):
        drain(mats.at[trio(index), 0:2, core], ring_sem.at[index])
        for at_y, half_strip, device in ((y_down, first, up), (y_up, second, down)):
            part = mats.at[trio(index), at_y, core, half_strip, :]
            send(part, part, ring_snd_sem, far_sem.at[index], device).start()

    def to_sibling(index):
        if index == 0:
            drain(mats.at[trio(index), 0:2, core], ring_sem.at[index])
        drain(mats.at[trio(index), y_far, core], far_sem.at[index])
        part = mats.at[trio(index), :, core]
        send(part, part, pair_snd_sem, pair_sem.at[index], sibling).start()

    def take(index):
        drain(mats.at[trio(index), :, 1 - core], pair_sem.at[index])
        parts = {}
        for m in range(3 * index, 3 * index + 3):
            parts[BLOCKS[m]] = split(mats[m].reshape(UNKNOWNS, UNKNOWNS))
            if BLOCKS[m][0] == "inv":
                mat_high[m], mat_rest[m] = parts[BLOCKS[m]]
        for m in range(3 * index, 3 * index + 3):
            name, level = BLOCKS[m][:2]
            if name == "low":
                both = multiply(parts[BLOCKS[m]], parts["inv", level], 0)
                mat_high[m], mat_rest[m] = split(both)
            elif level + 1 == LEVELS:
                turned = split(mats[m].reshape(UNKNOWNS, UNKNOWNS).T)
                mat_high[m], mat_rest[m] = split(multiply(turned, parts[BLOCKS[m]], 0))

    def thin(vectors, m, dim):
        return thin_product(vectors, mat_high[m], mat_rest[m], dim)

    for load in strip_loads:
        load.wait()
    along_x(0)
    for load in loads[2:]:
        load.wait()
    pick = [
        [jnp.where(loc_parent[i] == slot, 1.0, 0.0).astype(f32) for slot in range(2)]
        for i in range(LOCALS)
    ]

    y_others = [(up, y_up), (far, y_far), (down, y_down)]

    def local_updates(kind):
        for i in range(LOCALS):
            high, rest = split(low_s[i, kind])
            low_high[i, kind] = high
            low_rest[i, kind] = rest
            update = multiply((high, rest), split(solved_s[i]), 0)
            for slot in range(2):
                if i == 0:
                    sums_s[slot] = pick[i][slot] * update
                else:
                    sums_s[slot] += pick[i][slot] * update
        for slot in range(2):
            snd[kind, slot] = sums_s[slot].T.reshape(4, 2, SHARE, UNKNOWNS)

    def x_first():
        copies = [
            (snd.at[0, slot, :, there_core], x_part.at[x], part_snd_sem.at[0], part_sem.at[0], device)
            for device, slot, there_core in x_carriers
        ]
        for copy in copies[1:]:
            send(*copy).start()
        send_or_keep(copies[:1])

    def x_then_y():
        drain(x_part, part_sem.at[0])
        x_sum[...] = (x_part[0] + x_part[1]) + (x_part[2] + x_part[3])
        for device, there_y in y_others:
            send(
                x_sum.at[there_y], x_last.at[y], last_snd_sem, last_sem, device
            ).start()

    def straight():
        copies = [
            (
                snd.at[1, slot, index_y, there_core], y_last.at[rows],
                part_snd_sem.at[1], part_sem.at[1], device,
            )
            for (device, _, slot), (index_y, there_core) in zip(carriers, carrier_shares)
        ]
        for copy in copies[1:]:
            send(*copy).start()
        send_or_keep(copies[:1])

    local_updates(0)
    x_first()
    along_y(0)
    along_x(1)
    along_x(2)
    local_updates(1)
    straight()
    row = lax.broadcasted_iota(jnp.int32, (OCTET, 128), 0)
    names = jnp.zeros((OCTET, 128), f32)
    for k in range(2):
        for level in range(LEVELS - 1):
            names = jnp.where(row == 4 * k + level, lvl_parent[k, level].astype(f32), names)
    names_snd[...] = names
    send(names_snd, names_rcv, names_snd_sem, names_sem, sibling).start()
    for k in range(2):
        strips = [
            lvl_rhs_s[pl.ds(2 * STRIP * level + k, STRIP, stride=2), :] for level in range(LEVELS)
        ]
        strips.append(jnp.zeros((HALF - LEVELS * STRIP, COLUMNS), f32))
        extra = jnp.concatenate(strips, axis=0).T.reshape(SHARES, 2, OCTET, 128)
        right = pltpu.roll(extra[:, 1].reshape(SHARES * OCTET, 128), 64, 1)
        ride_snd[k] = extra[:, 0] + right.reshape(SHARES, OCTET, 128)
    rides = [
        (ride_snd.at[slot, index], ride_rcv.at[rows], ride_snd_sem, ride_sem, device)
        for device, index, slot in carriers
    ]
    for ride in rides[1:]:
        send(*ride).start()
    send_or_keep(rides[:1])
    along_y(1)
    x_then_y()
    along_y(2)

    def prepare_local(i):
        inverse = (inv_high[i], inv_rest[i])
        y_s[i] = product(solved_s[i].T, inv_high[i], inv_rest[i], 0)
        for kind in range(2):
            both = multiply((low_high[i, kind], low_rest[i, kind]), inverse, 0)
            high, rest = split(both.T if kind == 0 else both)
            low_high[i, kind] = high
            low_rest[i, kind] = rest

    to_sibling(0)
    drain(ride_rcv, ride_sem)
    parts = regroup(ride_rcv[...].reshape(2, 8, OCTET, 128))
    parts = [jnp.concatenate([part[0], part[1]], axis=1) for part in parts]
    rhs = [
        jnp.concatenate([parts[level], parts[LEVELS + level]], axis=0) for level in range(LEVELS)
    ]
    drain(names_rcv, names_sem)
    names = jnp.where(own, names_snd[...], names_rcv[...])
    parent = []
    for level in range(LEVELS - 1):
        name = jnp.where(place == 0, names[level : level + 1], names[4 + level : 5 + level])
        parent.append(jnp.broadcast_to(jnp.concatenate([name, name], axis=1), (SHARE, UNKNOWNS)))
    mine, places = place.astype(f32), [(1 - place).astype(f32), 2.0, 3.0]

    def chosen(name, at_place, value):
        return jnp.where(name == at_place, value, 0.0)

    def slot_at(index):
        return 0 if index == 0 else 1 + place

    def gathered(total, buffer, sem):
        drain(buffer, sem)
        for index in range(3):
            total = total + buffer[index]
        return total

    sums = []
    below = []
    take(0)
    to_far(1)
    drain(x_last.at[0:3], last_sem)
    above = x_sum[y]
    for _, there_y in y_others:
        above = above + x_last[there_y]
    for level in range(LEVELS):
        kinds = kinds_at(level)
        moved = rhs[level] - above
        if level + 1 < LEVELS:
            out = [thin(moved, low_at(level, kind), 1) for kind in range(kinds)]
            if level == 0:
                drain(y_last, part_sem.at[1])
                pending = y_last[0]
                for source in range(1, PEERS):
                    pending = pending + y_last[source]
            else:
                pending = gathered(own_pending, up_rcv.at[level - 1, 1], up_sem.at[level - 1, 1])
            out[0] = out[0] + pending
            for kind in range(kinds):
                for index in (1, 2, 0):
                    up_snd[level, kind, index] = chosen(parent[level], places[index], out[kind])
                    send(
                        up_snd.at[level, kind, index], up_rcv.at[level, kind, slot_at(index)],
                        up_snd_sem, up_sem.at[level, kind], partners[level][index],
                    ).start()
            own_pending = chosen(parent[level], mine, out[-1])
            if level == 0:
                to_sibling(1)
                to_far(2)
            sums.append(moved)
            if level + 1 < TRIOS:
                take(level + 1)
            else:
                for index, value in enumerate(sums):
                    below.append(thin(thin(value, inv_at(index), 1), inv_at(index), 0))
            if level == 0:
                to_sibling(2)
            own_above = chosen(parent[level], mine, out[0])
            above = gathered(own_above, up_rcv.at[level, 0], up_sem.at[level, 0])

    def send_down(level, kind, value):
        down_snd[level, kind] = value
        for index in (1, 2, 0):
            send(
                down_snd.at[level, kind], down_rcv.at[level, kind, slot_at(index)],
                down_snd_sem, down_sem.at[level, kind], partners[level][index],
            ).start()

    def pooled(level, kind, value):
        total = chosen(parent[level], mine, value)
        drain(down_rcv.at[level, kind], down_sem.at[level, kind])
        for index in range(3):
            total = total + chosen(parent[level], places[index], down_rcv[level, kind, index])
        return total

    def spread(step, landing, value):
        own_snd[step] = value.reshape(2, OCTET, UNKNOWNS)
        ring_rcv[step, y] = value[0:OCTET]
        for device, _ in y_others:
            send(
                own_snd.at[step, 0], ring_rcv.at[step, y],
                early_snd_sem.at[step], early_sem.at[step, 0], device,
            ).start()
        copies = [
            (
                own_snd.at[step, 1], landing.at[place, y, core, 1],
                early_snd_sem.at[step], early_sem.at[step, 1], device,
            )
            for device in x_holders
        ]
        for copy in copies[1:]:
            send(*copy).start()
        send_or_keep(copies[:1])

    def spread_on(step, landing):
        drain(ring_rcv.at[step, 0:3], early_sem.at[step, 0])
        copies = [
            (
                ring_rcv.at[step], landing.at[place, :, core, 0],
                late_snd_sem.at[step, 0], late_sem.at[step, 0], device,
            )
            for device in x_holders
        ]
        for copy in copies[1:]:
            send(*copy).start()
        send_or_keep(copies[:1])
        part = landing.at[:, y, :, 1]
        drain(part, early_sem.at[step, 1])
        for device, _ in y_others:
            send(part, part, late_snd_sem.at[step, 1], late_sem.at[step, 1], device).start()

    def spread_end(step, landing):
        drain(landing.at[:, :, :, 0], late_sem.at[step, 0])
        drain(landing.at[:, 0:3, :, 1], late_sem.at[step, 1])

    def whole(landing):
        return landing[...].reshape(2, COLUMNS, UNKNOWNS)

    current, current_parent = thin(moved, inv_at(LEVELS - 1), 0), None
    results = [None] * LEVELS
    results[LEVELS - 1] = current
    for level in range(LEVELS - 2, -1, -1):
        send_down(level, 0, current)
        if level == 0:
            spread(0, next_rcv, current)
        prepare_local(LEVELS - 2 - level)
        if level == 0:
            spread_on(0, next_rcv)
        left = below[level]
        if kinds_at(level) == 2:
            left = left - thin(pooled(level, 1, current_parent), low_at(level, 1), 0)
        current_parent = pooled(level, 0, current)
        if level > 0:
            send_down(level - 1, 1, current_parent)
        current = left - thin(current_parent, low_at(level, 0), 0)
        results[level] = current
    spread(1, x_rcv, current)

    spread_end(0, next_rcv)
    send(next_rcv, beside_rcv, beside_snd_sem, beside_sem, sibling).start()
    halves = []
    for octet in (slice(0, OCTET), slice(OCTET, SHARE)):
        for part in results[1:] + results[3:]:
            halves.append(jnp.stack([part[octet, 0:HALF], part[octet, HALF:]], axis=0))
    tiles = regroup(jnp.stack(halves, axis=1))
    for m in range(8):
        for h in range(2):
            sol_snd[8 * h + m] = tiles[m][h]
    spread_on(1, x_rcv)
    copies = [
        (sol_snd.at[device[1]], sol_rcv.at[place, share], sol_snd_sem, sol_sem, device)
        for device in holders
    ]
    for copy in copies[1:]:
        send(*copy).start()
    send_or_keep(copies[:1])
    drain(beside_rcv, beside_sem)
    own_next, beside_next = whole(next_rcv), whole(beside_rcv)
    for i in range(LOCALS):
        grand = None
        for at_place in range(4):
            weight = sum(
                pick[i][k] * jnp.where(lvl_parent[k, 0] == at_place, 1.0, 0.0).astype(f32)
                for k in range(2)
            )
            if at_place < 2:
                term = weight * own_next[at_place]
            else:
                term = weight * beside_next[at_place - 2]
            grand = term if grand is None else grand + term
        loc_out[i] = (y_s[i] - product(grand, low_high[i, 1], low_rest[i, 1], 0)).T
    drain(x_part.at[0:3], part_snd_sem.at[0])
    drain(y_last.at[1:], part_snd_sem.at[1])
    drain(x_last.at[0:3], last_snd_sem)
    drain(ride_rcv.at[1:], ride_snd_sem)
    drain(names_snd, names_snd_sem)
    for step in range(2):
        for _ in range(2):
            drain(ring_rcv.at[step, 0:3], early_snd_sem.at[step])
        for _ in range(3):
            drain(ring_rcv.at[step], late_snd_sem.at[step, 0])
        drain(x_rcv.at[:, 0:3, :, 1], late_snd_sem.at[step, 1])
    drain(sol_snd.at[1:], sol_snd_sem)
    drain(strips_s.at[0], strip_snd_sem)
    drain(mats.at[:, 0:3, 0], ring_snd_sem)
    drain(mats.at[:, :, 0], pair_snd_sem)
    drain(beside_rcv, beside_snd_sem)
    for level in range(LEVELS - 1):
        for kind in range(kinds_at(level)):
            drain(up_rcv.at[level, kind], up_snd_sem)
            drain(down_rcv.at[level, kind], down_snd_sem)

    @pl.when(jnp.logical_not(own))
    def _():
        drain(x_part.at[0], part_snd_sem.at[0])
        drain(y_last.at[0], part_snd_sem.at[1])
        drain(ride_rcv.at[0], ride_snd_sem)
        for step in range(2):
            drain(ring_rcv.at[step, 0], early_snd_sem.at[step])
            drain(ring_rcv.at[step], late_snd_sem.at[step, 0])
        drain(sol_snd.at[0], sol_snd_sem)
        drain(strips_s.at[0], strip_snd_sem)

    spread_end(1, x_rcv)
    x_all = whole(x_rcv)
    for i in range(LOCALS):
        above_x = pick[i][0] * x_all[0] + pick[i][1] * x_all[1]
        loc_out[i] -= multiply((low_high[i, 0], low_rest[i, 0]), split(above_x), 1)
    here = pl.ds(pl.multiple_of(STRIP * rows, STRIP), STRIP)
    for k in range(2):
        turned_s[k] = x_all[k].T
        sol_out[pl.ds(k, STRIP, stride=2), :] = turned_s[k, here, :]
    drain(sol_rcv, sol_sem)
    for k in range(2):
        packed = sol_rcv[k].reshape(SHARES * OCTET, 128)
        right = pltpu.roll(packed, 64, 1).reshape(SHARES, OCTET, 128)
        both = jnp.stack([sol_rcv[k], right], axis=1).reshape(COLUMNS, 128)
        strips = both.T
        for level in range(1, LEVELS):
            to = pl.ds(2 * STRIP * level + k, STRIP, stride=2)
            sol_out[to, :] = strips[STRIP * (level - 1) : STRIP * level]


def on_device(loc_rhs, loc_inv, loc_low, loc_parent, lvl_rhs, lvl_inv, lvl_low, lvl_parent):
    vmem = pl.BlockSpec(memory_space=pltpu.VMEM)
    far = pl.BlockSpec(memory_space=pltpu.HBM)
    dma = pltpu.SemaphoreType.DMA
    square = (UNKNOWNS, UNKNOWNS)
    loc_sol, sol = pl.pallas_call(
        kernel,
        out_shape=(
            jax.ShapeDtypeStruct((LOCALS, UNKNOWNS, COLUMNS), f32),
            jax.ShapeDtypeStruct((COLUMNS, 128), f32),
        ),
        in_specs=[far] * 8,
        out_specs=(vmem, vmem),
        scratch_shapes=[
            pltpu.SMEM((LOCALS,), jnp.int32),
            pltpu.SMEM((2, LEVELS - 1), jnp.int32),
            pltpu.VMEM((LOCALS, UNKNOWNS, COLUMNS), f32),
            pltpu.VMEM((LOCALS,) + square, f32),
            pltpu.VMEM((LOCALS, 2) + square, f32),
            pltpu.VMEM((LEVELS * STRIP * 2, COLUMNS), f32),
            pltpu.VMEM((LOCALS,) + square, bf16),
            pltpu.VMEM((LOCALS,) + square, bf16),
            pltpu.VMEM((LOCALS, 2) + square, bf16),
            pltpu.VMEM((LOCALS, 2) + square, bf16),
            pltpu.VMEM((LOCALS, COLUMNS, UNKNOWNS), f32),
            pltpu.VMEM((LOCALS, UNKNOWNS, COLUMNS), f32),
            pltpu.VMEM((2, UNKNOWNS, COLUMNS), f32),
            pltpu.VMEM((2, len(BLOCKS), STRIP, UNKNOWNS), f32),
            pltpu.VMEM((2, 2, 4, 2, SHARE, UNKNOWNS), f32),
            pltpu.VMEM((4, 4, SHARE, UNKNOWNS), f32),
            pltpu.VMEM((4, SHARE, UNKNOWNS), f32),
            pltpu.VMEM((4, SHARE, UNKNOWNS), f32),
            pltpu.VMEM((PEERS, SHARE, UNKNOWNS), f32),
            pltpu.VMEM((2, SHARES, OCTET, 128), f32),
            pltpu.VMEM((PEERS, OCTET, 128), f32),
            pltpu.VMEM((OCTET, 128), f32),
            pltpu.VMEM((OCTET, 128), f32),
            pltpu.VMEM((len(BLOCKS), 4, 2, 2 * STRIP, UNKNOWNS), f32),
            pltpu.VMEM((len(BLOCKS),) + square, bf16),
            pltpu.VMEM((len(BLOCKS),) + square, bf16),
            pltpu.VMEM((LEVELS - 1, 2, 3, SHARE, UNKNOWNS), f32),
            pltpu.VMEM((LEVELS - 1, 2, 3, SHARE, UNKNOWNS), f32),
            pltpu.VMEM((LEVELS - 1, 2, SHARE, UNKNOWNS), f32),
            pltpu.VMEM((LEVELS - 1, 2, 3, SHARE, UNKNOWNS), f32),
            pltpu.VMEM((2, 2, OCTET, UNKNOWNS), f32),
            pltpu.VMEM((2, 4, OCTET, UNKNOWNS), f32),
            pltpu.VMEM((2, 4, 2, 2, OCTET, UNKNOWNS), f32),
            pltpu.VMEM((2, 4, 2, 2, OCTET, UNKNOWNS), f32),
            pltpu.VMEM((2, 4, 2, 2, OCTET, UNKNOWNS), f32),
            pltpu.VMEM((PEERS, OCTET, 128), f32),
            pltpu.VMEM((2, SHARES, OCTET, 128), f32),
            pltpu.VMEM((2, UNKNOWNS, COLUMNS), f32),
            dma((6,)),
            dma((len(BLOCKS),)),
            dma((2,)),
            dma((2,)),
            dma,
            dma,
            dma,
            dma,
            dma,
            dma,
            dma,
            dma((TRIOS,)),
            dma,
            dma((TRIOS,)),
            dma((TRIOS,)),
            dma,
            dma((TRIOS,)),
            dma,
            dma((LEVELS - 1, 2)),
            dma,
            dma((LEVELS - 1, 2)),
            dma((2,)),
            dma((2, 2)),
            dma((2, 2)),
            dma((2, 2)),
            dma,
            dma,
            dma,
            dma,
        ],
        compiler_params=pltpu.CompilerParams(
            collective_id=0, has_side_effects=True, vmem_limit_bytes=40 * 1024 * 1024
        ),
    )(
        *(
            pltpu.with_memory_space_constraint(operand, pltpu.HBM)
            for operand in (
                loc_parent.reshape(LOCALS),
                loc_rhs.reshape(LOCALS, UNKNOWNS, COLUMNS),
                loc_inv.reshape((LOCALS,) + square),
                loc_low.reshape((LOCALS, 2) + square),
                lvl_rhs.reshape(LEVELS * STRIP * 2, COLUMNS),
                lvl_inv.reshape(LEVELS, 2, STRIP, UNKNOWNS),
                lvl_low.reshape(LEVELS - 1, 2, 2, STRIP, UNKNOWNS),
                lvl_parent.reshape(LEVELS - 1, 2).T,
            )
        )
    )
    return loc_sol[None, None], sol.reshape(1, LEVELS, STRIP, 2, COLUMNS)


def solution(mesh):
    in_specs = (
        P("leaf", "rows", None, None, None),
        P("leaf", "rows", None, None, None),
        P("leaf", "rows", None, None, None, None),
        P("leaf", "rows", None),
        P("leaf", None, "rows", None, None),
        P("leaf", None, None, "rows", None),
        P("leaf", None, None, None, "rows", None),
        P("leaf", None, None),
    )
    out_specs = (P("leaf", "rows", None, None, None), P("leaf", None, "rows", None, None))
    return jax.shard_map(
        on_device, mesh=mesh, in_specs=in_specs, out_specs=out_specs, check_vma=False
    )
```
